32 devices in a mesh: dp: 8 (over z, x), mp: 4 (over y, core).
Axes of the slice: x: 2, y: 2, z: 4, core: 2. Of those that a mesh axis runs over, the one named last changes fastest.
Arguments:
- query_states: bfloat16 [1024, 8192], P('dp', 'mp'), may hold values from -35.35534 to 35.35534
- key_states: bfloat16 [1024, 1024], P('dp', 'mp'), may hold values from -3 to 3
- value_states: bfloat16 [1024, 1024], P('dp', 'mp'), may hold values from -6 to 6
- grad_context: bfloat16 [1024, 8192], P('dp', 'mp'), may hold values from -6 to 6
- inputs_normed: bfloat16 [1024, 4096], P('dp'), may hold values from -6 to 6
- projections: bfloat16 [2, 4096, 1024], P(None, None, 'mp'), may hold values from -0.09375 to 0.09375
Outputs:
- grad_query: bfloat16 [1024, 8192], P('dp', 'mp')
- grad_input: bfloat16 [1024, 4096], P('dp', 'mp')
- grad_weights: float32 [4096, 1024], P('dp', 'mp')
The draws below stay inside these ranges and needn't reach their ends.
All inputs are finite; a program needn't handle non-finite values.
Results may differ from the reference program's by a relative error of at most 0.013.
Values may be sent and summed in bfloat16 or wider, within the bound.
No kernel may reach another device: no remote copies, remote signals or barrier semaphores. Data moves between devices by JAX's collectives and lax.ppermute only.
A program may use at most 64 MiB of HBM per device.

```python
import math
import jax
import jax.numpy as jnp
from jax import lax

D = 4096
HEAD_SIZE = 128
QUERY_HEADS = 64
KEY_VALUE_HEADS = 8
SEQUENCE_TOKENS = 128
QUERY_PER_KEY = 8
QW = 8192
KVW = 1024
TOTAL_TOKENS = 1024
N_DP = 8
N_MP = 4


def joint_draw(key):
    query_key = jax.random.fold_in(key, 101)
    random_key_for_keys = jax.random.fold_in(key, 202)
    queries = jnp.clip(jax.random.normal(query_key, (TOTAL_TOKENS, QUERY_HEADS * HEAD_SIZE), jnp.float32), -3.0, 3.0)
    random_key_list = jnp.clip(jax.random.normal(random_key_for_keys, (TOTAL_TOKENS, KEY_VALUE_HEADS * HEAD_SIZE), jnp.float32), -3.0, 3.0)
    return (queries, random_key_list)


def draw_query_states(key, part):
    return joint_draw(key)[0].astype(jnp.bfloat16)


def draw_key_states(key, part):
    return joint_draw(key)[1].astype(jnp.bfloat16)


def strengthened(array, rng, source, target, parts, factor):
    def block_of(position):
        return (jnp.arange(array.shape[position]) // (array.shape[position] // parts)).reshape((-1,) + (1,) * (array.ndim - 1 - position))

    one_side = jax.random.permutation(rng, parts)[block_of(target)]
    second = (block_of(target) + parts // 2) % parts
    return jnp.where((block_of(source) == one_side) | (block_of(source) == second), factor * array, array)


def block_scale(key, dims, split, least, largest):
    factor_of = 1.0
    for position, blocks in split:
        steps = jax.random.uniform(jax.random.fold_in(jax.random.fold_in(key, 6), position), (blocks,), jnp.float32, least / len(split), largest / len(split))
        factor_of = factor_of * jnp.repeat(jnp.exp(steps), dims[position] // blocks).reshape((-1,) + (1,) * (len(dims) - 1 - position))
    return factor_of


def bell_draw(own_key, extent, scale, most, pieces=(), held_as=jnp.bfloat16):
    factor_of = block_scale(own_key, extent, pieces, -0.22, 0.18) if pieces else 1.0
    drawn = jax.random.normal(own_key, extent, jnp.float32) * scale * factor_of
    return jnp.minimum(jnp.maximum(drawn, -most), most).astype(held_as)


def bell_draw_with(stream_key, extent, deviation, reach, pieces, heavy, kind=jnp.bfloat16):
    values = deviation * jax.random.normal(stream_key, extent, jnp.float32)
    if pieces:
        values = values * block_scale(stream_key, extent, pieces, -0.22, 0.18)
    return jnp.clip(strengthened(values, jax.random.fold_in(stream_key, 3), *heavy), -reach, reach).astype(kind)


def setup_inputs(seed: int = 0) -> dict:
    arg_keys = jax.random.split(jax.random.key(seed), 7)
    query_states = draw_query_states(jax.random.fold_in(arg_keys[6], 71), 0)
    key_states = draw_key_states(jax.random.fold_in(arg_keys[6], 71), 0)
    value_states = bell_draw(arg_keys[2], (TOTAL_TOKENS, KVW), 1.0, 6.0, ((0, 8), (1, 4)))
    grad_context = bell_draw(arg_keys[3], (TOTAL_TOKENS, QW), 1.0, 6.0, ((0, 8), (1, 4)))
    inputs_normed = bell_draw_with(arg_keys[4], (TOTAL_TOKENS, D), 1.0, 6.0, ((0, 8),), (0, 1, 8, 2.0))
    projections = bell_draw(arg_keys[5], (2, D, KVW), D ** -0.5, 0.09375, ((2, 4),))
    return dict(query_states=query_states, key_states=key_states, value_states=value_states, grad_context=grad_context, inputs_normed=inputs_normed, projections=projections)


def sequence_grads(query_token_rows, key_token_rows, value_token_rows, gradient_token_rows):
    scale = 1.0 / math.sqrt(HEAD_SIZE)
    query_per_head = query_token_rows.reshape(SEQUENCE_TOKENS, KEY_VALUE_HEADS, QUERY_PER_KEY, HEAD_SIZE).astype(jnp.float32)
    key_per_head = key_token_rows.reshape(SEQUENCE_TOKENS, KEY_VALUE_HEADS, HEAD_SIZE).astype(jnp.float32)
    value_per_head = value_token_rows.reshape(SEQUENCE_TOKENS, KEY_VALUE_HEADS, HEAD_SIZE).astype(jnp.float32)
    gradient_per_head = gradient_token_rows.reshape(SEQUENCE_TOKENS, KEY_VALUE_HEADS, QUERY_PER_KEY, HEAD_SIZE).astype(jnp.float32)
    scores = jnp.einsum('ikgd,jkd->kgij', query_per_head, key_per_head) * scale
    positions = jnp.arange(SEQUENCE_TOKENS, dtype=jnp.int32)[:, None]
    targets = jnp.arange(SEQUENCE_TOKENS, dtype=jnp.int32)[None, :]
    allowed = targets <= positions
    masked = jnp.where(allowed, scores, -1e+30)
    row_max = lax.optimization_barrier(jnp.max(masked, axis=-1, keepdims=True))
    raw_weights = jnp.where(allowed, jnp.exp(masked - row_max), 0.0)
    probs = raw_weights / lax.optimization_barrier(jnp.sum(raw_weights, axis=-1, keepdims=True))
    probs_low = lax.optimization_barrier(probs.astype(jnp.bfloat16))
    probs_b = probs_low.astype(jnp.float32)
    grad_value = jnp.einsum('kgij,ikgd->jkd', probs_b, gradient_per_head).astype(jnp.bfloat16)
    grad_probs = jnp.einsum('ikgd,jkd->kgij', gradient_per_head, value_per_head)
    delta = lax.optimization_barrier(jnp.sum(probs * grad_probs, axis=-1, keepdims=True))
    scores_low = lax.optimization_barrier((probs * (grad_probs - delta)).astype(jnp.bfloat16))
    grad_scores = scores_low.astype(jnp.float32)
    grad_query = (jnp.einsum('kgij,jkd->ikgd', grad_scores, key_per_head) * scale).astype(jnp.bfloat16)
    grad_key = (jnp.einsum('kgij,ikgd->jkd', grad_scores, query_per_head) * scale).astype(jnp.bfloat16)
    return (grad_query.reshape(SEQUENCE_TOKENS, QW), grad_key.reshape(SEQUENCE_TOKENS, KVW), grad_value.reshape(SEQUENCE_TOKENS, KVW))

def reference(query_states, key_states, value_states, grad_context, inputs_normed, projections):
    weights_wide = projections.astype(jnp.float32)
    weight_blocks = weights_wide.reshape(2, D, N_MP, KVW // N_MP)
    count_seqs = TOTAL_TOKENS // SEQUENCE_TOKENS

    def per_sequence(running, batch):
        query_token_rows, key_token_rows, value_token_rows, gradient_token_rows, normed_rows = batch
        grad_query, grad_key, grad_value = sequence_grads(query_token_rows, key_token_rows, value_token_rows, gradient_token_rows)
        both_grads = jnp.stack([grad_key, grad_value]).astype(jnp.float32)
        grad_blocks = both_grads.reshape(2, SEQUENCE_TOKENS, N_MP, KVW // N_MP)
        block_partial = jnp.einsum('tsmc,tdmc->msd', grad_blocks, weight_blocks)
        block_low = lax.optimization_barrier(block_partial.astype(jnp.bfloat16)).astype(jnp.float32)
        input_rows = lax.optimization_barrier(jnp.sum(block_low, axis=0)).astype(jnp.bfloat16)
        running = running + jnp.einsum('sd,sc->dc', normed_rows.astype(jnp.float32), both_grads[0])
        return (running, (grad_query, input_rows))
    initial = jnp.zeros((D, KVW), jnp.float32)
    batches = (query_states.reshape(count_seqs, SEQUENCE_TOKENS, QW), key_states.reshape(count_seqs, SEQUENCE_TOKENS, KVW), value_states.reshape(count_seqs, SEQUENCE_TOKENS, KVW), grad_context.reshape(count_seqs, SEQUENCE_TOKENS, QW), inputs_normed.reshape(count_seqs, SEQUENCE_TOKENS, D))
    summed, (query_grads, input_grads) = lax.scan(per_sequence, initial, batches)
    return (query_grads.reshape(TOTAL_TOKENS, QW), input_grads.reshape(TOTAL_TOKENS, D), summed / N_DP)
```

```python
import functools
import math

import jax
import jax.numpy as jnp
from jax import lax
from jax.experimental import pallas as pl
from jax.experimental.pallas import tpu as pltpu
from jax.sharding import PartitionSpec as P

HEAD_SIZE = 128
F32 = jnp.float32
BF16 = jnp.bfloat16
NT = (((1,), (1,)), ((), ()))
TN = (((0,), (0,)), ((), ()))
VMEM_LIMIT = 32 * 1024 * 1024


def dot(a, b, dims=(((1,), (0,)), ((), ()))):
    return lax.dot_general(a, b, dims, preferred_element_type=F32)


def attention_kernel(q_ref, k_ref, v_ref, do_ref, gk_ref, gv_ref, ds_ref):
    length = q_ref.shape[0]
    kv_heads = k_ref.shape[1] // HEAD_SIZE
    per_group = q_ref.shape[1] // k_ref.shape[1]
    scale = 1.0 / math.sqrt(HEAD_SIZE)
    targets = lax.broadcasted_iota(jnp.int32, (length, length), 0)
    positions = lax.broadcasted_iota(jnp.int32, (length, length), 1)
    allowed = targets <= positions
    for g in range(kv_heads):
        cols = slice(g * HEAD_SIZE, (g + 1) * HEAD_SIZE)
        key, value = k_ref[:, cols], v_ref[:, cols]
        acc_k = jnp.zeros((length, HEAD_SIZE), F32)
        acc_v = jnp.zeros((length, HEAD_SIZE), F32)
        for h in range(per_group):
            at = (g * per_group + h) * HEAD_SIZE
            query, grad = q_ref[:, at : at + HEAD_SIZE], do_ref[:, at : at + HEAD_SIZE]
            scores = jnp.where(allowed, dot(key, query, NT) * scale, -1e30)
            raw = jnp.exp(scores - jnp.max(scores, axis=0, keepdims=True))
            raw = jnp.where(allowed, raw, 0.0)
            probs = raw * (1.0 / jnp.sum(raw, axis=0, keepdims=True))
            grad_probs = dot(value, grad, NT)
            delta = jnp.sum(probs * grad_probs, axis=0, keepdims=True)
            grad_scores = (probs * (grad_probs - delta)).astype(BF16)
            ds_ref[:, at : at + length] = grad_scores
            acc_v += dot(probs.astype(BF16), grad)
            acc_k += dot(grad_scores, query)
        gk_ref[:, cols] = (acc_k * scale).astype(BF16)
        gv_ref[:, cols] = acc_v.astype(BF16)


def query_kernel(ds_ref, k_ref, gq_ref):
    kv_heads = k_ref.shape[1] // HEAD_SIZE
    per_group = gq_ref.shape[1] // k_ref.shape[1]
    scale = 1.0 / math.sqrt(HEAD_SIZE)
    for g in range(kv_heads):
        key = k_ref[:, g * HEAD_SIZE : (g + 1) * HEAD_SIZE]
        for h in range(per_group):
            at = (g * per_group + h) * HEAD_SIZE
            grad = dot(ds_ref[:, at : at + HEAD_SIZE], key, TN) * scale
            gq_ref[:, at : at + HEAD_SIZE] = grad.astype(BF16)


def partial_kernel(order_ref, gk_ref, gv_ref, p_ref, out_ref):
    del order_ref
    total = dot(gk_ref[...], p_ref[0], NT) + dot(gv_ref[...], p_ref[1], NT)
    out_ref[0] = total.astype(BF16)


def partials(order, grad_key, grad_value, projections, blocks):
    rows, width = grad_key.shape
    features = projections.shape[1] // blocks
    count = order.shape[0]
    return pl.pallas_call(
        partial_kernel,
        grid_spec=pltpu.PrefetchScalarGridSpec(
            num_scalar_prefetch=1,
            grid=(count,),
            in_specs=[
                pl.BlockSpec((rows, width), lambda t, order: (0, 0)),
                pl.BlockSpec((rows, width), lambda t, order: (0, 0)),
                pl.BlockSpec((2, features, width), lambda t, order: (0, order[t], 0)),
            ],
            out_specs=pl.BlockSpec((1, rows, features), lambda t, order: (t, 0, 0)),
        ),
        out_shape=jax.ShapeDtypeStruct((count, rows, features), BF16),
        compiler_params=pltpu.CompilerParams(vmem_limit_bytes=VMEM_LIMIT),
        cost_estimate=pl.CostEstimate(
            flops=4 * rows * width * features * count,
            bytes_accessed=count * features * (4 * width + 2 * rows),
            transcendentals=0,
        ),
    )(order, grad_key, grad_value, projections)


def split_kernel(core_ref, x_ref, out_ref):
    del core_ref
    width = out_ref.shape[2]
    for b in range(out_ref.shape[0]):
        out_ref[b] = x_ref[:, b * width : (b + 1) * width]


def column_blocks(core, inputs, parts):
    half = inputs.shape[0] // 2
    width = inputs.shape[1] // parts
    if width % 128:
        mine = lax.dynamic_slice_in_dim(inputs, core * half, half, 0)
        return mine.reshape(half, parts, width).transpose(1, 0, 2)
    return pl.pallas_call(
        split_kernel,
        grid_spec=pltpu.PrefetchScalarGridSpec(
            num_scalar_prefetch=1,
            grid=(1,),
            in_specs=[pl.BlockSpec((half, inputs.shape[1]), lambda t, core: (core[0], 0))],
            out_specs=pl.BlockSpec((parts, half, width), lambda t, core: (0, 0, 0)),
        ),
        out_shape=jax.ShapeDtypeStruct((parts, half, width), inputs.dtype),
    )(core.reshape(1), inputs)


def weights_kernel(core_ref, mine_ref, other_ref, keys_ref, out_ref):
    parts, half, width = mine_ref.shape
    columns = keys_ref.shape[2]
    core = core_ref[0]
    own = keys_ref[:, pl.ds(core * half, half), :].reshape(parts * half, columns)
    rest = keys_ref[:, pl.ds((1 - core) * half, half), :].reshape(parts * half, columns)
    total = dot(mine_ref[...].reshape(parts * half, width), own, TN)
    total += dot(other_ref[...].reshape(parts * half, width), rest, TN)
    out_ref[...] = total * (1.0 / parts)


def body(query_states, key_states, value_states, grad_context, inputs_normed, projections):
    parts = lax.axis_size("dp")
    groups = lax.axis_size("mp")
    chips = groups // 2
    place = lax.axis_index("mp")
    core, chip = lax.rem(place, 2), lax.div(place, 2)
    to_other_core = [(i, i ^ 1) for i in range(groups)]
    rows, width = key_states.shape
    query_width = query_states.shape[1]
    features = projections.shape[1] // groups
    half = rows // 2

    blocks = column_blocks(core, inputs_normed, parts)
    mine = lax.all_to_all(blocks, "dp", split_axis=0, concat_axis=0, tiled=True)
    other = lax.ppermute(mine, "mp", to_other_core)

    grad_key, grad_value, grad_scores = pl.pallas_call(
        attention_kernel,
        out_shape=(
            jax.ShapeDtypeStruct((rows, width), BF16),
            jax.ShapeDtypeStruct((rows, width), BF16),
            jax.ShapeDtypeStruct((rows, query_width), BF16),
        ),
        compiler_params=pltpu.CompilerParams(vmem_limit_bytes=VMEM_LIMIT),
        cost_estimate=pl.CostEstimate(
            flops=8 * rows * rows * query_width,
            bytes_accessed=6 * rows * query_width,
            transcendentals=rows * query_width,
        ),
    )(query_states, key_states, value_states, grad_context)

    all_keys = lax.all_gather(grad_key, "dp", axis=0)

    chip_order = [lax.rem(chip + k, chips) for k in range(1, chips + 1)]
    for_other = jnp.stack([2 * c + 1 - core for c in chip_order]).astype(jnp.int32)
    for_own = jnp.stack([2 * c + core for c in chip_order]).astype(jnp.int32)
    sent = partials(for_other, grad_key, grad_value, projections, groups)
    kept = partials(for_own, grad_key, grad_value, projections, groups)
    came = lax.ppermute(sent, "mp", to_other_core)
    pair = kept.astype(F32) + came.astype(F32)
    grad_input = pair[chips - 1]
    for k in range(1, chips):
        shift = [(i, (i + 2 * k) % groups) for i in range(groups)]
        grad_input += lax.ppermute(pair[k - 1].astype(BF16), "mp", shift).astype(F32)
    grad_input = grad_input.astype(BF16)

    grad_query = pl.pallas_call(
        query_kernel,
        out_shape=jax.ShapeDtypeStruct((rows, query_width), BF16),
        compiler_params=pltpu.CompilerParams(vmem_limit_bytes=VMEM_LIMIT),
        cost_estimate=pl.CostEstimate(
            flops=2 * rows * rows * query_width,
            bytes_accessed=4 * rows * query_width,
            transcendentals=0,
        ),
    )(grad_scores, key_states)

    spec = pl.BlockSpec(memory_space=pltpu.VMEM)
    grad_weights = pl.pallas_call(
        weights_kernel,
        in_specs=[pl.BlockSpec(memory_space=pltpu.SMEM), spec, spec, spec],
        out_specs=spec,
        out_shape=jax.ShapeDtypeStruct((inputs_normed.shape[1] // parts, width), F32),
        compiler_params=pltpu.CompilerParams(vmem_limit_bytes=VMEM_LIMIT),
        cost_estimate=pl.CostEstimate(
            flops=2 * rows * inputs_normed.shape[1] * width,
            bytes_accessed=4 * half * inputs_normed.shape[1],
            transcendentals=0,
        ),
    )(core.reshape(1), mine, other, all_keys)
    return (grad_query, grad_input, grad_weights)


def solution(mesh):
    placed = (
        P("dp", "mp"),
        P("dp", "mp"),
        P("dp", "mp"),
        P("dp", "mp"),
        P("dp", None),
        P(None, None, "mp"),
    )
    return jax.shard_map(
        body,
        mesh=mesh,
        in_specs=placed,
        out_specs=(P("dp", "mp"), P("dp", "mp"), P("dp", "mp")),
        check_vma=False,
    )
```

```python
import functools
import math

import jax
import jax.numpy as jnp
from jax import lax
from jax.experimental import pallas as pl
from jax.experimental.pallas import tpu as pltpu
from jax.sharding import PartitionSpec as P

HEAD_SIZE = 128
F32 = jnp.float32
BF16 = jnp.bfloat16
NN = (((1,), (0,)), ((), ()))
NT = (((1,), (1,)), ((), ()))
TN = (((0,), (0,)), ((), ()))
IN_HBM = pl.BlockSpec(memory_space=pltpu.HBM)
ANYWHERE = pl.BlockSpec(memory_space=pl.ANY)
IN_VMEM = pl.BlockSpec(memory_space=pltpu.VMEM)
IN_SMEM = pl.BlockSpec(memory_space=pltpu.SMEM)
CHUNK = 512
PARAMS = pltpu.CompilerParams(vmem_limit_bytes=24 * 1024 * 1024)
WHOLE = pltpu.CompilerParams()


def dot(a, b, dims=NN):
    return lax.dot_general(a, b, dims, preferred_element_type=F32)


def cost(flops, moved, transcendentals=0):
    return pl.CostEstimate(flops=flops, bytes_accessed=moved, transcendentals=transcendentals)


def attention_group(g, q, k, v, do, gk_ref, gv_ref, ds_ref):
    length = q.shape[0]
    per_group = q.shape[1] // k.shape[1]
    scale = 1.0 / math.sqrt(HEAD_SIZE)
    targets = lax.broadcasted_iota(jnp.int32, (length, length), 0)
    positions = lax.broadcasted_iota(jnp.int32, (length, length), 1)
    allowed = targets <= positions
    cols = slice(g * HEAD_SIZE, (g + 1) * HEAD_SIZE)
    key, value = k[:, cols], v[:, cols]
    acc_k = jnp.zeros((length, HEAD_SIZE), F32)
    acc_v = jnp.zeros((length, HEAD_SIZE), F32)
    for h in range(per_group):
        at = (g * per_group + h) * HEAD_SIZE
        query, grad = q[:, at : at + HEAD_SIZE], do[:, at : at + HEAD_SIZE]
        scores = jnp.where(allowed, dot(key, query, NT) * scale, -1e30)
        raw = jnp.exp(scores - jnp.max(scores, axis=0, keepdims=True))
        raw = jnp.where(allowed, raw, 0.0)
        probs = raw * (1.0 / jnp.sum(raw, axis=0, keepdims=True))
        grad_probs = dot(value, grad, NT)
        delta = jnp.sum(probs * grad_probs, axis=0, keepdims=True)
        grad_scores = (probs * (grad_probs - delta)).astype(BF16)
        ds_ref[:, at : at + length] = grad_scores
        acc_v += dot(probs.astype(BF16), grad)
        acc_k += dot(grad_scores, query)
    gk_ref[:, cols] = (acc_k * scale).astype(BF16)
    gv_ref[:, cols] = acc_v.astype(BF16)


def block_partials(p, gk, gv, out_ref):
    features = p.shape[2]
    step = min(CHUNK, features)
    for b in range(p.shape[0]):
        for at in range(0, features, step):
            rows = slice(at, at + step)
            total = dot(p[b, 0, rows, :], gk, NT) + dot(p[b, 1, rows, :], gv, NT)
            out_ref[b, rows, :] = total.astype(BF16)


def projection_copies(place_ref, p_hbm, p, sems, own):
    chips, features = p.shape[0], p.shape[2]
    chip, core = lax.div(place_ref[1], 2), lax.rem(place_ref[1], 2)
    column = core if own else 1 - core
    copies = []
    for b in range(chips):
        start = (2 * lax.rem(chip + b + 1, chips) + column) * features
        rows = pl.ds(pl.multiple_of(start, features), features)
        copies.append(pltpu.make_async_copy(p_hbm.at[:, rows, :], p.at[b], sems.at[b]))
    return copies


def attention_kernel(
    place_ref, q_hbm, k_hbm, v_hbm, do_hbm, p_hbm,
    gk_ref, gv_ref, ds_ref, sent_ref,
    q, k, v, do, p, sems, p_sems,
):
    kv_heads = k.shape[1] // HEAD_SIZE
    group = q.shape[1] // kv_heads
    small = [
        pltpu.make_async_copy(k_hbm, k, sems.at[0]),
        pltpu.make_async_copy(v_hbm, v, sems.at[1]),
    ]
    large = []
    for g in range(kv_heads):
        cols = pl.ds(g * group, group)
        large.append((
            pltpu.make_async_copy(q_hbm.at[:, cols], q.at[:, cols], sems.at[2 + 2 * g]),
            pltpu.make_async_copy(do_hbm.at[:, cols], do.at[:, cols], sems.at[3 + 2 * g]),
        ))
    blocks = projection_copies(place_ref, p_hbm, p, p_sems, own=False)
    for copy in small:
        copy.start()
    for pair in large:
        for copy in pair:
            copy.start()
    for copy in blocks:
        copy.start()
    for copy in small:
        copy.wait()
    for g in range(kv_heads):
        for copy in large[g]:
            copy.wait()
        attention_group(g, q, k, v, do, gk_ref, gv_ref, ds_ref)
    for copy in blocks:
        copy.wait()
    block_partials(p, gk_ref[...], gv_ref[...], sent_ref)


def own_partials_kernel(place_ref, gk_ref, gv_ref, p_hbm, kept_ref, p, p_sems):
    blocks = projection_copies(place_ref, p_hbm, p, p_sems, own=True)
    for copy in blocks:
        copy.start()
    for copy in blocks:
        copy.wait()
    block_partials(p, gk_ref[...], gv_ref[...], kept_ref)


def query_kernel(ds_ref, k_ref, gq_ref):
    kv_heads = k_ref.shape[1] // HEAD_SIZE
    per_group = gq_ref.shape[1] // k_ref.shape[1]
    scale = 1.0 / math.sqrt(HEAD_SIZE)
    for g in range(kv_heads):
        key = k_ref[:, g * HEAD_SIZE : (g + 1) * HEAD_SIZE]
        for h in range(per_group):
            at = (g * per_group + h) * HEAD_SIZE
            grad = dot(ds_ref[:, at : at + HEAD_SIZE], key, TN) * scale
            gq_ref[:, at : at + HEAD_SIZE] = grad.astype(BF16)


def input_kernel(kept_ref, came_ref, *refs):
    out_ref = refs[-1]
    total = kept_ref[len(refs) - 1].astype(F32) + came_ref[len(refs) - 1].astype(F32)
    for ref in refs[:-1]:
        total += ref[...].astype(F32)
    out_ref[...] = total.T.astype(BF16)


def column_blocks_kernel(index_ref, x_hbm, *refs):
    outs, sems = refs[:-1], refs[-1]
    width = outs[0].shape[1]
    copies = []
    for j, out in enumerate(outs):
        cols = pl.ds(pl.multiple_of(index_ref[j] * width, width), width)
        copies.append(pltpu.make_async_copy(x_hbm.at[:, cols], out, sems.at[j]))
    for copy in copies:
        copy.start()
    for copy in copies:
        copy.wait()


def weights_kernel(count, slot_ref, *refs):
    inputs, keys, out_ref, x, gk = refs[:count], refs[count : 2 * count], *refs[2 * count :]
    rows = inputs[0].shape[0]
    for j in range(count):
        x[pl.ds(pl.multiple_of(slot_ref[j] * rows, rows), rows), :] = inputs[j][...]
        gk[j * rows : (j + 1) * rows, :] = keys[j][...]
    out_ref[...] = dot(x[...], gk[...], TN) * (1.0 / count)


def outgoing_blocks(inputs, place, parts, groups):
    far = parts // 2
    part, member = place[0], place[1]
    core = lax.rem(member, 2)
    rows = inputs.shape[0]
    width = inputs.shape[1] // parts
    targets = [part ^ (far + member)] + [part ^ (k + core) for k in range(2, far, 2)]
    targets += [part ^ 1, part]
    return pl.pallas_call(
        column_blocks_kernel,
        in_specs=[IN_SMEM, IN_HBM],
        out_specs=[ANYWHERE] * len(targets),
        out_shape=[jax.ShapeDtypeStruct((rows, width), inputs.dtype)] * len(targets),
        scratch_shapes=[pltpu.SemaphoreType.DMA((len(targets),))],
        compiler_params=WHOLE,
        cost_estimate=cost(0, 4 * len(targets) * rows * width),
    )(jnp.stack(targets).astype(jnp.int32), inputs)


def exchanged_weights(inputs, blocks, grad_key, place, parts, groups):
    far = parts // 2
    part, member = place[0], place[1]
    core = lax.rem(member, 2)
    rows = inputs.shape[0]
    width = inputs.shape[1] // parts

    def along_dp(array, partner):
        pairs = [
            (i * groups + m, (i ^ partner(m)) * groups + m)
            for i in range(parts)
            for m in range(groups)
        ]
        return lax.ppermute(array, ("dp", "mp"), pairs)

    def along_mp(array, bit):
        return lax.ppermute(array, "mp", [(m, m ^ bit) for m in range(groups)])

    near = list(range(2, far, 2))
    slots, pieces = [jnp.int32(0)], [blocks[-1]]
    slots.append(jnp.int32(1))
    shared = {0: along_dp(blocks[0], lambda m: far + m)}
    for k, block in zip(near, blocks[1:]):
        first = along_dp(block, lambda m, k=k: k + m % 2)
        pieces += [first, along_mp(first, 1)]
        slots += [k + core, k + (core ^ 1)]
    pieces.insert(1, along_dp(blocks[-2], lambda m: 1))
    bit = groups // 2
    while bit:
        for j in list(shared):
            shared[j ^ bit] = along_mp(shared[j], bit)
        bit //= 2
    for j, piece in shared.items():
        pieces.append(piece)
        slots.append(far + (member ^ j))

    keys = {0: grad_key}
    for k in sorted(range(2, parts, 2), reverse=True):
        keys[k] = along_dp(grad_key, lambda m, k=k: k)
    for k in range(0, parts, 2):
        keys[k + 1] = along_dp(keys[k], lambda m: 1)

    columns = grad_key.shape[1]
    return pl.pallas_call(
        functools.partial(weights_kernel, parts),
        in_specs=[IN_SMEM] + [IN_VMEM] * (2 * parts),
        out_specs=IN_VMEM,
        out_shape=jax.ShapeDtypeStruct((width, columns), F32),
        scratch_shapes=[
            pltpu.VMEM((parts * rows, width), inputs.dtype),
            pltpu.VMEM((parts * rows, columns), BF16),
        ],
        compiler_params=PARAMS,
        cost_estimate=cost(
            2 * parts * rows * width * columns, 2 * parts * rows * (width + columns)
        ),
    )(jnp.stack(slots).astype(jnp.int32), *pieces, *[keys[k] for k in range(parts)])


def gathered_weights(inputs, grad_key, parts):
    rows = inputs.shape[0]
    width = inputs.shape[1] // parts
    blocks = inputs.reshape(rows, parts, width).transpose(1, 0, 2)
    mine = lax.all_to_all(blocks, "dp", split_axis=0, concat_axis=0, tiled=True)
    keys = lax.all_gather(grad_key, "dp", axis=0)
    return jnp.einsum("psd,psc->dc", mine, keys, preferred_element_type=F32) / parts


def body(query_states, key_states, value_states, grad_context, inputs_normed, projections):
    parts = lax.axis_size("dp")
    groups = lax.axis_size("mp")
    chips = groups // 2
    place = jnp.stack([lax.axis_index("dp"), lax.axis_index("mp")]).astype(jnp.int32)
    rows, width = key_states.shape
    query_width = query_states.shape[1]
    features = projections.shape[1] // groups
    kv_heads = width // HEAD_SIZE
    blocks = jax.ShapeDtypeStruct((chips, features, rows), BF16)
    p_scratch = [
        pltpu.VMEM((chips, 2, features, width), BF16),
        pltpu.SemaphoreType.DMA((chips,)),
    ]

    exchange = parts == 2 * groups
    if exchange:
        outgoing = outgoing_blocks(inputs_normed, place, parts, groups)
        place, outgoing = lax.optimization_barrier((place, outgoing))

    grad_key, grad_value, grad_scores, sent = pl.pallas_call(
        attention_kernel,
        in_specs=[IN_SMEM] + [IN_HBM] * 5,
        out_specs=[IN_VMEM] * 4,
        out_shape=(
            jax.ShapeDtypeStruct((rows, width), BF16),
            jax.ShapeDtypeStruct((rows, width), BF16),
            jax.ShapeDtypeStruct((rows, query_width), BF16),
            blocks,
        ),
        scratch_shapes=[
            pltpu.VMEM((rows, query_width), BF16),
            pltpu.VMEM((rows, width), BF16),
            pltpu.VMEM((rows, width), BF16),
            pltpu.VMEM((rows, query_width), BF16),
            p_scratch[0],
            pltpu.SemaphoreType.DMA((2 + 2 * kv_heads,)),
            p_scratch[1],
        ],
        compiler_params=WHOLE,
        cost_estimate=cost(
            8 * rows * rows * query_width + 4 * rows * width * features * chips,
            6 * rows * query_width + 4 * width * features * chips,
            rows * query_width,
        ),
    )(place, query_states, key_states, value_states, grad_context, projections)

    if exchange:
        grad_weights = exchanged_weights(
            inputs_normed, outgoing, grad_key, place, parts, groups
        )
    else:
        grad_weights = gathered_weights(inputs_normed, grad_key, parts)

    came = lax.ppermute(sent, "mp", [(m, m ^ 1) for m in range(groups)])
    kept = pl.pallas_call(
        own_partials_kernel,
        in_specs=[IN_SMEM, IN_VMEM, IN_VMEM, IN_HBM],
        out_specs=IN_VMEM,
        out_shape=blocks,
        scratch_shapes=p_scratch,
        compiler_params=WHOLE,
        cost_estimate=cost(
            4 * rows * width * features * chips, 4 * width * features * chips
        ),
    )(place, grad_key, grad_value, projections)
    arrived = []
    for b in range(chips - 1):
        pair = (kept[b].astype(F32) + came[b].astype(F32)).astype(BF16)
        shift = [(m, (m + 2 * (b + 1)) % groups) for m in range(groups)]
        arrived.append(lax.ppermute(pair, "mp", shift))
    grad_input = pl.pallas_call(
        input_kernel,
        in_specs=[IN_VMEM] * (2 + len(arrived)),
        out_specs=IN_VMEM,
        out_shape=jax.ShapeDtypeStruct((rows, features), BF16),
        compiler_params=PARAMS,
        cost_estimate=cost(rows * features, 8 * rows * features),
    )(kept, came, *arrived)

    grad_query = pl.pallas_call(
        query_kernel,
        out_shape=jax.ShapeDtypeStruct((rows, query_width), BF16),
        compiler_params=PARAMS,
        cost_estimate=cost(2 * rows * rows * query_width, 4 * rows * query_width),
    )(grad_scores, key_states)
    return (grad_query, grad_input, grad_weights)


def solution(mesh):
    placed = (
        P("dp", "mp"),
        P("dp", "mp"),
        P("dp", "mp"),
        P("dp", "mp"),
        P("dp", None),
        P(None, None, "mp"),
    )
    return jax.shard_map(
        body,
        mesh=mesh,
        in_specs=placed,
        out_specs=(P("dp", "mp"), P("dp", "mp"), P("dp", "mp")),
        check_vma=False,
    )
```

```python
import math

import jax
import jax.numpy as jnp
from jax import lax
from jax.experimental import pallas as pl
from jax.experimental.pallas import tpu as pltpu
from jax.sharding import PartitionSpec as P

HEAD_SIZE = 128
F32 = jnp.float32
BF16 = jnp.bfloat16
NN = (((1,), (0,)), ((), ()))
NT = (((1,), (1,)), ((), ()))
TN = (((0,), (0,)), ((), ()))
IN_HBM = pl.BlockSpec(memory_space=pltpu.HBM)
ANYWHERE = pl.BlockSpec(memory_space=pl.ANY)
IN_VMEM = pl.BlockSpec(memory_space=pltpu.VMEM)
CHUNK = 512
PARAMS = pltpu.CompilerParams(vmem_limit_bytes=24 * 1024 * 1024)
WHOLE = pltpu.CompilerParams()


def dot(a, b, dims=NN):
    return lax.dot_general(a, b, dims, preferred_element_type=F32)


def cost(flops, moved, transcendentals=0):
    return pl.CostEstimate(flops=flops, bytes_accessed=moved, transcendentals=transcendentals)


def attention_group(g, q, k, v, do, gk_ref, ds):
    length = q.shape[0]
    per_group = q.shape[1] // k.shape[1]
    together = 2 - per_group % 2
    wide = together * length
    scale = 1.0 / math.sqrt(HEAD_SIZE)
    targets = lax.broadcasted_iota(jnp.int32, (length, wide), 0)
    positions = lax.rem(lax.broadcasted_iota(jnp.int32, (length, wide), 1), length)
    allowed = targets <= positions
    cols = slice(g * HEAD_SIZE, (g + 1) * HEAD_SIZE)
    key, value = k[:, cols], v[:, cols]
    acc_k = jnp.zeros((length, HEAD_SIZE), F32)
    acc_v = jnp.zeros((length, HEAD_SIZE), F32)
    for h in range(0, per_group, together):
        at = [(g * per_group + h + e) * HEAD_SIZE for e in range(together)]
        query = jnp.concatenate([q[:, s : s + HEAD_SIZE] for s in at], axis=0)
        grad = jnp.concatenate([do[:, s : s + HEAD_SIZE] for s in at], axis=0)
        scores = jnp.where(allowed, dot(key, query, NT), -1e30)
        raw = jnp.exp((scores - jnp.max(scores, axis=0, keepdims=True)) * scale)
        probs = raw * (1.0 / jnp.sum(raw, axis=0, keepdims=True))
        grad_probs = dot(value, grad, NT)
        delta = jnp.sum(probs * grad_probs, axis=0, keepdims=True)
        grad_scores = (probs * (grad_probs - delta)).astype(BF16)
        ds[:, at[0] : at[0] + wide] = grad_scores
        acc_v += dot(probs.astype(BF16), grad)
        acc_k += dot(grad_scores, query)
    gk_ref[:, cols] = (acc_k * scale).astype(BF16)
    return acc_v.astype(BF16)


def attention_kernel(
    q_hbm, k_hbm, v_hbm, do_hbm, p_hbm,
    gk_ref, ds_hbm, sent_hbm, kept_hbm,
    q, k, v, do, p, ds, partial, sems, p_sems, out_sems,
):
    kv_heads = k.shape[1] // HEAD_SIZE
    group = q.shape[1] // kv_heads
    groups, features = p.shape[0], p.shape[2]
    chips = groups // 2
    member = lax.axis_index("mp")
    chip, core = lax.div(member, 2), lax.rem(member, 2)
    small = [
        pltpu.make_async_copy(k_hbm, k, sems.at[0]),
        pltpu.make_async_copy(v_hbm, v, sems.at[1]),
    ]
    large, stored = [], []
    for g in range(kv_heads):
        cols = pl.ds(g * group, group)
        large.append((
            pltpu.make_async_copy(q_hbm.at[:, cols], q.at[:, cols], sems.at[2 + 2 * g]),
            pltpu.make_async_copy(do_hbm.at[:, cols], do.at[:, cols], sems.at[3 + 2 * g]),
        ))
        stored.append(pltpu.make_async_copy(ds.at[:, cols], ds_hbm.at[:, cols], out_sems.at[g]))
    blocks = []
    for b in range(groups):
        column = core if b >= chips else 1 - core
        start = (2 * lax.rem(chip + b + 1, chips) + column) * features
        rows = pl.ds(pl.multiple_of(start, features), features)
        blocks.append(pltpu.make_async_copy(p_hbm.at[:, rows, :], p.at[b], p_sems.at[b]))
    for copy in small:
        copy.start()
    for pair in large:
        for copy in pair:
            copy.start()
    for copy in blocks:
        copy.start()
    for copy in small:
        copy.wait()
    values = []
    for g in range(kv_heads):
        for copy in large[g]:
            copy.wait()
        values.append(attention_group(g, q, k, v, do, gk_ref, ds))
        stored[g].start()
    gk = gk_ref[...]
    gv = jnp.concatenate(values, axis=1)
    step = min(CHUNK, features)
    for b in range(groups):
        blocks[b].wait()
        for at in range(0, features, step):
            rows = slice(at, at + step)
            total = dot(p[b, 0, rows, :], gk, NT) + dot(p[b, 1, rows, :], gv, NT)
            partial[b, rows, :] = total.astype(BF16)
        target = sent_hbm.at[b] if b < chips else kept_hbm.at[b - chips]
        stored.append(pltpu.make_async_copy(partial.at[b], target, out_sems.at[kv_heads + b]))
        stored[-1].start()
    for copy in stored:
        copy.wait()


def query_kernel(ds_ref, k_ref, gq_ref):
    kv_heads = k_ref.shape[1] // HEAD_SIZE
    per_group = gq_ref.shape[1] // k_ref.shape[1]
    scale = 1.0 / math.sqrt(HEAD_SIZE)
    for g in range(kv_heads):
        key = k_ref[:, g * HEAD_SIZE : (g + 1) * HEAD_SIZE]
        for h in range(per_group):
            at = (g * per_group + h) * HEAD_SIZE
            grad = dot(ds_ref[:, at : at + HEAD_SIZE], key, TN) * scale
            gq_ref[:, at : at + HEAD_SIZE] = grad.astype(BF16)


def input_kernel(kept_ref, came_ref, *refs):
    out_ref = refs[-1]
    total = kept_ref[len(refs) - 1].astype(F32) + came_ref[len(refs) - 1].astype(F32)
    for ref in refs[:-1]:
        total += ref[...].astype(F32)
    out_ref[...] = total.T.astype(BF16)


def turned_kernel(mine_ref, theirs_ref, next_ref, x_hbm, out_ref, own, sem):
    rows, width = next_ref.shape
    parts = out_ref.shape[1] // rows
    far, groups = parts // 2, parts // 2
    part, member = lax.axis_index("dp"), lax.axis_index("mp")
    cols = pl.ds(pl.multiple_of(part * width, width), width)
    copy = pltpu.make_async_copy(x_hbm.at[:, cols], own, sem)
    copy.start()

    def put(k, piece):
        place = 2 * lax.rem(k, far) + lax.div(k, far)
        out_ref[:, pl.ds(pl.multiple_of(place * rows, rows), rows)] = piece.T

    partners = [lambda m, j=j: far + (m ^ j) for j in range(0, groups, 2)]
    partners += [lambda m, k=k: k + lax.rem(m, 2) for k in range(2, far, 2)]
    for at, partner in enumerate(partners):
        put(partner(member), mine_ref[at * rows : (at + 1) * rows, :])
        put(partner(member ^ 1), theirs_ref[at * rows : (at + 1) * rows, :])
    put(jnp.int32(1), next_ref[...])
    copy.wait()
    put(jnp.int32(0), own[...])


def weights_kernel(x_ref, *refs):
    keys, out_ref = refs[:-1], refs[-1]
    rows = keys[0].shape[0]
    total = dot(x_ref[:, :rows], keys[0][...])
    for j in range(1, len(keys)):
        total += dot(x_ref[:, j * rows : (j + 1) * rows], keys[j][...])
    out_ref[...] = total * (1.0 / (2 * len(keys)))


def along_dp(array, partner, parts, groups):
    pairs = [
        (i * groups + m, (i ^ partner(m)) * groups + m)
        for i in range(parts)
        for m in range(groups)
    ]
    return lax.ppermute(array, ("dp", "mp"), pairs)


def along_mp(array, bit, groups):
    return lax.ppermute(array, "mp", [(m, m ^ bit) for m in range(groups)])


def sent_inputs(inputs, parts, groups):
    far = parts // 2
    part, member = lax.axis_index("dp"), lax.axis_index("mp")
    rows, width = inputs.shape[0], inputs.shape[1] // parts

    def block(k):
        return lax.dynamic_slice(inputs, (0, (part ^ k) * width), (rows, width))

    arrived = [along_dp(block(far + member), lambda m: far + m, parts, groups)]
    for k in range(2, far, 2):
        block_k = block(k + lax.rem(member, 2))
        arrived.append(along_dp(block_k, lambda m, k=k: k + m % 2, parts, groups))
    return arrived, block(1)


def exchanged_weights(inputs, arrived, next_block, grad_key, parts, groups):
    far = parts // 2
    rows, columns = grad_key.shape
    width = inputs.shape[1] // parts

    keys = [jnp.concatenate([grad_key, along_dp(grad_key, lambda m: far, parts, groups)])]
    next_inputs = along_dp(next_block, lambda m: 1, parts, groups)
    shared = {0: arrived[0]}
    bit = groups // 2
    while bit > 1:
        for j in list(shared):
            shared[j ^ bit] = along_mp(shared[j], bit, groups)
        bit //= 2
    mine = jnp.concatenate([shared[j] for j in range(0, groups, 2)] + arrived[1:])
    theirs = along_mp(mine, 1, groups)
    by_k = {0: keys[0]}
    bit = far // 2
    while bit:
        for k in list(by_k):
            by_k[k ^ bit] = along_dp(by_k[k], lambda m, bit=bit: bit, parts, groups)
        bit //= 2

    turned = pl.pallas_call(
        turned_kernel,
        in_specs=[IN_VMEM, IN_VMEM, IN_VMEM, IN_HBM],
        out_specs=IN_VMEM,
        out_shape=jax.ShapeDtypeStruct((width, parts * rows), inputs.dtype),
        scratch_shapes=[pltpu.VMEM((rows, width), inputs.dtype), pltpu.SemaphoreType.DMA],
        compiler_params=PARAMS,
        cost_estimate=cost(0, 4 * parts * rows * width),
    )(mine, theirs, next_inputs, inputs)
    return pl.pallas_call(
        weights_kernel,
        in_specs=[IN_VMEM] * (1 + far),
        out_specs=IN_VMEM,
        out_shape=jax.ShapeDtypeStruct((width, columns), F32),
        compiler_params=PARAMS,
        cost_estimate=cost(
            2 * parts * rows * width * columns, 2 * parts * rows * (width + columns)
        ),
    )(turned, *[by_k[k] for k in range(far)])


def gathered_weights(inputs, grad_key, parts):
    rows = inputs.shape[0]
    width = inputs.shape[1] // parts
    blocks = inputs.reshape(rows, parts, width).transpose(1, 0, 2)
    mine = lax.all_to_all(blocks, "dp", split_axis=0, concat_axis=0, tiled=True)
    keys = lax.all_gather(grad_key, "dp", axis=0)
    return jnp.einsum("psd,psc->dc", mine, keys, preferred_element_type=F32) / parts


def body(query_states, key_states, value_states, grad_context, inputs_normed, projections):
    parts = lax.axis_size("dp")
    groups = lax.axis_size("mp")
    chips = groups // 2
    rows, width = key_states.shape
    query_width = query_states.shape[1]
    features = projections.shape[1] // groups
    kv_heads = width // HEAD_SIZE
    blocks = jax.ShapeDtypeStruct((chips, features, rows), BF16)
    exchange = parts == 2 * groups and inputs_normed.shape[1] % (parts * 128) == 0
    if exchange:
        arrived, next_block = sent_inputs(inputs_normed, parts, groups)

    grad_key, grad_scores, sent, kept = pl.pallas_call(
        attention_kernel,
        in_specs=[IN_HBM] * 5,
        out_specs=[IN_VMEM, ANYWHERE, ANYWHERE, ANYWHERE],
        out_shape=(
            jax.ShapeDtypeStruct((rows, width), BF16),
            jax.ShapeDtypeStruct((rows, query_width), BF16),
            blocks,
            blocks,
        ),
        scratch_shapes=[
            pltpu.VMEM((rows, query_width), BF16),
            pltpu.VMEM((rows, width), BF16),
            pltpu.VMEM((rows, width), BF16),
            pltpu.VMEM((rows, query_width), BF16),
            pltpu.VMEM((groups, 2, features, width), BF16),
            pltpu.VMEM((rows, query_width), BF16),
            pltpu.VMEM((groups, features, rows), BF16),
            pltpu.SemaphoreType.DMA((2 + 2 * kv_heads,)),
            pltpu.SemaphoreType.DMA((groups,)),
            pltpu.SemaphoreType.DMA((kv_heads + groups,)),
        ],
        compiler_params=WHOLE,
        cost_estimate=cost(
            8 * rows * rows * query_width + 4 * rows * width * features * groups,
            6 * rows * query_width + 4 * width * features * groups,
            rows * query_width,
        ),
    )(query_states, key_states, value_states, grad_context, projections)

    if exchange:
        grad_weights = exchanged_weights(
            inputs_normed, arrived, next_block, grad_key, parts, groups
        )
    else:
        grad_weights = gathered_weights(inputs_normed, grad_key, parts)

    came = along_mp(sent, 1, groups)
    last = []
    for b in range(chips - 1):
        pair = (kept[b].astype(F32) + came[b].astype(F32)).astype(BF16)
        shift = [(m, (m + 2 * (b + 1)) % groups) for m in range(groups)]
        last.append(lax.ppermute(pair, "mp", shift))
    grad_input = pl.pallas_call(
        input_kernel,
        out_specs=IN_VMEM,
        out_shape=jax.ShapeDtypeStruct((rows, features), BF16),
        compiler_params=PARAMS,
        cost_estimate=cost(rows * features, 8 * rows * features),
    )(kept, came, *last)

    grad_query = pl.pallas_call(
        query_kernel,
        out_shape=jax.ShapeDtypeStruct((rows, query_width), BF16),
        compiler_params=PARAMS,
        cost_estimate=cost(2 * rows * rows * query_width, 4 * rows * query_width),
    )(grad_scores, key_states)
    return (grad_query, grad_input, grad_weights)


def solution(mesh):
    placed = (
        P("dp", "mp"),
        P("dp", "mp"),
        P("dp", "mp"),
        P("dp", "mp"),
        P("dp", None),
        P(None, None, "mp"),
    )
    return jax.shard_map(
        body,
        mesh=mesh,
        in_specs=placed,
        out_specs=(P("dp", "mp"), P("dp", "mp"), P("dp", "mp")),
        check_vma=False,
    )
```

```python
import math

import jax
import jax.numpy as jnp
from jax import lax
from jax.experimental import pallas as pl
from jax.experimental.pallas import tpu as pltpu
from jax.sharding import PartitionSpec as P

HEAD_SIZE = 128
F32 = jnp.float32
BF16 = jnp.bfloat16
NN = (((1,), (0,)), ((), ()))
NT = (((1,), (1,)), ((), ()))
TN = (((0,), (0,)), ((), ()))
IN_HBM = pl.BlockSpec(memory_space=pltpu.HBM)
ANYWHERE = pl.BlockSpec(memory_space=pl.ANY)
IN_VMEM = pl.BlockSpec(memory_space=pltpu.VMEM)
CHUNK = 512
PARAMS = pltpu.CompilerParams(vmem_limit_bytes=24 * 1024 * 1024)
WHOLE = pltpu.CompilerParams(vmem_limit_bytes=60 * 1024 * 1024)


def dot(a, b, dims=NN):
    return lax.dot_general(a, b, dims, preferred_element_type=F32)


def cost(flops, moved, transcendentals=0):
    return pl.CostEstimate(flops=flops, bytes_accessed=moved, transcendentals=transcendentals)


def attention_group(g, q, k, v, do, gk_ref, gv_ref, ds):
    length = q.shape[0]
    per_group = q.shape[1] // k.shape[1]
    together = 2 - per_group % 2
    wide = together * length
    scale = 1.0 / math.sqrt(HEAD_SIZE)
    targets = lax.broadcasted_iota(jnp.int32, (length, wide), 0)
    positions = lax.rem(lax.broadcasted_iota(jnp.int32, (length, wide), 1), length)
    allowed = targets <= positions
    cols = slice(g * HEAD_SIZE, (g + 1) * HEAD_SIZE)
    key, value = k[:, cols], v[:, cols]
    acc_k = jnp.zeros((length, HEAD_SIZE), F32)
    acc_v = jnp.zeros((length, HEAD_SIZE), F32)
    for h in range(0, per_group, together):
        at = [(g * per_group + h + e) * HEAD_SIZE for e in range(together)]
        query = jnp.concatenate([q[:, s : s + HEAD_SIZE] for s in at], axis=0)
        grad = jnp.concatenate([do[:, s : s + HEAD_SIZE] for s in at], axis=0)
        scores = jnp.where(allowed, dot(key, query, NT), -1e30)
        raw = jnp.exp((scores - jnp.max(scores, axis=0, keepdims=True)) * scale)
        probs = raw * (1.0 / jnp.sum(raw, axis=0, keepdims=True))
        grad_probs = dot(value, grad, NT)
        delta = jnp.sum(probs * grad_probs, axis=0, keepdims=True)
        grad_scores = (probs * (grad_probs - delta)).astype(BF16)
        ds[:, at[0] : at[0] + wide] = grad_scores
        acc_v += dot(probs.astype(BF16), grad)
        acc_k += dot(grad_scores, query)
    gk_ref[:, cols] = (acc_k * scale).astype(BF16)
    gv_ref[:, cols] = acc_v.astype(BF16)


def blocks_of_partial(p_hbm, p, sems, own):
    chips, features = p.shape[0], p.shape[2]
    member = lax.axis_index("mp")
    chip, core = lax.div(member, 2), lax.rem(member, 2)
    column = core if own else 1 - core
    copies = []
    for b in range(chips):
        start = (2 * lax.rem(chip + b + 1, chips) + column) * features
        rows = pl.ds(pl.multiple_of(start, features), features)
        copies.append(pltpu.make_async_copy(p_hbm.at[:, rows, :], p.at[b], sems.at[b]))
    return copies


def partials(copies, p, gk, gv, out_ref):
    features = p.shape[2]
    step = min(CHUNK, features)
    for b, copy in enumerate(copies):
        copy.wait()
        for at in range(0, features, step):
            rows = slice(at, at + step)
            total = dot(p[b, 0, rows, :], gk, NT) + dot(p[b, 1, rows, :], gv, NT)
            out_ref[b, rows, :] = total.astype(BF16)


def attention_kernel(
    q_hbm, k_hbm, v_hbm, do_hbm, p_hbm,
    gk_ref, gv_ref, sent_ref, ds_hbm,
    q, k, v, do, p, ds, sems, p_sems, out_sems,
):
    kv_heads = k.shape[1] // HEAD_SIZE
    group = q.shape[1] // kv_heads
    small = [
        pltpu.make_async_copy(k_hbm, k, sems.at[0]),
        pltpu.make_async_copy(v_hbm, v, sems.at[1]),
    ]
    large, stored = [], []
    for g in range(kv_heads):
        cols = pl.ds(g * group, group)
        large.append((
            pltpu.make_async_copy(q_hbm.at[:, cols], q.at[:, cols], sems.at[2 + 2 * g]),
            pltpu.make_async_copy(do_hbm.at[:, cols], do.at[:, cols], sems.at[3 + 2 * g]),
        ))
        stored.append(pltpu.make_async_copy(ds.at[:, cols], ds_hbm.at[:, cols], out_sems.at[g]))
    blocks = blocks_of_partial(p_hbm, p, p_sems, own=False)
    for copy in small:
        copy.start()
    for pair in large:
        for copy in pair:
            copy.start()
    for copy in blocks:
        copy.start()
    for copy in small:
        copy.wait()
    for g in range(kv_heads):
        for copy in large[g]:
            copy.wait()
        attention_group(g, q, k, v, do, gk_ref, gv_ref, ds)
        stored[g].start()
    partials(blocks, p, gk_ref[...], gv_ref[...], sent_ref)
    for copy in stored:
        copy.wait()


def kept_kernel(gk_ref, gv_ref, p_hbm, kept_ref, p, p_sems):
    blocks = blocks_of_partial(p_hbm, p, p_sems, own=True)
    for copy in blocks:
        copy.start()
    partials(blocks, p, gk_ref[...], gv_ref[...], kept_ref)


def query_kernel(ds_hbm, k_hbm, gq_hbm, ds, k, gq, sems, out_sems):
    kv_heads = k.shape[1] // HEAD_SIZE
    group = gq.shape[1] // kv_heads
    scale = 1.0 / math.sqrt(HEAD_SIZE)
    key_copy = pltpu.make_async_copy(k_hbm, k, sems.at[kv_heads])
    key_copy.start()
    loads, stores = [], []
    for g in range(kv_heads):
        cols = pl.ds(g * group, group)
        loads.append(pltpu.make_async_copy(ds_hbm.at[:, cols], ds.at[:, cols], sems.at[g]))
        stores.append(pltpu.make_async_copy(gq.at[:, cols], gq_hbm.at[:, cols], out_sems.at[g]))
        loads[-1].start()
    key_copy.wait()
    for g in range(kv_heads):
        loads[g].wait()
        key = k[:, g * HEAD_SIZE : (g + 1) * HEAD_SIZE]
        for at in range(g * group, (g + 1) * group, HEAD_SIZE):
            grad = dot(ds[:, at : at + HEAD_SIZE], key, TN) * scale
            gq[:, at : at + HEAD_SIZE] = grad.astype(BF16)
        stores[g].start()
    for copy in stores:
        copy.wait()


def input_kernel(kept_ref, came_ref, *refs):
    out_ref = refs[-1]
    total = kept_ref[len(refs) - 1].astype(F32) + came_ref[len(refs) - 1].astype(F32)
    for ref in refs[:-1]:
        total += ref[...].astype(F32)
    out_ref[...] = total.T.astype(BF16)


def turned_kernel(mine_ref, theirs_ref, out_ref):
    parts = 2 * lax.axis_size("mp")
    far = parts // 2
    rows = out_ref.shape[1] // parts
    member = lax.axis_index("mp")

    def put(k, piece):
        place = far * lax.rem(k, 2) + 2 * lax.div(lax.rem(k, far), 2) + lax.div(k, far)
        out_ref[:, pl.ds(pl.multiple_of(place * rows, rows), rows)] = piece.T

    for at in range(far):
        k = far * (at % 2) + (member ^ (at // 2 * 2))
        put(k, mine_ref[at * rows : (at + 1) * rows, :])
        put(k ^ 1, theirs_ref[at * rows : (at + 1) * rows, :])


def weights_kernel(x_ref, *refs):
    keys, out_ref = refs[:-1], refs[-1]
    rows = keys[0].shape[0]
    total = dot(x_ref[:, :rows], keys[0][...])
    for j in range(1, len(keys)):
        total += dot(x_ref[:, j * rows : (j + 1) * rows], keys[j][...])
    out_ref[...] = total * (1.0 / (2 * len(keys)))


def along_dp(array, partner, parts, groups):
    pairs = [
        (i * groups + m, (i ^ partner(m)) * groups + m)
        for i in range(parts)
        for m in range(groups)
    ]
    return lax.ppermute(array, ("dp", "mp"), pairs)


def along_mp(array, bit, groups):
    return lax.ppermute(array, "mp", [(m, m ^ bit) for m in range(groups)])


def sent_inputs(inputs, parts, groups):
    far = parts // 2
    part, member = lax.axis_index("dp"), lax.axis_index("mp")
    rows, width = inputs.shape[0], inputs.shape[1] // parts

    def sent(k):
        block = lax.dynamic_slice(inputs, (0, (part ^ (k + member)) * width), (rows, width))
        return along_dp(block, lambda m: k + m, parts, groups)

    return sent(0), sent(far)


def gathered_inputs(arrived, after, parts, groups):
    rows, width = arrived.shape[0] // 2, arrived.shape[1]
    pieces = [arrived]
    bit = 2
    while bit < groups:
        pieces += [along_mp(piece, bit, groups) for piece in pieces]
        bit *= 2
    pieces, _ = lax.optimization_barrier((pieces, after))
    mine = jnp.concatenate(pieces)
    theirs = along_mp(mine, 1, groups)
    return pl.pallas_call(
        turned_kernel,
        out_specs=IN_VMEM,
        out_shape=jax.ShapeDtypeStruct((width, parts * rows), arrived.dtype),
        compiler_params=PARAMS,
        cost_estimate=cost(0, 4 * parts * rows * width),
    )(mine, theirs)


def gathered_keys(first, parts, groups):
    far = parts // 2
    keys = {0: first}
    bit = far // 2
    while bit > 1:
        for k in list(keys):
            keys[k ^ bit] = along_dp(keys[k], lambda m, bit=bit: bit, parts, groups)
        bit //= 2
    return [keys[k] for k in range(0, far, 2)]


def summed_weights(turned, keys):
    width, columns = turned.shape[0], keys[0].shape[1]
    return pl.pallas_call(
        weights_kernel,
        out_specs=IN_VMEM,
        out_shape=jax.ShapeDtypeStruct((width, columns), F32),
        compiler_params=PARAMS,
        cost_estimate=cost(
            2 * turned.size * columns, 2 * turned.size + 4 * width * columns
        ),
    )(turned, *keys)


def gathered_weights(inputs, grad_key, parts):
    rows = inputs.shape[0]
    width = inputs.shape[1] // parts
    blocks = inputs.reshape(rows, parts, width).transpose(1, 0, 2)
    mine = lax.all_to_all(blocks, "dp", split_axis=0, concat_axis=0, tiled=True)
    keys = lax.all_gather(grad_key, "dp", axis=0)
    return jnp.einsum("psd,psc->dc", mine, keys, preferred_element_type=F32) / parts


def body(query_states, key_states, value_states, grad_context, inputs_normed, projections):
    parts = lax.axis_size("dp")
    groups = lax.axis_size("mp")
    chips = groups // 2
    rows, width = key_states.shape
    query_width = query_states.shape[1]
    features = projections.shape[1] // groups
    kv_heads = width // HEAD_SIZE
    partial = jax.ShapeDtypeStruct((chips, features, rows), BF16)
    exchange = parts == 2 * groups and inputs_normed.shape[1] % (parts * 128) == 0
    if exchange:
        near, distant = sent_inputs(inputs_normed, parts, groups)

    p_scratch = [
        pltpu.VMEM((chips, 2, features, width), BF16),
        pltpu.SemaphoreType.DMA((chips,)),
    ]
    whole = pltpu.VMEM((rows, query_width), BF16)
    narrow = pltpu.VMEM((rows, width), BF16)
    grad_key, grad_value, sent, grad_scores = pl.pallas_call(
        attention_kernel,
        in_specs=[IN_HBM] * 5,
        out_specs=[IN_VMEM, IN_VMEM, IN_VMEM, ANYWHERE],
        out_shape=(
            jax.ShapeDtypeStruct((rows, width), BF16),
            jax.ShapeDtypeStruct((rows, width), BF16),
            partial,
            jax.ShapeDtypeStruct((rows, query_width), BF16),
        ),
        scratch_shapes=[whole, narrow, narrow, whole, p_scratch[0], whole]
        + [pltpu.SemaphoreType.DMA((2 + 2 * kv_heads,)), p_scratch[1]]
        + [pltpu.SemaphoreType.DMA((kv_heads,))],
        compiler_params=WHOLE,
        cost_estimate=cost(
            8 * rows * rows * query_width + 4 * rows * width * features * chips,
            6 * rows * query_width + 4 * width * features * chips,
            rows * query_width,
        ),
    )(query_states, key_states, value_states, grad_context, projections)

    if exchange:
        ready, near = lax.optimization_barrier((grad_key, near))
        first = along_dp(ready, lambda m: parts // 2, parts, groups)
        arrived = jnp.concatenate([near, distant])
        grad_value, sent, arrived = lax.optimization_barrier((grad_value, sent, arrived))
    came = along_mp(sent, 1, groups)
    kept = pl.pallas_call(
        kept_kernel,
        in_specs=[IN_VMEM, IN_VMEM, IN_HBM],
        out_specs=IN_VMEM,
        out_shape=partial,
        scratch_shapes=p_scratch,
        compiler_params=WHOLE,
        cost_estimate=cost(
            4 * rows * width * features * chips, 4 * width * features * chips
        ),
    )(grad_key, grad_value, projections)
    if exchange:
        kept, first = lax.optimization_barrier((kept, first))
        keys = gathered_keys(jnp.concatenate([grad_key, first]), parts, groups)
        keys += [along_dp(key, lambda m: 1, parts, groups) for key in keys]
    last, pairs = [], []
    for b in range(chips - 1):
        pairs.append((kept[b].astype(F32) + came[b].astype(F32)).astype(BF16))
        shift = [(m, (m + 2 * (b + 1)) % groups) for m in range(groups)]
        last.append(lax.ppermute(pairs[b], "mp", shift))
    if exchange:
        turned = gathered_inputs(arrived, (keys[parts // 4 - 1], keys[parts // 4], pairs), parts, groups)
    grad_input = pl.pallas_call(
        input_kernel,
        out_specs=IN_VMEM,
        out_shape=jax.ShapeDtypeStruct((rows, features), BF16),
        compiler_params=PARAMS,
        cost_estimate=cost(rows * features, 8 * rows * features),
    )(kept, came, *last)

    grad_query = pl.pallas_call(
        query_kernel,
        in_specs=[IN_HBM, IN_HBM],
        out_specs=ANYWHERE,
        out_shape=jax.ShapeDtypeStruct((rows, query_width), BF16),
        scratch_shapes=[whole, narrow, whole]
        + [pltpu.SemaphoreType.DMA((1 + kv_heads,)), pltpu.SemaphoreType.DMA((kv_heads,))],
        compiler_params=WHOLE,
        cost_estimate=cost(2 * rows * rows * query_width, 4 * rows * query_width),
    )(grad_scores, key_states)

    if exchange:
        keys[-1], grad_input, grad_query = lax.optimization_barrier(
            (keys[-1], grad_input, grad_query)
        )
        grad_weights = summed_weights(turned, keys)
    else:
        grad_weights = gathered_weights(inputs_normed, grad_key, parts)
    return (grad_query, grad_input, grad_weights)


def solution(mesh):
    placed = (
        P("dp", "mp"),
        P("dp", "mp"),
        P("dp", "mp"),
        P("dp", "mp"),
        P("dp", None),
        P(None, None, "mp"),
    )
    return jax.shard_map(
        body,
        mesh=mesh,
        in_specs=placed,
        out_specs=(P("dp", "mp"), P("dp", "mp"), P("dp", "mp")),
        check_vma=False,
    )
```

```python
import math

import jax
import jax.numpy as jnp
from jax import lax
from jax.experimental import pallas as pl
from jax.experimental.pallas import tpu as pltpu
from jax.sharding import PartitionSpec as P

HEAD_SIZE = 128
F32 = jnp.float32
BF16 = jnp.bfloat16
NN = (((1,), (0,)), ((), ()))
NT = (((1,), (1,)), ((), ()))
TN = (((0,), (0,)), ((), ()))
IN_HBM = pl.BlockSpec(memory_space=pltpu.HBM)
ANYWHERE = pl.BlockSpec(memory_space=pl.ANY)
IN_VMEM = pl.BlockSpec(memory_space=pltpu.VMEM)
CHUNK = 512
PARAMS = pltpu.CompilerParams(vmem_limit_bytes=24 * 1024 * 1024)
WHOLE = pltpu.CompilerParams(vmem_limit_bytes=60 * 1024 * 1024)


def dot(a, b, dims=NN):
    return lax.dot_general(a, b, dims, preferred_element_type=F32)


def cost(flops, moved, transcendentals=0):
    return pl.CostEstimate(flops=flops, bytes_accessed=moved, transcendentals=transcendentals)


def attention_scores(g, q, k, v, do, scores, grad_probs):
    per_group = q.shape[1] // k.shape[1]
    cols = slice(g * HEAD_SIZE, (g + 1) * HEAD_SIZE)
    scores[g] = dot(k[:, cols], stacked(q, g, per_group), NT)
    grad_probs[g] = dot(v[:, cols], stacked(do, g, per_group), NT)


def stacked(array, g, per_group):
    first = g * per_group * HEAD_SIZE
    heads = [array[:, first + h * HEAD_SIZE : first + (h + 1) * HEAD_SIZE] for h in range(per_group)]
    return jnp.concatenate(heads, axis=0)


def attention_softmax(g, scores, grad_probs, probs_b, ds):
    length = scores.shape[1]
    group = scores.shape[2]
    scale = 1.0 / math.sqrt(HEAD_SIZE)
    targets = lax.broadcasted_iota(jnp.int32, (length, length), 0)
    positions = lax.broadcasted_iota(jnp.int32, (length, length), 1)
    allowed = targets <= positions
    for at in range(0, group, length):
        cols = slice(at, at + length)
        masked = jnp.where(allowed, scores[g, :, cols], -1e30)
        raw = jnp.exp((masked - jnp.max(masked, axis=0, keepdims=True)) * scale)
        probs = raw * (1.0 / jnp.sum(raw, axis=0, keepdims=True))
        slopes = grad_probs[g, :, cols]
        delta = jnp.sum(probs * slopes, axis=0, keepdims=True)
        probs_b[:, g * group + at : g * group + at + length] = probs.astype(BF16)
        ds[:, g * group + at : g * group + at + length] = (probs * (slopes - delta)).astype(BF16)


def attention_kernel(
    q_hbm, k_hbm, v_hbm, do_hbm, p_hbm,
    gk_ref, ds_hbm, sent_hbm, kept_hbm,
    q, k, v, do, p, probs_b, ds, scores, grad_probs, partial, sems, p_sems, out_sems,
):
    kv_heads = k.shape[1] // HEAD_SIZE
    group = q.shape[1] // kv_heads
    per_group = group // HEAD_SIZE
    groups, features = p.shape[0], p.shape[2]
    chips = groups // 2
    member = lax.axis_index("mp")
    chip, core = lax.div(member, 2), lax.rem(member, 2)
    small = [
        pltpu.make_async_copy(k_hbm, k, sems.at[0]),
        pltpu.make_async_copy(v_hbm, v, sems.at[1]),
    ]
    large, stored = [], []
    for g in range(kv_heads):
        cols = pl.ds(g * group, group)
        large.append((
            pltpu.make_async_copy(q_hbm.at[:, cols], q.at[:, cols], sems.at[2 + 2 * g]),
            pltpu.make_async_copy(do_hbm.at[:, cols], do.at[:, cols], sems.at[3 + 2 * g]),
        ))
        stored.append(pltpu.make_async_copy(ds.at[:, cols], ds_hbm.at[:, cols], out_sems.at[g]))
    blocks = []
    for b in range(groups):
        column = core if b >= chips else 1 - core
        start = (2 * lax.rem(chip + b + 1, chips) + column) * features
        rows = pl.ds(pl.multiple_of(start, features), features)
        blocks.append(pltpu.make_async_copy(p_hbm.at[:, rows, :], p.at[b], p_sems.at[b]))
    for copy in small:
        copy.start()
    for pair in large:
        for copy in pair:
            copy.start()
    for copy in blocks:
        copy.start()
    for copy in small:
        copy.wait()
    for g in range(kv_heads):
        for copy in large[g]:
            copy.wait()
        attention_scores(g, q, k, v, do, scores, grad_probs)
    scale = 1.0 / math.sqrt(HEAD_SIZE)
    values, keys = [], []
    for g in range(kv_heads):
        attention_softmax(g, scores, grad_probs, probs_b, ds)
        stored[g].start()
        cols = slice(g * group, (g + 1) * group)
        values.append(dot(probs_b[:, cols], stacked(do, g, per_group)).astype(BF16))
        keys.append((dot(ds[:, cols], stacked(q, g, per_group)) * scale).astype(BF16))
    gk = jnp.concatenate(keys, axis=1)
    gk_ref[...] = gk
    grads = jnp.concatenate([gk] + values, axis=1)
    step = min(CHUNK, features)
    for b in range(groups):
        blocks[b].wait()
        for at in range(0, features, step):
            rows = slice(at, at + step)
            both = jnp.concatenate([p[b, 0, rows, :], p[b, 1, rows, :]], axis=1)
            partial[b, rows, :] = dot(both, grads, NT).astype(BF16)
        target = sent_hbm.at[b] if b < chips else kept_hbm.at[b - chips]
        stored.append(pltpu.make_async_copy(partial.at[b], target, out_sems.at[kv_heads + b]))
        stored[-1].start()
    for copy in stored:
        copy.wait()


def query_kernel(ds_hbm, k_hbm, gq_hbm, ds, k, gq, sems, out_sems):
    kv_heads = k.shape[1] // HEAD_SIZE
    group = gq.shape[1] // kv_heads
    scale = 1.0 / math.sqrt(HEAD_SIZE)
    key_copy = pltpu.make_async_copy(k_hbm, k, sems.at[kv_heads])
    key_copy.start()
    loads, stores = [], []
    for g in range(kv_heads):
        cols = pl.ds(g * group, group)
        loads.append(pltpu.make_async_copy(ds_hbm.at[:, cols], ds.at[:, cols], sems.at[g]))
        stores.append(pltpu.make_async_copy(gq.at[:, cols], gq_hbm.at[:, cols], out_sems.at[g]))
        loads[-1].start()
    key_copy.wait()
    for g in range(kv_heads):
        loads[g].wait()
        key = k[:, g * HEAD_SIZE : (g + 1) * HEAD_SIZE]
        for at in range(g * group, (g + 1) * group, HEAD_SIZE):
            grad = dot(ds[:, at : at + HEAD_SIZE], key, TN) * scale
            gq[:, at : at + HEAD_SIZE] = grad.astype(BF16)
        stores[g].start()
    for copy in stores:
        copy.wait()


def input_kernel(kept_ref, came_ref, *refs):
    out_ref = refs[-1]
    total = kept_ref[len(refs) - 1].astype(F32) + came_ref[len(refs) - 1].astype(F32)
    for ref in refs[:-1]:
        total += ref[...].astype(F32)
    out_ref[...] = total.T.astype(BF16)


def turned_kernel(mine_ref, theirs_ref, next_ref, x_hbm, out_ref, own, sem):
    rows, width = next_ref.shape
    parts = out_ref.shape[1] // rows
    far = groups = parts // 2
    part, member = lax.axis_index("dp"), lax.axis_index("mp")
    cols = pl.ds(pl.multiple_of(part * width, width), width)
    copy = pltpu.make_async_copy(x_hbm.at[:, cols], own, sem)
    copy.start()

    def put(k, piece):
        place = far * lax.rem(k, 2) + 2 * lax.div(lax.rem(k, far), 2) + lax.div(k, far)
        out_ref[:, pl.ds(pl.multiple_of(place * rows, rows), rows)] = piece.T

    partners = [far + (member ^ j) for j in range(0, groups, 2)]
    partners += [k + lax.rem(member, 2) for k in range(2, far, 2)]
    for at, k in enumerate(partners):
        put(k, mine_ref[at * rows : (at + 1) * rows, :])
        put(k ^ 1, theirs_ref[at * rows : (at + 1) * rows, :])
    put(jnp.int32(1), next_ref[...])
    copy.wait()
    put(jnp.int32(0), own[...])


def weights_kernel(x_ref, *refs):
    keys, out_ref = refs[:-1], refs[-1]
    rows = keys[0].shape[0]
    total = dot(x_ref[:, :rows], keys[0][...])
    for j in range(1, len(keys)):
        total += dot(x_ref[:, j * rows : (j + 1) * rows], keys[j][...])
    out_ref[...] = total * (1.0 / (2 * len(keys)))


def along_dp(array, partner, parts, groups):
    pairs = [
        (i * groups + m, (i ^ partner(m)) * groups + m)
        for i in range(parts)
        for m in range(groups)
    ]
    return lax.ppermute(array, ("dp", "mp"), pairs)


def along_mp(array, bit, groups):
    return lax.ppermute(array, "mp", [(m, m ^ bit) for m in range(groups)])


def sent_inputs(inputs, parts, groups):
    far = parts // 2
    part, member = lax.axis_index("dp"), lax.axis_index("mp")
    rows, width = inputs.shape[0], inputs.shape[1] // parts

    def block(k):
        return lax.dynamic_slice(inputs, (0, (part ^ k) * width), (rows, width))

    distant = along_dp(block(far + member), lambda m: far + m, parts, groups)
    near = []
    for k in range(2, far, 2):
        sent = block(k + lax.rem(member, 2))
        near.append(along_dp(sent, lambda m, k=k: k + m % 2, parts, groups))
    return distant, near, along_dp(block(1), lambda m: 1, parts, groups)


def shared_inputs(piece, groups):
    pieces = [piece]
    bit = 2
    while bit < groups:
        pieces += [along_mp(piece, bit, groups) for piece in pieces]
        bit *= 2
    return pieces


def turned_inputs(mine, theirs, next_inputs, inputs):
    rows, width = next_inputs.shape
    return pl.pallas_call(
        turned_kernel,
        in_specs=[IN_VMEM, IN_VMEM, IN_VMEM, IN_HBM],
        out_specs=IN_VMEM,
        out_shape=jax.ShapeDtypeStruct((width, inputs.shape[1] // width * rows), inputs.dtype),
        scratch_shapes=[pltpu.VMEM((rows, width), inputs.dtype), pltpu.SemaphoreType.DMA],
        compiler_params=PARAMS,
        cost_estimate=cost(0, 4 * inputs.size),
    )(mine, theirs, next_inputs, inputs)


def summed_weights(turned, keys):
    width, columns = turned.shape[0], keys[0].shape[1]
    return pl.pallas_call(
        weights_kernel,
        out_specs=IN_VMEM,
        out_shape=jax.ShapeDtypeStruct((width, columns), F32),
        compiler_params=PARAMS,
        cost_estimate=cost(
            2 * turned.size * columns, 2 * turned.size + 4 * width * columns
        ),
    )(turned, *keys)


def gathered_weights(inputs, grad_key, parts):
    rows = inputs.shape[0]
    width = inputs.shape[1] // parts
    blocks = inputs.reshape(rows, parts, width).transpose(1, 0, 2)
    mine = lax.all_to_all(blocks, "dp", split_axis=0, concat_axis=0, tiled=True)
    keys = lax.all_gather(grad_key, "dp", axis=0)
    return jnp.einsum("psd,psc->dc", mine, keys, preferred_element_type=F32) / parts


def body(query_states, key_states, value_states, grad_context, inputs_normed, projections):
    parts = lax.axis_size("dp")
    groups = lax.axis_size("mp")
    chips = groups // 2
    rows, width = key_states.shape
    query_width = query_states.shape[1]
    features = projections.shape[1] // groups
    kv_heads = width // HEAD_SIZE
    partial = jax.ShapeDtypeStruct((chips, features, rows), BF16)
    exchange = parts == 2 * groups and inputs_normed.shape[1] % (parts * 128) == 0
    if exchange:
        distant, near, next_inputs = sent_inputs(inputs_normed, parts, groups)

    whole = pltpu.VMEM((rows, query_width), BF16)
    narrow = pltpu.VMEM((rows, width), BF16)
    wide = pltpu.VMEM((kv_heads, rows, query_width // kv_heads), F32)
    grad_key, grad_scores, sent, kept = pl.pallas_call(
        attention_kernel,
        in_specs=[IN_HBM] * 5,
        out_specs=[IN_VMEM, ANYWHERE, ANYWHERE, ANYWHERE],
        out_shape=(
            jax.ShapeDtypeStruct((rows, width), BF16),
            jax.ShapeDtypeStruct((rows, query_width), BF16),
            partial,
            partial,
        ),
        scratch_shapes=[whole, narrow, narrow, whole]
        + [pltpu.VMEM((groups, 2, features, width), BF16), whole, whole, wide, wide]
        + [pltpu.VMEM((groups, features, rows), BF16)]
        + [pltpu.SemaphoreType.DMA((2 + 2 * kv_heads,)), pltpu.SemaphoreType.DMA((groups,))]
        + [pltpu.SemaphoreType.DMA((kv_heads + groups,))],
        compiler_params=WHOLE,
        cost_estimate=cost(
            8 * rows * rows * query_width + 4 * rows * width * features * groups,
            6 * rows * query_width + 4 * width * features * groups,
            rows * query_width,
        ),
    )(query_states, key_states, value_states, grad_context, projections)

    grad_query = pl.pallas_call(
        query_kernel,
        in_specs=[IN_HBM, IN_HBM],
        out_specs=ANYWHERE,
        out_shape=jax.ShapeDtypeStruct((rows, query_width), BF16),
        scratch_shapes=[whole, narrow, whole]
        + [pltpu.SemaphoreType.DMA((1 + kv_heads,)), pltpu.SemaphoreType.DMA((kv_heads,))],
        compiler_params=WHOLE,
        cost_estimate=cost(2 * rows * rows * query_width, 4 * rows * query_width),
    )(grad_scores, key_states)

    if exchange:
        ready, near, next_inputs = lax.optimization_barrier((grad_key, near, next_inputs))
        sent, distant, near = lax.optimization_barrier((sent, distant, near))
        first = along_dp(ready, lambda m: parts // 2, parts, groups)
        pieces = shared_inputs(distant, groups)
    came = along_mp(sent, 1, groups)
    pairs = [(kept[b].astype(F32) + came[b].astype(F32)).astype(BF16) for b in range(chips - 1)]
    if exchange:
        first, pieces, pairs = lax.optimization_barrier((first, pieces, pairs))
        keys = {0: jnp.concatenate([grad_key, first])}
        mine = jnp.concatenate(pieces + near)
        theirs = along_mp(mine, 1, groups)
        bit = parts // 4
        while bit > 1:
            for k in list(keys):
                keys[k ^ bit] = along_dp(keys[k], lambda m, bit=bit: bit, parts, groups)
            bit //= 2
    last = []
    for b in range(chips - 1):
        shift = [(m, (m + 2 * (b + 1)) % groups) for m in range(groups)]
        last.append(lax.ppermute(pairs[b], "mp", shift))
    grad_input = pl.pallas_call(
        input_kernel,
        out_specs=IN_VMEM,
        out_shape=jax.ShapeDtypeStruct((rows, features), BF16),
        compiler_params=PARAMS,
        cost_estimate=cost(rows * features, 8 * rows * features),
    )(kept, came, *last)

    if exchange:
        beside = []
        for k in range(0, parts // 2, 2):
            pair, beside = lax.optimization_barrier((keys[k], beside))
            beside.append(along_dp(pair, lambda m: 1, parts, groups))
        turned = turned_inputs(mine, theirs, next_inputs, inputs_normed)
        beside[-1], grad_input = lax.optimization_barrier((beside[-1], grad_input))
        keys = [keys[k] for k in range(0, parts // 2, 2)] + beside
        grad_weights = summed_weights(turned, keys)
    else:
        grad_weights = gathered_weights(inputs_normed, grad_key, parts)
    return (grad_query, grad_input, grad_weights)


def solution(mesh):
    placed = (
        P("dp", "mp"),
        P("dp", "mp"),
        P("dp", "mp"),
        P("dp", "mp"),
        P("dp", None),
        P(None, None, "mp"),
    )
    return jax.shard_map(
        body,
        mesh=mesh,
        in_specs=placed,
        out_specs=(P("dp", "mp"), P("dp", "mp"), P("dp", "mp")),
        check_vma=False,
    )
```

```python
import math

import jax
import jax.numpy as jnp
from jax import lax
from jax.experimental import pallas as pl
from jax.experimental.pallas import tpu as pltpu
from jax.sharding import PartitionSpec as P

HEAD_SIZE = 128
F32 = jnp.float32
BF16 = jnp.bfloat16
NN = (((1,), (0,)), ((), ()))
NT = (((1,), (1,)), ((), ()))
TN = (((0,), (0,)), ((), ()))
IN_HBM = pl.BlockSpec(memory_space=pltpu.HBM)
ANYWHERE = pl.BlockSpec(memory_space=pl.ANY)
IN_VMEM = pl.BlockSpec(memory_space=pltpu.VMEM)
CHUNK = 512
PARAMS = pltpu.CompilerParams(vmem_limit_bytes=24 * 1024 * 1024)
WHOLE = pltpu.CompilerParams(vmem_limit_bytes=60 * 1024 * 1024)


def dot(a, b, dims=NN):
    return lax.dot_general(a, b, dims, preferred_element_type=F32)


def cost(flops, moved, transcendentals=0):
    return pl.CostEstimate(flops=flops, bytes_accessed=moved, transcendentals=transcendentals)


def attention_scores(g, q, k, v, do, scores, grad_probs):
    per_group = q.shape[1] // k.shape[1]
    cols = slice(g * HEAD_SIZE, (g + 1) * HEAD_SIZE)
    scores[g] = dot(k[:, cols], stacked(q, g, per_group), NT)
    grad_probs[g] = dot(v[:, cols], stacked(do, g, per_group), NT)


def stacked(array, g, per_group):
    first = g * per_group * HEAD_SIZE
    heads = [array[:, first + h * HEAD_SIZE : first + (h + 1) * HEAD_SIZE] for h in range(per_group)]
    return jnp.concatenate(heads, axis=0)


def attention_softmax(g, scores, grad_probs, probs_b, ds):
    length = scores.shape[1]
    group = scores.shape[2]
    scale = 1.0 / math.sqrt(HEAD_SIZE)
    targets = lax.broadcasted_iota(jnp.int32, (length, length), 0)
    positions = lax.broadcasted_iota(jnp.int32, (length, length), 1)
    allowed = targets <= positions
    for at in range(0, group, length):
        cols = slice(at, at + length)
        masked = jnp.where(allowed, scores[g, :, cols], -1e30)
        raw = jnp.exp((masked - jnp.max(masked, axis=0, keepdims=True)) * scale)
        probs = raw * (1.0 / jnp.sum(raw, axis=0, keepdims=True))
        slopes = grad_probs[g, :, cols]
        delta = jnp.sum(probs * slopes, axis=0, keepdims=True)
        probs_b[:, g * group + at : g * group + at + length] = probs.astype(BF16)
        ds[:, g * group + at : g * group + at + length] = (probs * (slopes - delta)).astype(BF16)


def attention_kernel(
    q_hbm, k_hbm, v_hbm, do_hbm, p_hbm,
    gk_ref, ds_hbm, sent_hbm, kept_hbm,
    q, k, v, do, p, probs_b, ds, scores, grad_probs, partial, sems, p_sems, out_sems,
):
    kv_heads = k.shape[1] // HEAD_SIZE
    group = q.shape[1] // kv_heads
    per_group = group // HEAD_SIZE
    groups, features = p.shape[0], p.shape[2]
    chips = groups // 2
    member = lax.axis_index("mp")
    chip, core = lax.div(member, 2), lax.rem(member, 2)
    small = [
        pltpu.make_async_copy(k_hbm, k, sems.at[0]),
        pltpu.make_async_copy(v_hbm, v, sems.at[1]),
    ]
    large, stored = [], []
    for g in range(kv_heads):
        cols = pl.ds(g * group, group)
        large.append((
            pltpu.make_async_copy(q_hbm.at[:, cols], q.at[:, cols], sems.at[2 + 2 * g]),
            pltpu.make_async_copy(do_hbm.at[:, cols], do.at[:, cols], sems.at[3 + 2 * g]),
        ))
        stored.append(pltpu.make_async_copy(ds.at[:, cols], ds_hbm.at[:, cols], out_sems.at[g]))
    blocks = []
    for b in range(groups):
        column = core if b >= chips else 1 - core
        start = (2 * lax.rem(chip + b + 1, chips) + column) * features
        rows = pl.ds(pl.multiple_of(start, features), features)
        blocks.append(pltpu.make_async_copy(p_hbm.at[:, rows, :], p.at[b], p_sems.at[b]))
    for copy in small:
        copy.start()
    for pair in large:
        for copy in pair:
            copy.start()
    for copy in blocks:
        copy.start()
    for copy in small:
        copy.wait()
    for g in range(kv_heads):
        for copy in large[g]:
            copy.wait()
        attention_scores(g, q, k, v, do, scores, grad_probs)
    scale = 1.0 / math.sqrt(HEAD_SIZE)
    values, keys = [], []
    for g in range(kv_heads):
        attention_softmax(g, scores, grad_probs, probs_b, ds)
        stored[g].start()
        cols = slice(g * group, (g + 1) * group)
        values.append(dot(probs_b[:, cols], stacked(do, g, per_group)).astype(BF16))
        keys.append((dot(ds[:, cols], stacked(q, g, per_group)) * scale).astype(BF16))
    gk = jnp.concatenate(keys, axis=1)
    gk_ref[...] = gk
    grads = jnp.concatenate([gk] + values, axis=1)
    step = min(CHUNK, features)
    for b in range(groups):
        blocks[b].wait()
        for at in range(0, features, step):
            rows = slice(at, at + step)
            both = jnp.concatenate([p[b, 0, rows, :], p[b, 1, rows, :]], axis=1)
            partial[b, :, rows] = dot(grads, both, NT).astype(BF16)
        target = sent_hbm.at[b] if b < chips else kept_hbm.at[b - chips]
        stored.append(pltpu.make_async_copy(partial.at[b], target, out_sems.at[kv_heads + b]))
        stored[-1].start()
    for copy in stored:
        copy.wait()


def query_kernel(ds_hbm, k_hbm, gq_hbm, ds, k, gq, sems, out_sems):
    kv_heads = k.shape[1] // HEAD_SIZE
    group = gq.shape[1] // kv_heads
    scale = 1.0 / math.sqrt(HEAD_SIZE)
    key_copy = pltpu.make_async_copy(k_hbm, k, sems.at[kv_heads])
    key_copy.start()
    loads, stores = [], []
    for g in range(kv_heads):
        cols = pl.ds(g * group, group)
        loads.append(pltpu.make_async_copy(ds_hbm.at[:, cols], ds.at[:, cols], sems.at[g]))
        stores.append(pltpu.make_async_copy(gq.at[:, cols], gq_hbm.at[:, cols], out_sems.at[g]))
        loads[-1].start()
    key_copy.wait()
    for g in range(kv_heads):
        loads[g].wait()
        key = k[:, g * HEAD_SIZE : (g + 1) * HEAD_SIZE]
        for at in range(g * group, (g + 1) * group, HEAD_SIZE):
            grad = dot(ds[:, at : at + HEAD_SIZE], key, TN) * scale
            gq[:, at : at + HEAD_SIZE] = grad.astype(BF16)
        stores[g].start()
    for copy in stores:
        copy.wait()


def turned_kernel(mine_ref, theirs_ref, next_ref, x_hbm, out_ref, own, sem):
    rows, width = next_ref.shape
    parts = out_ref.shape[1] // rows
    far = groups = parts // 2
    part, member = lax.axis_index("dp"), lax.axis_index("mp")
    cols = pl.ds(pl.multiple_of(part * width, width), width)
    copy = pltpu.make_async_copy(x_hbm.at[:, cols], own, sem)
    copy.start()

    def put(k, piece):
        place = far * lax.rem(k, 2) + 2 * lax.div(lax.rem(k, far), 2) + lax.div(k, far)
        out_ref[:, pl.ds(pl.multiple_of(place * rows, rows), rows)] = piece.T

    partners = [far + (member ^ j) for j in range(0, groups, 2)]
    partners += [k + lax.rem(member, 2) for k in range(2, far, 2)]
    for at, k in enumerate(partners):
        put(k, mine_ref[at * rows : (at + 1) * rows, :])
        put(k ^ 1, theirs_ref[at * rows : (at + 1) * rows, :])
    put(jnp.int32(1), next_ref[...])
    copy.wait()
    put(jnp.int32(0), own[...])


def weights_kernel(x_ref, *refs):
    keys, out_ref = refs[:-1], refs[-1]
    rows = keys[0].shape[0]
    total = dot(x_ref[:, :rows], keys[0][...])
    for j in range(1, len(keys)):
        total += dot(x_ref[:, j * rows : (j + 1) * rows], keys[j][...])
    out_ref[...] = total * (1.0 / (2 * len(keys)))


def along_dp(array, partner, parts, groups):
    pairs = [
        (i * groups + m, (i ^ partner(m)) * groups + m)
        for i in range(parts)
        for m in range(groups)
    ]
    return lax.ppermute(array, ("dp", "mp"), pairs)


def along_mp(array, bit, groups):
    return lax.ppermute(array, "mp", [(m, m ^ bit) for m in range(groups)])


def sent_inputs(inputs, parts, groups):
    far = parts // 2
    part, member = lax.axis_index("dp"), lax.axis_index("mp")
    rows, width = inputs.shape[0], inputs.shape[1] // parts

    def block(k):
        return lax.dynamic_slice(inputs, (0, (part ^ k) * width), (rows, width))

    distant = along_dp(block(far + member), lambda m: far + m, parts, groups)
    near = []
    for k in range(2, far, 2):
        sent = block(k + lax.rem(member, 2))
        near.append(along_dp(sent, lambda m, k=k: k + m % 2, parts, groups))
    return distant, near, block(1)


def shared_inputs(piece, groups):
    pieces = [piece]
    bit = 2
    while bit < groups:
        pieces += [along_mp(piece, bit, groups) for piece in pieces]
        bit *= 2
    return pieces


def turned_inputs(mine, theirs, next_inputs, inputs):
    rows, width = next_inputs.shape
    return pl.pallas_call(
        turned_kernel,
        in_specs=[IN_VMEM, IN_VMEM, IN_VMEM, IN_HBM],
        out_specs=IN_VMEM,
        out_shape=jax.ShapeDtypeStruct((width, inputs.shape[1] // width * rows), inputs.dtype),
        scratch_shapes=[pltpu.VMEM((rows, width), inputs.dtype), pltpu.SemaphoreType.DMA],
        compiler_params=PARAMS,
        cost_estimate=cost(0, 4 * inputs.size),
    )(mine, theirs, next_inputs, inputs)


def summed_weights(turned, keys):
    width, columns = turned.shape[0], keys[0].shape[1]
    return pl.pallas_call(
        weights_kernel,
        out_specs=IN_VMEM,
        out_shape=jax.ShapeDtypeStruct((width, columns), F32),
        compiler_params=PARAMS,
        cost_estimate=cost(
            2 * turned.size * columns, 2 * turned.size + 4 * width * columns
        ),
    )(turned, *keys)


def gathered_weights(inputs, grad_key, parts):
    rows = inputs.shape[0]
    width = inputs.shape[1] // parts
    blocks = inputs.reshape(rows, parts, width).transpose(1, 0, 2)
    mine = lax.all_to_all(blocks, "dp", split_axis=0, concat_axis=0, tiled=True)
    keys = lax.all_gather(grad_key, "dp", axis=0)
    return jnp.einsum("psd,psc->dc", mine, keys, preferred_element_type=F32) / parts


def body(query_states, key_states, value_states, grad_context, inputs_normed, projections):
    parts = lax.axis_size("dp")
    groups = lax.axis_size("mp")
    chips = groups // 2
    rows, width = key_states.shape
    query_width = query_states.shape[1]
    features = projections.shape[1] // groups
    kv_heads = width // HEAD_SIZE
    partial = jax.ShapeDtypeStruct((chips, rows, features), BF16)
    exchange = parts == 2 * groups and inputs_normed.shape[1] % (parts * 128) == 0
    if exchange:
        distant, near, next_block = sent_inputs(inputs_normed, parts, groups)

    whole = pltpu.VMEM((rows, query_width), BF16)
    narrow = pltpu.VMEM((rows, width), BF16)
    wide = pltpu.VMEM((kv_heads, rows, query_width // kv_heads), F32)
    grad_key, grad_scores, sent, kept = pl.pallas_call(
        attention_kernel,
        in_specs=[IN_HBM] * 5,
        out_specs=[IN_VMEM, ANYWHERE, ANYWHERE, ANYWHERE],
        out_shape=(
            jax.ShapeDtypeStruct((rows, width), BF16),
            jax.ShapeDtypeStruct((rows, query_width), BF16),
            partial,
            partial,
        ),
        scratch_shapes=[whole, narrow, narrow, whole]
        + [pltpu.VMEM((groups, 2, features, width), BF16), whole, whole, wide, wide]
        + [pltpu.VMEM((groups, rows, features), BF16)]
        + [pltpu.SemaphoreType.DMA((2 + 2 * kv_heads,)), pltpu.SemaphoreType.DMA((groups,))]
        + [pltpu.SemaphoreType.DMA((kv_heads + groups,))],
        compiler_params=WHOLE,
        cost_estimate=cost(
            8 * rows * rows * query_width + 4 * rows * width * features * groups,
            6 * rows * query_width + 4 * width * features * groups,
            rows * query_width,
        ),
    )(query_states, key_states, value_states, grad_context, projections)

    grad_query = pl.pallas_call(
        query_kernel,
        in_specs=[IN_HBM, IN_HBM],
        out_specs=ANYWHERE,
        out_shape=jax.ShapeDtypeStruct((rows, query_width), BF16),
        scratch_shapes=[whole, narrow, whole]
        + [pltpu.SemaphoreType.DMA((1 + kv_heads,)), pltpu.SemaphoreType.DMA((kv_heads,))],
        compiler_params=WHOLE,
        cost_estimate=cost(2 * rows * rows * query_width, 4 * rows * query_width),
    )(grad_scores, key_states)

    if exchange:
        distant, near = lax.optimization_barrier((distant, near))
        ready, sent, distant, near = lax.optimization_barrier(
            (grad_key, sent, distant, near)
        )
        first = along_dp(ready, lambda m: parts // 2, parts, groups)
        pieces = shared_inputs(distant, groups)
        next_inputs = along_dp(next_block, lambda m: 1, parts, groups)
    came = along_mp(sent, 1, groups)
    if exchange:
        came, ready = lax.optimization_barrier((came, grad_key))
        twice = jnp.concatenate([ready, ready])
    total = kept.astype(F32) + came.astype(F32)
    pairs = [total[b].astype(BF16) for b in range(chips - 1)]
    if exchange:
        first, twice, pieces, pairs, next_inputs = lax.optimization_barrier(
            (first, twice, pieces, pairs, next_inputs)
        )
        keys = {0: lax.dynamic_update_slice(twice, first, (rows, 0))}
        mine = jnp.concatenate(pieces + near)
        theirs = along_mp(mine, 1, groups)
        bit = parts // 4
        while bit > 1:
            for k in list(keys):
                keys[k ^ bit] = along_dp(keys[k], lambda m, bit=bit: bit, parts, groups)
            bit //= 2
    grad_input = total[chips - 1]
    for b in range(chips - 1):
        shift = [(m, (m + 2 * (b + 1)) % groups) for m in range(groups)]
        grad_input += lax.ppermute(pairs[b], "mp", shift).astype(F32)
    grad_input = grad_input.astype(BF16)

    if exchange:
        beside = []
        for k in range(0, parts // 2, 2):
            if k:
                keys[k], beside, grad_query = lax.optimization_barrier(
                    (keys[k], beside, grad_query)
                )
            beside.append(along_dp(keys[k], lambda m: 1, parts, groups))
        turned = turned_inputs(mine, theirs, next_inputs, inputs_normed)
        beside[-1], grad_input = lax.optimization_barrier((beside[-1], grad_input))
        keys = [keys[k] for k in range(0, parts // 2, 2)] + beside
        grad_weights = summed_weights(turned, keys)
    else:
        grad_weights = gathered_weights(inputs_normed, grad_key, parts)
    return (grad_query, grad_input, grad_weights)


def solution(mesh):
    placed = (
        P("dp", "mp"),
        P("dp", "mp"),
        P("dp", "mp"),
        P("dp", "mp"),
        P("dp", None),
        P(None, None, "mp"),
    )
    return jax.shard_map(
        body,
        mesh=mesh,
        in_specs=placed,
        out_specs=(P("dp", "mp"), P("dp", "mp"), P("dp", "mp")),
        check_vma=False,
    )
```

```python
import math

import jax
import jax.numpy as jnp
from jax import lax
from jax.experimental import pallas as pl
from jax.experimental.pallas import tpu as pltpu
from jax.sharding import PartitionSpec as P

HEAD_SIZE = 128
F32 = jnp.float32
BF16 = jnp.bfloat16
NN = (((1,), (0,)), ((), ()))
NT = (((1,), (1,)), ((), ()))
TN = (((0,), (0,)), ((), ()))
IN_HBM = pl.BlockSpec(memory_space=pltpu.HBM)
ANYWHERE = pl.BlockSpec(memory_space=pl.ANY)
IN_VMEM = pl.BlockSpec(memory_space=pltpu.VMEM)
CHUNK = 512
PARAMS = pltpu.CompilerParams(vmem_limit_bytes=24 * 1024 * 1024)
WHOLE = pltpu.CompilerParams(vmem_limit_bytes=60 * 1024 * 1024)


def dot(a, b, dims=NN):
    return lax.dot_general(a, b, dims, preferred_element_type=F32)


def cost(flops, moved, transcendentals=0):
    return pl.CostEstimate(flops=flops, bytes_accessed=moved, transcendentals=transcendentals)


def attention_scores(g, q, k, v, do, scores, grad_probs):
    per_group = q.shape[1] // k.shape[1]
    cols = slice(g * HEAD_SIZE, (g + 1) * HEAD_SIZE)
    scores[g] = dot(k[:, cols], stacked(q, g, per_group), NT)
    grad_probs[g] = dot(v[:, cols], stacked(do, g, per_group), NT)


def stacked(array, g, per_group):
    first = g * per_group * HEAD_SIZE
    heads = [array[:, first + h * HEAD_SIZE : first + (h + 1) * HEAD_SIZE] for h in range(per_group)]
    return jnp.concatenate(heads, axis=0)


def attention_softmax(g, scores, grad_probs, probs_b, ds):
    length = scores.shape[1]
    group = scores.shape[2]
    scale = 1.0 / math.sqrt(HEAD_SIZE)
    targets = lax.broadcasted_iota(jnp.int32, (length, length), 0)
    positions = lax.broadcasted_iota(jnp.int32, (length, length), 1)
    allowed = targets <= positions
    for at in range(0, group, length):
        cols = slice(at, at + length)
        masked = jnp.where(allowed, scores[g, :, cols], -1e30)
        raw = jnp.exp((masked - jnp.max(masked, axis=0, keepdims=True)) * scale)
        probs = raw * (1.0 / jnp.sum(raw, axis=0, keepdims=True))
        slopes = grad_probs[g, :, cols]
        delta = jnp.sum(probs * slopes, axis=0, keepdims=True)
        probs_b[:, g * group + at : g * group + at + length] = probs.astype(BF16)
        ds[:, g * group + at : g * group + at + length] = (probs * (slopes - delta)).astype(BF16)


def attention_kernel(
    q_hbm, k_hbm, v_hbm, do_hbm, p_hbm,
    gk_ref, ds_hbm, sent_hbm, kept_hbm,
    q, k, v, do, p, probs_b, ds, scores, grad_probs, partial, sems, p_sems, out_sems,
):
    kv_heads = k.shape[1] // HEAD_SIZE
    group = q.shape[1] // kv_heads
    per_group = group // HEAD_SIZE
    groups, features = p.shape[0], p.shape[2]
    chips = groups // 2
    member = lax.axis_index("mp")
    chip, core = lax.div(member, 2), lax.rem(member, 2)
    small = [
        pltpu.make_async_copy(k_hbm, k, sems.at[0]),
        pltpu.make_async_copy(v_hbm, v, sems.at[1]),
    ]
    large, stored = [], []
    for g in range(kv_heads):
        cols = pl.ds(g * group, group)
        large.append((
            pltpu.make_async_copy(q_hbm.at[:, cols], q.at[:, cols], sems.at[2 + 2 * g]),
            pltpu.make_async_copy(do_hbm.at[:, cols], do.at[:, cols], sems.at[3 + 2 * g]),
        ))
        stored.append(pltpu.make_async_copy(ds.at[:, cols], ds_hbm.at[:, cols], out_sems.at[g]))
    blocks = []
    for b in range(groups):
        column = core if b >= chips else 1 - core
        start = (2 * lax.rem(chip + b + 1, chips) + column) * features
        rows = pl.ds(pl.multiple_of(start, features), features)
        blocks.append(pltpu.make_async_copy(p_hbm.at[:, rows, :], p.at[b], p_sems.at[b]))
    for copy in small:
        copy.start()
    for pair in large:
        for copy in pair:
            copy.start()
    for copy in blocks:
        copy.start()
    for copy in small:
        copy.wait()
    for g in range(kv_heads):
        for copy in large[g]:
            copy.wait()
        attention_scores(g, q, k, v, do, scores, grad_probs)
    scale = 1.0 / math.sqrt(HEAD_SIZE)
    values, keys = [], []
    for g in range(kv_heads):
        attention_softmax(g, scores, grad_probs, probs_b, ds)
        stored[g].start()
        cols = slice(g * group, (g + 1) * group)
        values.append(dot(probs_b[:, cols], stacked(do, g, per_group)).astype(BF16))
        keys.append((dot(ds[:, cols], stacked(q, g, per_group)) * scale).astype(BF16))
    gk = jnp.concatenate(keys, axis=1)
    gk_ref[...] = gk
    grads = jnp.concatenate([gk] + values, axis=1)
    step = min(CHUNK, features)
    for b in range(groups):
        blocks[b].wait()
        for at in range(0, features, step):
            rows = slice(at, at + step)
            both = jnp.concatenate([p[b, 0, rows, :], p[b, 1, rows, :]], axis=1)
            partial[b, :, rows] = dot(grads, both, NT).astype(BF16)
        target = sent_hbm.at[b] if b < chips else kept_hbm.at[b - chips]
        stored.append(pltpu.make_async_copy(partial.at[b], target, out_sems.at[kv_heads + b]))
        stored[-1].start()
    for copy in stored:
        copy.wait()


def query_kernel(ds_hbm, k_hbm, gq_hbm, ds, k, gq, sems, out_sems):
    kv_heads = k.shape[1] // HEAD_SIZE
    group = gq.shape[1] // kv_heads
    scale = 1.0 / math.sqrt(HEAD_SIZE)
    key_copy = pltpu.make_async_copy(k_hbm, k, sems.at[kv_heads])
    key_copy.start()
    loads, stores = [], []
    for g in range(kv_heads):
        cols = pl.ds(g * group, group)
        loads.append(pltpu.make_async_copy(ds_hbm.at[:, cols], ds.at[:, cols], sems.at[g]))
        stores.append(pltpu.make_async_copy(gq.at[:, cols], gq_hbm.at[:, cols], out_sems.at[g]))
        loads[-1].start()
    key_copy.wait()
    for g in range(kv_heads):
        loads[g].wait()
        key = k[:, g * HEAD_SIZE : (g + 1) * HEAD_SIZE]
        for at in range(g * group, (g + 1) * group, HEAD_SIZE):
            grad = dot(ds[:, at : at + HEAD_SIZE], key, TN) * scale
            gq[:, at : at + HEAD_SIZE] = grad.astype(BF16)
        stores[g].start()
    for copy in stores:
        copy.wait()


def turned_kernel(mine_ref, theirs_ref, next_ref, x_hbm, out_ref, own, sem):
    rows, width = next_ref.shape
    parts = out_ref.shape[1] // rows
    far = groups = parts // 2
    part, member = lax.axis_index("dp"), lax.axis_index("mp")
    cols = pl.ds(pl.multiple_of(part * width, width), width)
    copy = pltpu.make_async_copy(x_hbm.at[:, cols], own, sem)
    copy.start()

    def put(k, piece):
        place = far * lax.rem(k, 2) + 2 * lax.div(lax.rem(k, far), 2) + lax.div(k, far)
        out_ref[:, pl.ds(pl.multiple_of(place * rows, rows), rows)] = piece.T

    partners = [far + (member ^ j) for j in range(0, groups, 2)]
    partners += [k + lax.rem(member, 2) for k in range(2, far, 2)]
    for at, k in enumerate(partners):
        put(k, mine_ref[at * rows : (at + 1) * rows, :])
        put(k ^ 1, theirs_ref[at * rows : (at + 1) * rows, :])
    put(jnp.int32(1), next_ref[...])
    copy.wait()
    put(jnp.int32(0), own[...])


def weights_kernel(x_ref, *refs):
    keys, out_ref = refs[:-1], refs[-1]
    rows = keys[0].shape[0]
    total = dot(x_ref[:, :rows], keys[0][...])
    for j in range(1, len(keys)):
        total += dot(x_ref[:, j * rows : (j + 1) * rows], keys[j][...])
    out_ref[...] = total * (1.0 / (2 * len(keys)))


def along_dp(array, partner, parts, groups):
    pairs = [
        (i * groups + m, (i ^ partner(m)) * groups + m)
        for i in range(parts)
        for m in range(groups)
    ]
    return lax.ppermute(array, ("dp", "mp"), pairs)


def along_mp(array, bit, groups):
    return lax.ppermute(array, "mp", [(m, m ^ bit) for m in range(groups)])


def sent_inputs(inputs, parts, groups):
    far = parts // 2
    part, member = lax.axis_index("dp"), lax.axis_index("mp")
    rows, width = inputs.shape[0], inputs.shape[1] // parts

    def block(k):
        return lax.dynamic_slice(inputs, (0, (part ^ k) * width), (rows, width))

    distant = along_dp(block(far + member), lambda m: far + m, parts, groups)
    near = []
    for k in range(2, far, 2):
        sent = block(k + lax.rem(member, 2))
        near.append(along_dp(sent, lambda m, k=k: k + m % 2, parts, groups))
    return distant, near, block(1)


def shared_inputs(piece, groups):
    pieces = [piece]
    bit = 2
    while bit < groups:
        pieces += [along_mp(piece, bit, groups) for piece in pieces]
        bit *= 2
    return pieces


def turned_inputs(mine, theirs, next_inputs, inputs):
    rows, width = next_inputs.shape
    return pl.pallas_call(
        turned_kernel,
        in_specs=[IN_VMEM, IN_VMEM, IN_VMEM, IN_HBM],
        out_specs=IN_VMEM,
        out_shape=jax.ShapeDtypeStruct((width, inputs.shape[1] // width * rows), inputs.dtype),
        scratch_shapes=[pltpu.VMEM((rows, width), inputs.dtype), pltpu.SemaphoreType.DMA],
        compiler_params=PARAMS,
        cost_estimate=cost(0, 4 * inputs.size),
    )(mine, theirs, next_inputs, inputs)


def summed_weights(turned, keys):
    width, columns = turned.shape[0], keys[0].shape[1]
    return pl.pallas_call(
        weights_kernel,
        out_specs=IN_VMEM,
        out_shape=jax.ShapeDtypeStruct((width, columns), F32),
        compiler_params=PARAMS,
        cost_estimate=cost(
            2 * turned.size * columns, 2 * turned.size + 4 * width * columns
        ),
    )(turned, *keys)


def query_gradient(grad_scores, key_states):
    rows, query_width = grad_scores.shape
    width = key_states.shape[1]
    kv_heads = width // HEAD_SIZE
    whole = pltpu.VMEM((rows, query_width), BF16)
    narrow = pltpu.VMEM((rows, width), BF16)
    return pl.pallas_call(
        query_kernel,
        in_specs=[IN_HBM, IN_HBM],
        out_specs=ANYWHERE,
        out_shape=jax.ShapeDtypeStruct((rows, query_width), BF16),
        scratch_shapes=[whole, narrow, whole]
        + [pltpu.SemaphoreType.DMA((1 + kv_heads,)), pltpu.SemaphoreType.DMA((kv_heads,))],
        compiler_params=WHOLE,
        cost_estimate=cost(2 * rows * rows * query_width, 4 * rows * query_width),
    )(grad_scores, key_states)


def gathered_weights(inputs, grad_key, parts):
    rows = inputs.shape[0]
    width = inputs.shape[1] // parts
    blocks = inputs.reshape(rows, parts, width).transpose(1, 0, 2)
    mine = lax.all_to_all(blocks, "dp", split_axis=0, concat_axis=0, tiled=True)
    keys = lax.all_gather(grad_key, "dp", axis=0)
    return jnp.einsum("psd,psc->dc", mine, keys, preferred_element_type=F32) / parts


def body(query_states, key_states, value_states, grad_context, inputs_normed, projections):
    parts = lax.axis_size("dp")
    groups = lax.axis_size("mp")
    chips = groups // 2
    rows, width = key_states.shape
    query_width = query_states.shape[1]
    features = projections.shape[1] // groups
    kv_heads = width // HEAD_SIZE
    partial = jax.ShapeDtypeStruct((chips, rows, features), BF16)
    exchange = parts == 2 * groups and inputs_normed.shape[1] % (parts * width) == 0
    if exchange:
        distant, near, next_block = sent_inputs(inputs_normed, parts, groups)

    whole = pltpu.VMEM((rows, query_width), BF16)
    narrow = pltpu.VMEM((rows, width), BF16)
    wide = pltpu.VMEM((kv_heads, rows, query_width // kv_heads), F32)
    grad_key, grad_scores, sent, kept = pl.pallas_call(
        attention_kernel,
        in_specs=[IN_HBM] * 5,
        out_specs=[IN_VMEM, ANYWHERE, ANYWHERE, ANYWHERE],
        out_shape=(
            jax.ShapeDtypeStruct((rows, width), BF16),
            jax.ShapeDtypeStruct((rows, query_width), BF16),
            partial,
            partial,
        ),
        scratch_shapes=[whole, narrow, narrow, whole]
        + [pltpu.VMEM((groups, 2, features, width), BF16), whole, whole, wide, wide]
        + [pltpu.VMEM((groups, rows, features), BF16)]
        + [pltpu.SemaphoreType.DMA((2 + 2 * kv_heads,)), pltpu.SemaphoreType.DMA((groups,))]
        + [pltpu.SemaphoreType.DMA((kv_heads + groups,))],
        compiler_params=WHOLE,
        cost_estimate=cost(
            8 * rows * rows * query_width + 4 * rows * width * features * groups,
            6 * rows * query_width + 4 * width * features * groups,
            rows * query_width,
        ),
    )(query_states, key_states, value_states, grad_context, projections)

    if exchange:
        ready, next_block = lax.optimization_barrier((grad_key, next_block))
        first = along_dp(ready, lambda m: parts // 2, parts, groups)
        next_inputs = along_dp(next_block, lambda m: 1, parts, groups)
    grad_query = query_gradient(grad_scores, key_states)
    if exchange:
        twice = jnp.concatenate([grad_key, grad_key])
        first, twice, grad_query, sent, kept, distant, near, next_inputs = (
            lax.optimization_barrier(
                (first, twice, grad_query, sent, kept, distant, near, next_inputs)
            )
        )
        pieces = shared_inputs(distant, groups)
        keys = {0: lax.dynamic_update_slice(twice, first, (rows, 0))}
        bit = parts // 4
        while bit > 1:
            for k in list(keys):
                keys[k ^ bit] = along_dp(keys[k], lambda m, bit=bit: bit, parts, groups)
            bit //= 2
        beside = [along_dp(keys[0], lambda m: 1, parts, groups)]
    came = along_mp(sent, 1, groups)
    total = kept.astype(F32) + came.astype(F32)
    if exchange:
        keys, pieces, total, beside = lax.optimization_barrier((keys, pieces, total, beside))
        beside += [
            along_dp(keys[k], lambda m: 1, parts, groups) for k in range(2, parts // 2, 2)
        ]
        mine = jnp.concatenate(pieces + near)
        theirs = along_mp(mine, 1, groups)
    grad_input = total[chips - 1]
    for b in range(chips - 1):
        shift = [(m, (m + 2 * (b + 1)) % groups) for m in range(groups)]
        grad_input += lax.ppermute(total[b].astype(BF16), "mp", shift).astype(F32)
    grad_input = grad_input.astype(BF16)

    if exchange:
        turned = turned_inputs(mine, theirs, next_inputs, inputs_normed)
        keys = [keys[k] for k in range(0, parts // 2, 2)] + beside
        grad_weights = summed_weights(turned, keys)
    else:
        grad_weights = gathered_weights(inputs_normed, grad_key, parts)
    return (grad_query, grad_input, grad_weights)


def solution(mesh):
    placed = (
        P("dp", "mp"),
        P("dp", "mp"),
        P("dp", "mp"),
        P("dp", "mp"),
        P("dp", None),
        P(None, None, "mp"),
    )
    return jax.shard_map(
        body,
        mesh=mesh,
        in_specs=placed,
        out_specs=(P("dp", "mp"), P("dp", "mp"), P("dp", "mp")),
        check_vma=False,
    )
```

```python
import math

import jax
import jax.numpy as jnp
from jax import lax
from jax.experimental import pallas as pl
from jax.experimental.pallas import tpu as pltpu
from jax.sharding import PartitionSpec as P

HEAD_SIZE = 128
F32 = jnp.float32
BF16 = jnp.bfloat16
NN = (((1,), (0,)), ((), ()))
NT = (((1,), (1,)), ((), ()))
TN = (((0,), (0,)), ((), ()))
IN_HBM = pl.BlockSpec(memory_space=pltpu.HBM)
ANYWHERE = pl.BlockSpec(memory_space=pl.ANY)
IN_VMEM = pl.BlockSpec(memory_space=pltpu.VMEM)
CHUNK = 512
PARAMS = pltpu.CompilerParams(vmem_limit_bytes=24 * 1024 * 1024)
WHOLE = pltpu.CompilerParams(vmem_limit_bytes=60 * 1024 * 1024)


def dot(a, b, dims=NN):
    return lax.dot_general(a, b, dims, preferred_element_type=F32)


def cost(flops, moved, transcendentals=0):
    return pl.CostEstimate(flops=flops, bytes_accessed=moved, transcendentals=transcendentals)


def attention_scores(g, q, k, v, do, scores, grad_probs):
    per_group = q.shape[1] // k.shape[1]
    cols = slice(g * HEAD_SIZE, (g + 1) * HEAD_SIZE)
    scores[g] = dot(k[:, cols], stacked(q, g, per_group), NT)
    grad_probs[g] = dot(v[:, cols], stacked(do, g, per_group), NT)


def stacked(array, g, per_group):
    first = g * per_group * HEAD_SIZE
    heads = [array[:, first + h * HEAD_SIZE : first + (h + 1) * HEAD_SIZE] for h in range(per_group)]
    return jnp.concatenate(heads, axis=0)


def attention_softmax(g, scores, grad_probs, probs_b, ds):
    length = scores.shape[1]
    group = scores.shape[2]
    scale = 1.0 / math.sqrt(HEAD_SIZE)
    targets = lax.broadcasted_iota(jnp.int32, (length, length), 0)
    positions = lax.broadcasted_iota(jnp.int32, (length, length), 1)
    allowed = targets <= positions
    for at in range(0, group, length):
        cols = slice(at, at + length)
        masked = jnp.where(allowed, scores[g, :, cols], -1e30)
        raw = jnp.exp((masked - jnp.max(masked, axis=0, keepdims=True)) * scale)
        probs = raw * (1.0 / jnp.sum(raw, axis=0, keepdims=True))
        slopes = grad_probs[g, :, cols]
        delta = jnp.sum(probs * slopes, axis=0, keepdims=True)
        probs_b[:, g * group + at : g * group + at + length] = probs.astype(BF16)
        ds[:, g * group + at : g * group + at + length] = (probs * (slopes - delta)).astype(BF16)


def attention_kernel(
    q_hbm, k_hbm, v_hbm, do_hbm, p_hbm,
    gk_ref, gq_hbm, sent_hbm, kept_hbm,
    q, k, v, do, p, probs_b, ds, gq, scores, grad_probs, partial, sems, p_sems, out_sems,
):
    kv_heads = k.shape[1] // HEAD_SIZE
    group = q.shape[1] // kv_heads
    per_group = group // HEAD_SIZE
    groups, features = p.shape[0], p.shape[2]
    chips = groups // 2
    member = lax.axis_index("mp")
    chip, core = lax.div(member, 2), lax.rem(member, 2)
    small = [
        pltpu.make_async_copy(k_hbm, k, sems.at[0]),
        pltpu.make_async_copy(v_hbm, v, sems.at[1]),
    ]
    large, stored = [], []
    for g in range(kv_heads):
        cols = pl.ds(g * group, group)
        large.append((
            pltpu.make_async_copy(q_hbm.at[:, cols], q.at[:, cols], sems.at[2 + 2 * g]),
            pltpu.make_async_copy(do_hbm.at[:, cols], do.at[:, cols], sems.at[3 + 2 * g]),
        ))
        stored.append(pltpu.make_async_copy(gq.at[:, cols], gq_hbm.at[:, cols], out_sems.at[g]))
    blocks = []
    for b in range(groups):
        column = core if b >= chips else 1 - core
        start = (2 * lax.rem(chip + b + 1, chips) + column) * features
        rows = pl.ds(pl.multiple_of(start, features), features)
        blocks.append(pltpu.make_async_copy(p_hbm.at[:, rows, :], p.at[b], p_sems.at[b]))
    for copy in small:
        copy.start()
    for pair in large:
        for copy in pair:
            copy.start()
    for copy in blocks:
        copy.start()
    for copy in small:
        copy.wait()
    for g in range(kv_heads):
        for copy in large[g]:
            copy.wait()
        attention_scores(g, q, k, v, do, scores, grad_probs)
    scale = 1.0 / math.sqrt(HEAD_SIZE)
    values, keys = [], []
    for g in range(kv_heads):
        attention_softmax(g, scores, grad_probs, probs_b, ds)
        cols = slice(g * group, (g + 1) * group)
        values.append(dot(probs_b[:, cols], stacked(do, g, per_group)).astype(BF16))
        keys.append((dot(ds[:, cols], stacked(q, g, per_group)) * scale).astype(BF16))
        grad_query = dot(ds[:, cols], k[:, g * HEAD_SIZE : (g + 1) * HEAD_SIZE], TN) * scale
        length = q.shape[0]
        for h in range(per_group):
            at = g * group + h * HEAD_SIZE
            gq[:, at : at + HEAD_SIZE] = grad_query[h * length : (h + 1) * length].astype(BF16)
        stored[g].start()
    gk = jnp.concatenate(keys, axis=1)
    gk_ref[...] = gk
    grads = jnp.concatenate([gk] + values, axis=1)
    step = min(CHUNK, features)
    for b in range(groups):
        blocks[b].wait()
        for at in range(0, features, step):
            rows = slice(at, at + step)
            both = jnp.concatenate([p[b, 0, rows, :], p[b, 1, rows, :]], axis=1)
            partial[b, :, rows] = dot(grads, both, NT).astype(BF16)
        target = sent_hbm.at[b] if b < chips else kept_hbm.at[b - chips]
        stored.append(pltpu.make_async_copy(partial.at[b], target, out_sems.at[kv_heads + b]))
        stored[-1].start()
    for copy in stored:
        copy.wait()


def turned_kernel(*refs):
    *blocks, next_ref, x_hbm, out_ref, own, sem = refs
    rows, width = own.shape
    parts = out_ref.shape[1] // rows
    far = groups = parts // 2
    part, member = lax.axis_index("dp"), lax.axis_index("mp")
    cols = pl.ds(pl.multiple_of(part * width, width), width)
    copy = pltpu.make_async_copy(x_hbm.at[:, cols], own, sem)
    copy.start()

    def put(k, piece):
        place = far * lax.rem(k, 2) + 2 * lax.div(lax.rem(k, far), 2) + lax.div(k, far)
        out_ref[:, pl.ds(pl.multiple_of(place * rows, rows), rows)] = piece.T

    partners = [far + (member ^ j) for j in range(0, groups, 2)]
    partners += [k + lax.rem(member, 2) for k in range(2, far, 2)]
    for k, mine, theirs in zip(partners, blocks[: len(partners)], blocks[len(partners) :]):
        put(k, mine[...])
        put(k ^ 1, theirs[...])
    put(jnp.int32(1), next_ref[...])
    copy.wait()
    put(jnp.int32(0), own[...])


def weights_kernel(x_ref, *refs):
    keys, out_ref = refs[:-1], refs[-1]
    rows = keys[0].shape[0]
    total = dot(x_ref[:, :rows], keys[0][...])
    for j in range(1, len(keys)):
        total += dot(x_ref[:, j * rows : (j + 1) * rows], keys[j][...])
    out_ref[...] = total * (1.0 / (2 * len(keys)))


def along_dp(array, partner, parts, groups):
    pairs = [
        (i * groups + m, (i ^ partner(m)) * groups + m)
        for i in range(parts)
        for m in range(groups)
    ]
    return lax.ppermute(array, ("dp", "mp"), pairs)


def along_mp(array, bit, groups):
    return lax.ppermute(array, "mp", [(m, m ^ bit) for m in range(groups)])


def sent_inputs(inputs, parts, groups):
    far = parts // 2
    part, member = lax.axis_index("dp"), lax.axis_index("mp")
    rows, width = inputs.shape[0], inputs.shape[1] // parts

    def block(k):
        return lax.dynamic_slice(inputs, (0, (part ^ k) * width), (rows, width))

    distant = along_dp(block(far + member), lambda m: far + m, parts, groups)
    near = []
    for k in range(2, far, 2):
        sent = block(k + lax.rem(member, 2))
        near.append(along_dp(sent, lambda m, k=k: k + m % 2, parts, groups))
    return distant, near, along_dp(block(1), lambda m: 1, parts, groups)


def shared_inputs(piece, groups):
    pieces = [piece]
    bit = 2
    while bit < groups:
        pieces += [along_mp(piece, bit, groups) for piece in pieces]
        bit *= 2
    return pieces


def turned_inputs(mine, theirs, next_inputs, inputs):
    rows, width = next_inputs.shape
    blocks = [*mine, *theirs, next_inputs]
    return pl.pallas_call(
        turned_kernel,
        in_specs=[IN_VMEM] * len(blocks) + [IN_HBM],
        out_specs=IN_VMEM,
        out_shape=jax.ShapeDtypeStruct((width, inputs.shape[1] // width * rows), inputs.dtype),
        scratch_shapes=[pltpu.VMEM((rows, width), inputs.dtype), pltpu.SemaphoreType.DMA],
        compiler_params=PARAMS,
        cost_estimate=cost(0, 4 * inputs.size),
    )(*blocks, inputs)


def summed_weights(turned, keys):
    width, columns = turned.shape[0], keys[0].shape[1]
    return pl.pallas_call(
        weights_kernel,
        out_specs=IN_VMEM,
        out_shape=jax.ShapeDtypeStruct((width, columns), F32),
        compiler_params=PARAMS,
        cost_estimate=cost(
            2 * turned.size * columns, 2 * turned.size + 4 * width * columns
        ),
    )(turned, *keys)


def gathered_weights(inputs, grad_key, parts):
    rows = inputs.shape[0]
    width = inputs.shape[1] // parts
    blocks = inputs.reshape(rows, parts, width).transpose(1, 0, 2)
    mine = lax.all_to_all(blocks, "dp", split_axis=0, concat_axis=0, tiled=True)
    keys = lax.all_gather(grad_key, "dp", axis=0)
    return jnp.einsum("psd,psc->dc", mine, keys, preferred_element_type=F32) / parts


def body(query_states, key_states, value_states, grad_context, inputs_normed, projections):
    parts = lax.axis_size("dp")
    groups = lax.axis_size("mp")
    chips = groups // 2
    rows, width = key_states.shape
    query_width = query_states.shape[1]
    features = projections.shape[1] // groups
    kv_heads = width // HEAD_SIZE
    partial = jax.ShapeDtypeStruct((chips, rows, features), BF16)
    exchange = parts == 2 * groups and inputs_normed.shape[1] % (parts * 128) == 0
    if exchange:
        distant, near, next_inputs = sent_inputs(inputs_normed, parts, groups)

    whole = pltpu.VMEM((rows, query_width), BF16)
    narrow = pltpu.VMEM((rows, width), BF16)
    wide = pltpu.VMEM((kv_heads, rows, query_width // kv_heads), F32)
    grad_key, grad_query, sent, kept = pl.pallas_call(
        attention_kernel,
        in_specs=[IN_HBM] * 5,
        out_specs=[IN_VMEM, ANYWHERE, ANYWHERE, ANYWHERE],
        out_shape=(
            jax.ShapeDtypeStruct((rows, width), BF16),
            jax.ShapeDtypeStruct((rows, query_width), BF16),
            partial,
            partial,
        ),
        scratch_shapes=[whole, narrow, narrow, whole]
        + [pltpu.VMEM((groups, 2, features, width), BF16), whole, whole, whole, wide, wide]
        + [pltpu.VMEM((groups, rows, features), BF16)]
        + [pltpu.SemaphoreType.DMA((2 + 2 * kv_heads,)), pltpu.SemaphoreType.DMA((groups,))]
        + [pltpu.SemaphoreType.DMA((kv_heads + groups,))],
        compiler_params=WHOLE,
        cost_estimate=cost(
            8 * rows * rows * query_width + 4 * rows * width * features * groups,
            6 * rows * query_width + 4 * width * features * groups,
            rows * query_width,
        ),
    )(query_states, key_states, value_states, grad_context, projections)

    if exchange:
        ready, distant = lax.optimization_barrier((grad_key, distant))
        sent, distant, near, next_inputs = lax.optimization_barrier(
            (sent, distant, near, next_inputs)
        )
        first = along_dp(ready, lambda m: parts // 2, parts, groups)
        pieces = shared_inputs(distant, groups)
    came = along_mp(sent, 1, groups)
    if exchange:
        came, ready = lax.optimization_barrier((came, grad_key))
        twice = jnp.concatenate([ready, ready])
    total = kept.astype(F32) + came.astype(F32)
    pairs = [total[b].astype(BF16) for b in range(chips - 1)]
    if exchange:
        first, twice, pieces, pairs = lax.optimization_barrier((first, twice, pieces, pairs))
        keys = {0: lax.dynamic_update_slice(twice, first, (rows, 0))}
        mine = pieces + near
        theirs = [along_mp(piece, 1, groups) for piece in mine]
        bit = parts // 4
        while bit > 1:
            for k in list(keys):
                keys[k ^ bit] = along_dp(keys[k], lambda m, bit=bit: bit, parts, groups)
            bit //= 2
    grad_input = total[chips - 1]
    for b in range(chips - 1):
        shift = [(m, (m + 2 * (b + 1)) % groups) for m in range(groups)]
        grad_input += lax.ppermute(pairs[b], "mp", shift).astype(F32)
    grad_input = grad_input.astype(BF16)

    if exchange:
        beside = []
        for k in range(0, parts // 2, 2):
            if k:
                keys[k], beside = lax.optimization_barrier((keys[k], beside))
            beside.append(along_dp(keys[k], lambda m: 1, parts, groups))
        turned = turned_inputs(mine, theirs, next_inputs, inputs_normed)
        beside[-1], grad_input = lax.optimization_barrier((beside[-1], grad_input))
        keys = [keys[k] for k in range(0, parts // 2, 2)] + beside
        grad_weights = summed_weights(turned, keys)
    else:
        grad_weights = gathered_weights(inputs_normed, grad_key, parts)
    return (grad_query, grad_input, grad_weights)


def solution(mesh):
    placed = (
        P("dp", "mp"),
        P("dp", "mp"),
        P("dp", "mp"),
        P("dp", "mp"),
        P("dp", None),
        P(None, None, "mp"),
    )
    return jax.shard_map(
        body,
        mesh=mesh,
        in_specs=placed,
        out_specs=(P("dp", "mp"), P("dp", "mp"), P("dp", "mp")),
        check_vma=False,
    )
```

```python
import math

import jax
import jax.numpy as jnp
from jax import lax
from jax.experimental import pallas as pl
from jax.experimental.pallas import tpu as pltpu
from jax.sharding import PartitionSpec as P

HEAD_SIZE = 128
F32 = jnp.float32
BF16 = jnp.bfloat16
NN = (((1,), (0,)), ((), ()))
NT = (((1,), (1,)), ((), ()))
TN = (((0,), (0,)), ((), ()))
IN_HBM = pl.BlockSpec(memory_space=pltpu.HBM)
ANYWHERE = pl.BlockSpec(memory_space=pl.ANY)
IN_VMEM = pl.BlockSpec(memory_space=pltpu.VMEM)
CHUNK = 512
PARAMS = pltpu.CompilerParams(vmem_limit_bytes=24 * 1024 * 1024)
WHOLE = pltpu.CompilerParams(vmem_limit_bytes=60 * 1024 * 1024)


def dot(a, b, dims=NN):
    return lax.dot_general(a, b, dims, preferred_element_type=F32)


def cost(flops, moved, transcendentals=0):
    return pl.CostEstimate(flops=flops, bytes_accessed=moved, transcendentals=transcendentals)


def attention_scores(g, q, k, v, do, scores, grad_probs):
    per_group = q.shape[1] // k.shape[1]
    cols = slice(g * HEAD_SIZE, (g + 1) * HEAD_SIZE)
    scores[g] = dot(k[:, cols], stacked(q, g, per_group), NT)
    grad_probs[g] = dot(v[:, cols], stacked(do, g, per_group), NT)


def stacked(array, g, per_group):
    first = g * per_group * HEAD_SIZE
    heads = [array[:, first + h * HEAD_SIZE : first + (h + 1) * HEAD_SIZE] for h in range(per_group)]
    return jnp.concatenate(heads, axis=0)


def attention_softmax(g, scores, grad_probs, probs_b, ds):
    length = scores.shape[1]
    group = scores.shape[2]
    scale = 1.0 / math.sqrt(HEAD_SIZE)
    targets = lax.broadcasted_iota(jnp.int32, (length, length), 0)
    positions = lax.broadcasted_iota(jnp.int32, (length, length), 1)
    allowed = targets <= positions
    for at in range(0, group, length):
        cols = slice(at, at + length)
        masked = jnp.where(allowed, scores[g, :, cols], -1e30)
        raw = jnp.exp((masked - jnp.max(masked, axis=0, keepdims=True)) * scale)
        probs = raw * (1.0 / jnp.sum(raw, axis=0, keepdims=True))
        slopes = grad_probs[g, :, cols]
        delta = jnp.sum(probs * slopes, axis=0, keepdims=True)
        probs_b[:, g * group + at : g * group + at + length] = probs.astype(BF16)
        ds[:, g * group + at : g * group + at + length] = (probs * (slopes - delta)).astype(BF16)


def attention_kernel(
    q_hbm, k_hbm, v_hbm, do_hbm, gk_ref, gv_ref, gq_hbm,
    q, k, v, do, probs_b, ds, gq, scores, grad_probs, sems, out_sems,
):
    length = q.shape[0]
    kv_heads = k.shape[1] // HEAD_SIZE
    group = q.shape[1] // kv_heads
    per_group = group // HEAD_SIZE
    small = [
        pltpu.make_async_copy(k_hbm, k, sems.at[0]),
        pltpu.make_async_copy(v_hbm, v, sems.at[1]),
    ]
    large, stored = [], []
    for g in range(kv_heads):
        cols = pl.ds(g * group, group)
        large.append((
            pltpu.make_async_copy(q_hbm.at[:, cols], q.at[:, cols], sems.at[2 + 2 * g]),
            pltpu.make_async_copy(do_hbm.at[:, cols], do.at[:, cols], sems.at[3 + 2 * g]),
        ))
        stored.append(pltpu.make_async_copy(gq.at[:, cols], gq_hbm.at[:, cols], out_sems.at[g]))
    for copy in small:
        copy.start()
    for pair in large:
        for copy in pair:
            copy.start()
    for copy in small:
        copy.wait()
    for g in range(kv_heads):
        for copy in large[g]:
            copy.wait()
        attention_scores(g, q, k, v, do, scores, grad_probs)
    scale = 1.0 / math.sqrt(HEAD_SIZE)
    for g in range(kv_heads):
        attention_softmax(g, scores, grad_probs, probs_b, ds)
        cols = slice(g * group, (g + 1) * group)
        head = slice(g * HEAD_SIZE, (g + 1) * HEAD_SIZE)
        grad_query = dot(ds[:, cols], k[:, head], TN) * scale
        for h in range(per_group):
            at = g * group + h * HEAD_SIZE
            gq[:, at : at + HEAD_SIZE] = grad_query[h * length : (h + 1) * length].astype(BF16)
        stored[g].start()
        grad_key = dot(ds[:, cols], stacked(q, g, per_group)) * scale
        gk_ref[:, head] = grad_key.astype(BF16)
        gv_ref[:, head] = dot(probs_b[:, cols], stacked(do, g, per_group)).astype(BF16)
    for copy in stored:
        copy.wait()


def partials_kernel(gk_ref, gv_ref, p_hbm, sent_hbm, kept_hbm, p, partial, p_sems, out_sems):
    groups, features = p.shape[0], p.shape[2]
    chips = groups // 2
    member = lax.axis_index("mp")
    chip, core = lax.div(member, 2), lax.rem(member, 2)
    blocks, stored = [], []
    for b in range(groups):
        column = core if b >= chips else 1 - core
        start = (2 * lax.rem(chip + b + 1, chips) + column) * features
        rows = pl.ds(pl.multiple_of(start, features), features)
        blocks.append(pltpu.make_async_copy(p_hbm.at[:, rows, :], p.at[b], p_sems.at[b]))
    for copy in blocks:
        copy.start()
    grads = jnp.concatenate([gk_ref[...], gv_ref[...]], axis=1)
    step = min(CHUNK, features)
    for b in range(groups):
        blocks[b].wait()
        for at in range(0, features, step):
            rows = slice(at, at + step)
            both = jnp.concatenate([p[b, 0, rows, :], p[b, 1, rows, :]], axis=1)
            partial[b, :, rows] = dot(grads, both, NT).astype(BF16)
        target = sent_hbm.at[b] if b < chips else kept_hbm.at[b - chips]
        stored.append(pltpu.make_async_copy(partial.at[b], target, out_sems.at[b]))
        stored[-1].start()
    for copy in stored:
        copy.wait()


def turned_kernel(*refs):
    *blocks, next_ref, x_hbm, out_ref, own, sem = refs
    rows, width = own.shape
    parts = out_ref.shape[1] // rows
    far = groups = parts // 2
    part, member = lax.axis_index("dp"), lax.axis_index("mp")
    cols = pl.ds(pl.multiple_of(part * width, width), width)
    copy = pltpu.make_async_copy(x_hbm.at[:, cols], own, sem)
    copy.start()

    def put(k, piece):
        place = far * lax.rem(k, 2) + 2 * lax.div(lax.rem(k, far), 2) + lax.div(k, far)
        out_ref[:, pl.ds(pl.multiple_of(place * rows, rows), rows)] = piece.T

    partners = [far + (member ^ j) for j in range(0, groups, 2)]
    partners += [k + lax.rem(member, 2) for k in range(2, far, 2)]
    for k, mine, theirs in zip(partners, blocks[: len(partners)], blocks[len(partners) :]):
        put(k, mine[...])
        put(k ^ 1, theirs[...])
    put(jnp.int32(1), next_ref[...])
    copy.wait()
    put(jnp.int32(0), own[...])


def weights_kernel(x_ref, *refs):
    keys, out_ref = refs[:-1], refs[-1]
    rows = keys[0].shape[0]
    total = dot(x_ref[:, :rows], keys[0][...])
    for j in range(1, len(keys)):
        total += dot(x_ref[:, j * rows : (j + 1) * rows], keys[j][...])
    out_ref[...] = total * (1.0 / (2 * len(keys)))


def along_dp(array, partner, parts, groups):
    pairs = [
        (i * groups + m, (i ^ partner(m)) * groups + m)
        for i in range(parts)
        for m in range(groups)
    ]
    return lax.ppermute(array, ("dp", "mp"), pairs)


def along_mp(array, bit, groups):
    return lax.ppermute(array, "mp", [(m, m ^ bit) for m in range(groups)])


def sent_inputs(inputs, parts, groups):
    far = parts // 2
    part, member = lax.axis_index("dp"), lax.axis_index("mp")
    rows, width = inputs.shape[0], inputs.shape[1] // parts

    def block(k):
        return lax.dynamic_slice(inputs, (0, (part ^ k) * width), (rows, width))

    distant = along_dp(block(far + member), lambda m: far + m, parts, groups)
    near = []
    for k in range(2, far, 2):
        sent = block(k + lax.rem(member, 2))
        near.append(along_dp(sent, lambda m, k=k: k + m % 2, parts, groups))
    return distant, near, along_dp(block(1), lambda m: 1, parts, groups)


def shared_inputs(piece, groups):
    pieces = [piece]
    bit = 2
    while bit < groups:
        pieces += [along_mp(piece, bit, groups) for piece in pieces]
        bit *= 2
    return pieces


def turned_inputs(mine, theirs, next_inputs, inputs):
    rows, width = next_inputs.shape
    blocks = [*mine, *theirs, next_inputs]
    return pl.pallas_call(
        turned_kernel,
        in_specs=[IN_VMEM] * len(blocks) + [IN_HBM],
        out_specs=IN_VMEM,
        out_shape=jax.ShapeDtypeStruct((width, inputs.shape[1] // width * rows), inputs.dtype),
        scratch_shapes=[pltpu.VMEM((rows, width), inputs.dtype), pltpu.SemaphoreType.DMA],
        compiler_params=PARAMS,
        cost_estimate=cost(0, 4 * inputs.size),
    )(*blocks, inputs)


def summed_weights(turned, keys):
    width, columns = turned.shape[0], keys[0].shape[1]
    return pl.pallas_call(
        weights_kernel,
        out_specs=IN_VMEM,
        out_shape=jax.ShapeDtypeStruct((width, columns), F32),
        compiler_params=PARAMS,
        cost_estimate=cost(
            2 * turned.size * columns, 2 * turned.size + 4 * width * columns
        ),
    )(turned, *keys)


def gathered_weights(inputs, grad_key, parts):
    rows = inputs.shape[0]
    width = inputs.shape[1] // parts
    blocks = inputs.reshape(rows, parts, width).transpose(1, 0, 2)
    mine = lax.all_to_all(blocks, "dp", split_axis=0, concat_axis=0, tiled=True)
    keys = lax.all_gather(grad_key, "dp", axis=0)
    return jnp.einsum("psd,psc->dc", mine, keys, preferred_element_type=F32) / parts


def body(query_states, key_states, value_states, grad_context, inputs_normed, projections):
    parts = lax.axis_size("dp")
    groups = lax.axis_size("mp")
    chips = groups // 2
    rows, width = key_states.shape
    query_width = query_states.shape[1]
    features = projections.shape[1] // groups
    kv_heads = width // HEAD_SIZE
    partial = jax.ShapeDtypeStruct((chips, rows, features), BF16)
    exchange = parts == 2 * groups and inputs_normed.shape[1] % (parts * 128) == 0
    if exchange:
        distant, near, next_inputs = sent_inputs(inputs_normed, parts, groups)

    whole = pltpu.VMEM((rows, query_width), BF16)
    narrow = pltpu.VMEM((rows, width), BF16)
    wide = pltpu.VMEM((kv_heads, rows, query_width // kv_heads), F32)
    grad_key, grad_value, grad_query = pl.pallas_call(
        attention_kernel,
        in_specs=[IN_HBM] * 4,
        out_specs=[IN_VMEM, IN_VMEM, ANYWHERE],
        out_shape=(
            jax.ShapeDtypeStruct((rows, width), BF16),
            jax.ShapeDtypeStruct((rows, width), BF16),
            jax.ShapeDtypeStruct((rows, query_width), BF16),
        ),
        scratch_shapes=[whole, narrow, narrow, whole, whole, whole, whole, wide, wide]
        + [pltpu.SemaphoreType.DMA((2 + 2 * kv_heads,)), pltpu.SemaphoreType.DMA((kv_heads,))],
        compiler_params=WHOLE,
        cost_estimate=cost(
            10 * rows * rows * query_width, 6 * rows * query_width, rows * query_width
        ),
    )(query_states, key_states, value_states, grad_context)

    sent, kept = pl.pallas_call(
        partials_kernel,
        in_specs=[IN_VMEM, IN_VMEM, IN_HBM],
        out_specs=[ANYWHERE, ANYWHERE],
        out_shape=(partial, partial),
        scratch_shapes=[
            pltpu.VMEM((groups, 2, features, width), BF16),
            pltpu.VMEM((groups, rows, features), BF16),
            pltpu.SemaphoreType.DMA((groups,)),
            pltpu.SemaphoreType.DMA((groups,)),
        ],
        compiler_params=WHOLE,
        cost_estimate=cost(
            4 * rows * width * features * groups, 4 * width * features * groups
        ),
    )(grad_key, grad_value, projections)

    if exchange:
        ready, near = lax.optimization_barrier((grad_key, near))
        first = along_dp(ready, lambda m: parts // 2, parts, groups)
        twice = jnp.concatenate([grad_key, grad_key])
        first, twice, sent, kept, distant, near, next_inputs = lax.optimization_barrier(
            (first, twice, sent, kept, distant, near, next_inputs)
        )
        pieces = shared_inputs(distant, groups)
        keys = {0: lax.dynamic_update_slice(twice, first, (rows, 0))}
        mine = pieces + near
        theirs = [along_mp(piece, 1, groups) for piece in mine]
        bit = parts // 4
        while bit > 1:
            for k in list(keys):
                keys[k ^ bit] = along_dp(keys[k], lambda m, bit=bit: bit, parts, groups)
            bit //= 2
    came = along_mp(sent, 1, groups)
    total = kept.astype(F32) + came.astype(F32)
    grad_input = total[chips - 1]
    for b in range(chips - 1):
        shift = [(m, (m + 2 * (b + 1)) % groups) for m in range(groups)]
        grad_input += lax.ppermute(total[b].astype(BF16), "mp", shift).astype(F32)
    grad_input = grad_input.astype(BF16)

    if exchange:
        beside = []
        for k in range(0, parts // 2, 2):
            if k:
                keys[k], beside = lax.optimization_barrier((keys[k], beside))
            beside.append(along_dp(keys[k], lambda m: 1, parts, groups))
        turned = turned_inputs(mine, theirs, next_inputs, inputs_normed)
        beside[-1], grad_input = lax.optimization_barrier((beside[-1], grad_input))
        keys = [keys[k] for k in range(0, parts // 2, 2)] + beside
        grad_weights = summed_weights(turned, keys)
    else:
        grad_weights = gathered_weights(inputs_normed, grad_key, parts)
    return (grad_query, grad_input, grad_weights)


def solution(mesh):
    placed = (
        P("dp", "mp"),
        P("dp", "mp"),
        P("dp", "mp"),
        P("dp", "mp"),
        P("dp", None),
        P(None, None, "mp"),
    )
    return jax.shard_map(
        body,
        mesh=mesh,
        in_specs=placed,
        out_specs=(P("dp", "mp"), P("dp", "mp"), P("dp", "mp")),
        check_vma=False,
    )
```

```python
import math

import jax
import jax.numpy as jnp
from jax import lax
from jax.experimental import pallas as pl
from jax.experimental.pallas import tpu as pltpu
from jax.sharding import PartitionSpec as P

HEAD_SIZE = 128
F32 = jnp.float32
BF16 = jnp.bfloat16
NN = (((1,), (0,)), ((), ()))
NT = (((1,), (1,)), ((), ()))
TN = (((0,), (0,)), ((), ()))
IN_HBM = pl.BlockSpec(memory_space=pltpu.HBM)
ANYWHERE = pl.BlockSpec(memory_space=pl.ANY)
IN_VMEM = pl.BlockSpec(memory_space=pltpu.VMEM)
CHUNK = 512
PARAMS = pltpu.CompilerParams(vmem_limit_bytes=24 * 1024 * 1024)
WHOLE = pltpu.CompilerParams(vmem_limit_bytes=60 * 1024 * 1024)


def dot(a, b, dims=NN):
    return lax.dot_general(a, b, dims, preferred_element_type=F32)


def cost(flops, moved, transcendentals=0):
    return pl.CostEstimate(flops=flops, bytes_accessed=moved, transcendentals=transcendentals)


def attention_scores(g, q, k, v, do, scores, grad_probs):
    per_group = q.shape[1] // k.shape[1]
    cols = slice(g * HEAD_SIZE, (g + 1) * HEAD_SIZE)
    scores[g] = dot(k[:, cols], stacked(q, g, per_group), NT)
    grad_probs[g] = dot(v[:, cols], stacked(do, g, per_group), NT)


def stacked(array, g, per_group):
    first = g * per_group * HEAD_SIZE
    heads = [array[:, first + h * HEAD_SIZE : first + (h + 1) * HEAD_SIZE] for h in range(per_group)]
    return jnp.concatenate(heads, axis=0)


def attention_softmax(g, scores, grad_probs, probs_b, ds):
    length = scores.shape[1]
    group = scores.shape[2]
    scale = 1.0 / math.sqrt(HEAD_SIZE)
    targets = lax.broadcasted_iota(jnp.int32, (length, length), 0)
    positions = lax.broadcasted_iota(jnp.int32, (length, length), 1)
    allowed = targets <= positions
    for at in range(0, group, length):
        cols = slice(at, at + length)
        masked = jnp.where(allowed, scores[g, :, cols], -1e30)
        raw = jnp.exp((masked - jnp.max(masked, axis=0, keepdims=True)) * scale)
        probs = raw * (1.0 / jnp.sum(raw, axis=0, keepdims=True))
        slopes = grad_probs[g, :, cols]
        delta = jnp.sum(probs * slopes, axis=0, keepdims=True)
        probs_b[:, g * group + at : g * group + at + length] = probs.astype(BF16)
        ds[:, g * group + at : g * group + at + length] = (probs * (slopes - delta)).astype(BF16)


def attention_kernel(
    q_hbm, k_hbm, v_hbm, do_hbm, gk_ref, gv_ref, twice_ref, gq_hbm,
    q, k, v, do, probs_b, ds, gq, scores, grad_probs, sems, out_sems,
):
    length = q.shape[0]
    kv_heads = k.shape[1] // HEAD_SIZE
    group = q.shape[1] // kv_heads
    per_group = group // HEAD_SIZE
    small = [
        pltpu.make_async_copy(k_hbm, k, sems.at[0]),
        pltpu.make_async_copy(v_hbm, v, sems.at[1]),
    ]
    large, stored = [], []
    for g in range(kv_heads):
        cols = pl.ds(g * group, group)
        large.append((
            pltpu.make_async_copy(q_hbm.at[:, cols], q.at[:, cols], sems.at[2 + 2 * g]),
            pltpu.make_async_copy(do_hbm.at[:, cols], do.at[:, cols], sems.at[3 + 2 * g]),
        ))
        stored.append(pltpu.make_async_copy(gq.at[:, cols], gq_hbm.at[:, cols], out_sems.at[g]))
    for copy in small:
        copy.start()
    for pair in large:
        for copy in pair:
            copy.start()
    for copy in small:
        copy.wait()
    for g in range(kv_heads):
        for copy in large[g]:
            copy.wait()
        attention_scores(g, q, k, v, do, scores, grad_probs)
    scale = 1.0 / math.sqrt(HEAD_SIZE)
    for g in range(kv_heads):
        attention_softmax(g, scores, grad_probs, probs_b, ds)
        cols = slice(g * group, (g + 1) * group)
        head = slice(g * HEAD_SIZE, (g + 1) * HEAD_SIZE)
        grad_query = dot(ds[:, cols], k[:, head], TN) * scale
        for h in range(per_group):
            at = g * group + h * HEAD_SIZE
            gq[:, at : at + HEAD_SIZE] = grad_query[h * length : (h + 1) * length].astype(BF16)
        stored[g].start()
        grad_key = dot(ds[:, cols], stacked(q, g, per_group)) * scale
        gk_ref[:, head] = grad_key.astype(BF16)
        twice_ref[:length, head] = grad_key.astype(BF16)
        twice_ref[length:, head] = grad_key.astype(BF16)
        gv_ref[:, head] = dot(probs_b[:, cols], stacked(do, g, per_group)).astype(BF16)
    for copy in stored:
        copy.wait()


def partials_kernel(gk_ref, gv_ref, p_hbm, sent_hbm, kept_hbm, p, partial, p_sems, out_sems):
    groups, features = p.shape[0], p.shape[2]
    chips = groups // 2
    member = lax.axis_index("mp")
    chip, core = lax.div(member, 2), lax.rem(member, 2)
    step = min(CHUNK, features)
    pieces = [(b, at) for b in range(groups) for at in range(0, features, step)]
    loads, stored = [], []
    for j, (b, at) in enumerate(pieces):
        column = core if b >= chips else 1 - core
        start = (2 * lax.rem(chip + b + 1, chips) + column) * features + at
        rows = pl.ds(pl.multiple_of(start, step), step)
        target = p.at[b, :, pl.ds(at, step), :]
        loads.append(pltpu.make_async_copy(p_hbm.at[:, rows, :], target, p_sems.at[j]))
    for copy in loads:
        copy.start()
    grads = jnp.concatenate([gk_ref[...], gv_ref[...]], axis=1)
    for j, (b, at) in enumerate(pieces):
        loads[j].wait()
        rows = slice(at, at + step)
        both = jnp.concatenate([p[b, 0, rows, :], p[b, 1, rows, :]], axis=1)
        partial[b, :, rows] = dot(grads, both, NT).astype(BF16)
        target = sent_hbm.at[b] if b < chips else kept_hbm.at[b - chips]
        cols = pl.ds(at, step)
        copy = pltpu.make_async_copy(partial.at[b, :, cols], target.at[:, cols], out_sems.at[j])
        copy.start()
        stored.append(copy)
    for copy in stored:
        copy.wait()


def turned_kernel(*refs):
    *blocks, next_ref, x_hbm, out_ref, own, sem = refs
    rows, width = own.shape
    parts = out_ref.shape[1] // rows
    far = groups = parts // 2
    part, member = lax.axis_index("dp"), lax.axis_index("mp")
    cols = pl.ds(pl.multiple_of(part * width, width), width)
    copy = pltpu.make_async_copy(x_hbm.at[:, cols], own, sem)
    copy.start()

    def put(k, piece):
        place = far * lax.rem(k, 2) + 2 * lax.div(lax.rem(k, far), 2) + lax.div(k, far)
        out_ref[:, pl.ds(pl.multiple_of(place * rows, rows), rows)] = piece.T

    partners = [far + (member ^ j) for j in range(0, groups, 2)]
    partners += [k + lax.rem(member, 2) for k in range(2, far, 2)]
    for k, mine, theirs in zip(partners, blocks[: len(partners)], blocks[len(partners) :]):
        put(k, mine[...])
        put(k ^ 1, theirs[...])
    put(jnp.int32(1), next_ref[...])
    copy.wait()
    put(jnp.int32(0), own[...])


def weights_kernel(x_ref, *refs):
    *keys, out_hbm, out, sems = refs
    rows = keys[0].shape[0]
    half = x_ref.shape[0] // 2
    copies = []
    for h in range(2):
        part = slice(h * half, (h + 1) * half)
        total = dot(x_ref[part, :rows], keys[0][...])
        for j in range(1, len(keys)):
            total += dot(x_ref[part, j * rows : (j + 1) * rows], keys[j][...])
        out[part, :] = total * (1.0 / (2 * len(keys)))
        copies.append(pltpu.make_async_copy(out.at[part, :], out_hbm.at[part, :], sems.at[h]))
        copies[h].start()
    for copy in copies:
        copy.wait()


def along_dp(array, partner, parts, groups):
    pairs = [
        (i * groups + m, (i ^ partner(m)) * groups + m)
        for i in range(parts)
        for m in range(groups)
    ]
    return lax.ppermute(array, ("dp", "mp"), pairs)


def along_mp(array, bit, groups):
    return lax.ppermute(array, "mp", [(m, m ^ bit) for m in range(groups)])


def sent_inputs(inputs, parts, groups):
    far = parts // 2
    part, member = lax.axis_index("dp"), lax.axis_index("mp")
    rows, width = inputs.shape[0], inputs.shape[1] // parts

    def block(k):
        return lax.dynamic_slice(inputs, (0, (part ^ k) * width), (rows, width))

    distant = along_dp(block(far + member), lambda m: far + m, parts, groups)
    near = []
    for k in range(2, far, 2):
        sent = block(k + lax.rem(member, 2))
        near.append(along_dp(sent, lambda m, k=k: k + m % 2, parts, groups))
    return distant, near, along_dp(block(1), lambda m: 1, parts, groups)


def shared_inputs(piece, groups):
    pieces = [piece]
    bit = 2
    while bit < groups:
        pieces += [along_mp(piece, bit, groups) for piece in pieces]
        bit *= 2
    return pieces


def turned_inputs(mine, theirs, next_inputs, inputs):
    rows, width = next_inputs.shape
    blocks = [*mine, *theirs, next_inputs]
    return pl.pallas_call(
        turned_kernel,
        in_specs=[IN_VMEM] * len(blocks) + [IN_HBM],
        out_specs=IN_VMEM,
        out_shape=jax.ShapeDtypeStruct((width, inputs.shape[1] // width * rows), inputs.dtype),
        scratch_shapes=[pltpu.VMEM((rows, width), inputs.dtype), pltpu.SemaphoreType.DMA],
        compiler_params=PARAMS,
        cost_estimate=cost(0, 4 * inputs.size),
    )(*blocks, inputs)


def summed_weights(turned, keys):
    width, columns = turned.shape[0], keys[0].shape[1]
    return pl.pallas_call(
        weights_kernel,
        out_specs=ANYWHERE,
        out_shape=jax.ShapeDtypeStruct((width, columns), F32),
        scratch_shapes=[pltpu.VMEM((width, columns), F32), pltpu.SemaphoreType.DMA((2,))],
        compiler_params=PARAMS,
        cost_estimate=cost(
            2 * turned.size * columns, 2 * turned.size + 4 * width * columns
        ),
    )(turned, *keys)


def gathered_weights(inputs, grad_key, parts):
    rows = inputs.shape[0]
    width = inputs.shape[1] // parts
    blocks = inputs.reshape(rows, parts, width).transpose(1, 0, 2)
    mine = lax.all_to_all(blocks, "dp", split_axis=0, concat_axis=0, tiled=True)
    keys = lax.all_gather(grad_key, "dp", axis=0)
    return jnp.einsum("psd,psc->dc", mine, keys, preferred_element_type=F32) / parts


def body(query_states, key_states, value_states, grad_context, inputs_normed, projections):
    parts = lax.axis_size("dp")
    groups = lax.axis_size("mp")
    chips = groups // 2
    rows, width = key_states.shape
    query_width = query_states.shape[1]
    features = projections.shape[1] // groups
    kv_heads = width // HEAD_SIZE
    partial = jax.ShapeDtypeStruct((chips, rows, features), BF16)
    exchange = parts == 2 * groups and inputs_normed.shape[1] % (parts * 128) == 0
    if exchange:
        distant, near, next_inputs = sent_inputs(inputs_normed, parts, groups)

    whole = pltpu.VMEM((rows, query_width), BF16)
    narrow = pltpu.VMEM((rows, width), BF16)
    wide = pltpu.VMEM((kv_heads, rows, query_width // kv_heads), F32)
    grad_key, grad_value, twice, grad_query = pl.pallas_call(
        attention_kernel,
        in_specs=[IN_HBM] * 4,
        out_specs=[IN_VMEM, IN_VMEM, IN_VMEM, ANYWHERE],
        out_shape=(
            jax.ShapeDtypeStruct((rows, width), BF16),
            jax.ShapeDtypeStruct((rows, width), BF16),
            jax.ShapeDtypeStruct((2 * rows, width), BF16),
            jax.ShapeDtypeStruct((rows, query_width), BF16),
        ),
        scratch_shapes=[whole, narrow, narrow, whole, whole, whole, whole, wide, wide]
        + [pltpu.SemaphoreType.DMA((2 + 2 * kv_heads,)), pltpu.SemaphoreType.DMA((kv_heads,))],
        compiler_params=WHOLE,
        cost_estimate=cost(
            10 * rows * rows * query_width, 6 * rows * query_width, rows * query_width
        ),
    )(query_states, key_states, value_states, grad_context)

    copies = groups * (features // min(CHUNK, features))
    sent, kept = pl.pallas_call(
        partials_kernel,
        in_specs=[IN_VMEM, IN_VMEM, IN_HBM],
        out_specs=[ANYWHERE, ANYWHERE],
        out_shape=(partial, partial),
        scratch_shapes=[
            pltpu.VMEM((groups, 2, features, width), BF16),
            pltpu.VMEM((groups, rows, features), BF16),
            pltpu.SemaphoreType.DMA((copies,)),
            pltpu.SemaphoreType.DMA((copies,)),
        ],
        compiler_params=WHOLE,
        cost_estimate=cost(
            4 * rows * width * features * groups, 4 * width * features * groups
        ),
    )(grad_key, grad_value, projections)

    if exchange:
        ready, near = lax.optimization_barrier((grad_key, near))
        first = along_dp(ready, lambda m: parts // 2, parts, groups)
        first, twice, sent, kept, distant, near, next_inputs = lax.optimization_barrier(
            (first, twice, sent, kept, distant, near, next_inputs)
        )
        pieces = shared_inputs(distant, groups)
        keys = {0: lax.dynamic_update_slice(twice, first, (rows, 0))}
        bit = parts // 4
        while bit > 1:
            for k in list(keys):
                keys[k ^ bit] = along_dp(keys[k], lambda m, bit=bit: bit, parts, groups)
            bit //= 2
        beside = [along_dp(keys[0], lambda m: 1, parts, groups)]
        pieces[1:], _ = lax.optimization_barrier((pieces[1:], (beside, keys)))
        mine = pieces + near
        theirs = [along_mp(piece, 1, groups) for piece in mine]
    came = along_mp(sent, 1, groups)
    total = kept.astype(F32) + came.astype(F32)
    grad_input = total[chips - 1]
    for b in range(chips - 1):
        shift = [(m, (m + 2 * (b + 1)) % groups) for m in range(groups)]
        grad_input += lax.ppermute(total[b].astype(BF16), "mp", shift).astype(F32)
    grad_input = grad_input.astype(BF16)

    if exchange:
        for k in range(2, parts // 2, 2):
            beside.append(along_dp(keys[k], lambda m: 1, parts, groups))
        turned = turned_inputs(mine, theirs, next_inputs, inputs_normed)
        beside[-1], grad_input = lax.optimization_barrier((beside[-1], grad_input))
        keys = [keys[k] for k in range(0, parts // 2, 2)] + beside
        grad_weights = summed_weights(turned, keys)
    else:
        grad_weights = gathered_weights(inputs_normed, grad_key, parts)
    return (grad_query, grad_input, grad_weights)


def solution(mesh):
    placed = (
        P("dp", "mp"),
        P("dp", "mp"),
        P("dp", "mp"),
        P("dp", "mp"),
        P("dp", None),
        P(None, None, "mp"),
    )
    return jax.shard_map(
        body,
        mesh=mesh,
        in_specs=placed,
        out_specs=(P("dp", "mp"), P("dp", "mp"), P("dp", "mp")),
        check_vma=False,
    )
```

```python
import math

import jax
import jax.numpy as jnp
from jax import lax
from jax.experimental import pallas as pl
from jax.experimental.pallas import tpu as pltpu
from jax.sharding import PartitionSpec as P

HEAD_SIZE = 128
F32 = jnp.float32
BF16 = jnp.bfloat16
NN = (((1,), (0,)), ((), ()))
NT = (((1,), (1,)), ((), ()))
TN = (((0,), (0,)), ((), ()))
IN_HBM = pl.BlockSpec(memory_space=pltpu.HBM)
ANYWHERE = pl.BlockSpec(memory_space=pl.ANY)
IN_VMEM = pl.BlockSpec(memory_space=pltpu.VMEM)
CHUNK = 512
PARAMS = pltpu.CompilerParams(vmem_limit_bytes=24 * 1024 * 1024)
WHOLE = pltpu.CompilerParams(vmem_limit_bytes=60 * 1024 * 1024)


def dot(a, b, dims=NN):
    return lax.dot_general(a, b, dims, preferred_element_type=F32)


def cost(flops, moved, transcendentals=0):
    return pl.CostEstimate(flops=flops, bytes_accessed=moved, transcendentals=transcendentals)


def attention_scores(g, q, k, v, do, scores, grad_probs):
    per_group = q.shape[1] // k.shape[1]
    cols = slice(g * HEAD_SIZE, (g + 1) * HEAD_SIZE)
    scores[g] = dot(k[:, cols], stacked(q, g, per_group), NT)
    grad_probs[g] = dot(v[:, cols], stacked(do, g, per_group), NT)


def stacked(array, g, per_group):
    first = g * per_group * HEAD_SIZE
    heads = [array[:, first + h * HEAD_SIZE : first + (h + 1) * HEAD_SIZE] for h in range(per_group)]
    return jnp.concatenate(heads, axis=0)


def attention_softmax(g, scores, grad_probs, probs_b, ds):
    length = scores.shape[1]
    group = scores.shape[2]
    scale = 1.0 / math.sqrt(HEAD_SIZE)
    targets = lax.broadcasted_iota(jnp.int32, (length, length), 0)
    positions = lax.broadcasted_iota(jnp.int32, (length, length), 1)
    allowed = targets <= positions
    for at in range(0, group, length):
        cols = slice(at, at + length)
        masked = jnp.where(allowed, scores[g, :, cols], -1e30)
        raw = jnp.exp((masked - jnp.max(masked, axis=0, keepdims=True)) * scale)
        probs = raw * (1.0 / jnp.sum(raw, axis=0, keepdims=True))
        slopes = grad_probs[g, :, cols]
        delta = jnp.sum(probs * slopes, axis=0, keepdims=True)
        probs_b[:, g * group + at : g * group + at + length] = probs.astype(BF16)
        ds[:, g * group + at : g * group + at + length] = (probs * (slopes - delta)).astype(BF16)


def attention_kernel(
    q_hbm, k_hbm, v_hbm, do_hbm, gk_ref, gv_ref, twice_ref, gq_hbm,
    q, k, v, do, probs_b, ds, gq, scores, grad_probs, sems, out_sems,
):
    length = q.shape[0]
    kv_heads = k.shape[1] // HEAD_SIZE
    group = q.shape[1] // kv_heads
    per_group = group // HEAD_SIZE
    small = [
        pltpu.make_async_copy(k_hbm, k, sems.at[0]),
        pltpu.make_async_copy(v_hbm, v, sems.at[1]),
    ]
    large, stored = [], []
    for g in range(kv_heads):
        cols = pl.ds(g * group, group)
        large.append((
            pltpu.make_async_copy(q_hbm.at[:, cols], q.at[:, cols], sems.at[2 + 2 * g]),
            pltpu.make_async_copy(do_hbm.at[:, cols], do.at[:, cols], sems.at[3 + 2 * g]),
        ))
        stored.append(pltpu.make_async_copy(gq.at[:, cols], gq_hbm.at[:, cols], out_sems.at[g]))
    for copy in small:
        copy.start()
    for pair in large:
        for copy in pair:
            copy.start()
    for copy in small:
        copy.wait()
    for g in range(kv_heads):
        for copy in large[g]:
            copy.wait()
        attention_scores(g, q, k, v, do, scores, grad_probs)
    scale = 1.0 / math.sqrt(HEAD_SIZE)
    for g in range(kv_heads):
        attention_softmax(g, scores, grad_probs, probs_b, ds)
        cols = slice(g * group, (g + 1) * group)
        head = slice(g * HEAD_SIZE, (g + 1) * HEAD_SIZE)
        grad_query = dot(ds[:, cols], k[:, head], TN) * scale
        for h in range(per_group):
            at = g * group + h * HEAD_SIZE
            gq[:, at : at + HEAD_SIZE] = grad_query[h * length : (h + 1) * length].astype(BF16)
        stored[g].start()
        grad_key = dot(ds[:, cols], stacked(q, g, per_group)) * scale
        gk_ref[:, head] = grad_key.astype(BF16)
        twice_ref[:length, head] = grad_key.astype(BF16)
        twice_ref[length:, head] = grad_key.astype(BF16)
        gv_ref[:, head] = dot(probs_b[:, cols], stacked(do, g, per_group)).astype(BF16)
    for copy in stored:
        copy.wait()


def partials_kernel(
    gk_hbm, gv_hbm, p_hbm, sent_hbm, kept_hbm, grads, p, partial, sems, p_sems, out_sems,
):
    groups, features = p.shape[0], p.shape[2]
    chips = groups // 2
    member = lax.axis_index("mp")
    chip, core = lax.div(member, 2), lax.rem(member, 2)
    step = min(CHUNK, features)
    pieces = [(b, at) for b in range(groups) for at in range(0, features, step)]
    loads, stored = [], []
    for j, (b, at) in enumerate(pieces):
        column = core if b >= chips else 1 - core
        start = (2 * lax.rem(chip + b + 1, chips) + column) * features + at
        rows = pl.ds(pl.multiple_of(start, step), step)
        target = p.at[b, :, pl.ds(at, step), :]
        loads.append(pltpu.make_async_copy(p_hbm.at[:, rows, :], target, p_sems.at[j]))
    width = p.shape[3]
    small = [
        pltpu.make_async_copy(gk_hbm, grads.at[:, pl.ds(0, width)], sems.at[0]),
        pltpu.make_async_copy(gv_hbm, grads.at[:, pl.ds(width, width)], sems.at[1]),
    ]
    for copy in small + loads:
        copy.start()
    for copy in small:
        copy.wait()
    both_grads = grads[...]
    for j, (b, at) in enumerate(pieces):
        loads[j].wait()
        rows = slice(at, at + step)
        both = jnp.concatenate([p[b, 0, rows, :], p[b, 1, rows, :]], axis=1)
        partial[b, :, rows] = dot(both_grads, both, NT).astype(BF16)
        target = sent_hbm.at[b] if b < chips else kept_hbm.at[b - chips]
        cols = pl.ds(at, step)
        copy = pltpu.make_async_copy(partial.at[b, :, cols], target.at[:, cols], out_sems.at[j])
        copy.start()
        stored.append(copy)
    for copy in stored:
        copy.wait()


def turned_kernel(*refs):
    *blocks, next_ref, x_hbm, out_ref, own, sem = refs
    rows, width = own.shape
    parts = out_ref.shape[1] // rows
    far = groups = parts // 2
    part, member = lax.axis_index("dp"), lax.axis_index("mp")
    cols = pl.ds(pl.multiple_of(part * width, width), width)
    copy = pltpu.make_async_copy(x_hbm.at[:, cols], own, sem)
    copy.start()

    def put(k, piece):
        place = far * lax.rem(k, 2) + 2 * lax.div(lax.rem(k, far), 2) + lax.div(k, far)
        out_ref[:, pl.ds(pl.multiple_of(place * rows, rows), rows)] = piece.T

    partners = [far + (member ^ j) for j in range(0, groups, 2)]
    partners += [k + lax.rem(member, 2) for k in range(2, far, 2)]
    for k, mine, theirs in zip(partners, blocks[: len(partners)], blocks[len(partners) :]):
        put(k, mine[...])
        put(k ^ 1, theirs[...])
    put(jnp.int32(1), next_ref[...])
    copy.wait()
    put(jnp.int32(0), own[...])


def weights_kernel(x_ref, *refs):
    *keys, out_hbm, out, sems = refs
    rows = keys[0].shape[0]
    half = x_ref.shape[0] // 2
    copies = []
    for h in range(2):
        part = slice(h * half, (h + 1) * half)
        total = dot(x_ref[part, :rows], keys[0][...])
        for j in range(1, len(keys)):
            total += dot(x_ref[part, j * rows : (j + 1) * rows], keys[j][...])
        out[part, :] = total * (1.0 / (2 * len(keys)))
        copies.append(pltpu.make_async_copy(out.at[part, :], out_hbm.at[part, :], sems.at[h]))
        copies[h].start()
    for copy in copies:
        copy.wait()


def along_dp(array, partner, parts, groups):
    pairs = [
        (i * groups + m, (i ^ partner(m)) * groups + m)
        for i in range(parts)
        for m in range(groups)
    ]
    return lax.ppermute(array, ("dp", "mp"), pairs)


def along_mp(array, bit, groups):
    return lax.ppermute(array, "mp", [(m, m ^ bit) for m in range(groups)])


def sent_inputs(inputs, parts, groups):
    far = parts // 2
    part, member = lax.axis_index("dp"), lax.axis_index("mp")
    rows, width = inputs.shape[0], inputs.shape[1] // parts

    def block(k):
        return lax.dynamic_slice(inputs, (0, (part ^ k) * width), (rows, width))

    distant = along_dp(block(far + member), lambda m: far + m, parts, groups)
    near = []
    for k in range(2, far, 2):
        sent = block(k + lax.rem(member, 2))
        near.append(along_dp(sent, lambda m, k=k: k + m % 2, parts, groups))
    return distant, near, along_dp(block(1), lambda m: 1, parts, groups)


def shared_inputs(piece, groups):
    pieces = [piece]
    bit = 2
    while bit < groups:
        pieces += [along_mp(piece, bit, groups) for piece in pieces]
        bit *= 2
    return pieces


def turned_inputs(mine, theirs, next_inputs, inputs):
    rows, width = next_inputs.shape
    blocks = [*mine, *theirs, next_inputs]
    return pl.pallas_call(
        turned_kernel,
        in_specs=[IN_VMEM] * len(blocks) + [IN_HBM],
        out_specs=IN_VMEM,
        out_shape=jax.ShapeDtypeStruct((width, inputs.shape[1] // width * rows), inputs.dtype),
        scratch_shapes=[pltpu.VMEM((rows, width), inputs.dtype), pltpu.SemaphoreType.DMA],
        compiler_params=PARAMS,
        cost_estimate=cost(0, 4 * inputs.size),
    )(*blocks, inputs)


def summed_weights(turned, keys):
    width, columns = turned.shape[0], keys[0].shape[1]
    return pl.pallas_call(
        weights_kernel,
        out_specs=ANYWHERE,
        out_shape=jax.ShapeDtypeStruct((width, columns), F32),
        scratch_shapes=[pltpu.VMEM((width, columns), F32), pltpu.SemaphoreType.DMA((2,))],
        compiler_params=PARAMS,
        cost_estimate=cost(
            2 * turned.size * columns, 2 * turned.size + 4 * width * columns
        ),
    )(turned, *keys)


def gathered_weights(inputs, grad_key, parts):
    rows = inputs.shape[0]
    width = inputs.shape[1] // parts
    blocks = inputs.reshape(rows, parts, width).transpose(1, 0, 2)
    mine = lax.all_to_all(blocks, "dp", split_axis=0, concat_axis=0, tiled=True)
    keys = lax.all_gather(grad_key, "dp", axis=0)
    return jnp.einsum("psd,psc->dc", mine, keys, preferred_element_type=F32) / parts


def body(query_states, key_states, value_states, grad_context, inputs_normed, projections):
    parts = lax.axis_size("dp")
    groups = lax.axis_size("mp")
    chips = groups // 2
    rows, width = key_states.shape
    query_width = query_states.shape[1]
    features = projections.shape[1] // groups
    kv_heads = width // HEAD_SIZE
    partial = jax.ShapeDtypeStruct((chips, rows, features), BF16)
    exchange = parts == 2 * groups and inputs_normed.shape[1] % (parts * 128) == 0
    if exchange:
        distant, near, next_inputs = sent_inputs(inputs_normed, parts, groups)

    whole = pltpu.VMEM((rows, query_width), BF16)
    narrow = pltpu.VMEM((rows, width), BF16)
    wide = pltpu.VMEM((kv_heads, rows, query_width // kv_heads), F32)
    grad_key, grad_value, twice, grad_query = pl.pallas_call(
        attention_kernel,
        in_specs=[IN_HBM] * 4,
        out_specs=[IN_VMEM, IN_VMEM, IN_VMEM, ANYWHERE],
        out_shape=(
            jax.ShapeDtypeStruct((rows, width), BF16),
            jax.ShapeDtypeStruct((rows, width), BF16),
            jax.ShapeDtypeStruct((2 * rows, width), BF16),
            jax.ShapeDtypeStruct((rows, query_width), BF16),
        ),
        scratch_shapes=[whole, narrow, narrow, whole, whole, whole, whole, wide, wide]
        + [pltpu.SemaphoreType.DMA((2 + 2 * kv_heads,)), pltpu.SemaphoreType.DMA((kv_heads,))],
        compiler_params=WHOLE,
        cost_estimate=cost(
            10 * rows * rows * query_width, 6 * rows * query_width, rows * query_width
        ),
    )(query_states, key_states, value_states, grad_context)

    copies = groups * (features // min(CHUNK, features))
    sent, kept = pl.pallas_call(
        partials_kernel,
        in_specs=[IN_HBM] * 3,
        out_specs=[ANYWHERE, ANYWHERE],
        out_shape=(partial, partial),
        scratch_shapes=[
            pltpu.VMEM((rows, 2 * width), BF16),
            pltpu.VMEM((groups, 2, features, width), BF16),
            pltpu.VMEM((groups, rows, features), BF16),
            pltpu.SemaphoreType.DMA((2,)),
            pltpu.SemaphoreType.DMA((copies,)),
            pltpu.SemaphoreType.DMA((copies,)),
        ],
        compiler_params=WHOLE,
        cost_estimate=cost(
            4 * rows * width * features * groups, 4 * width * features * groups
        ),
    )(grad_key, grad_value, projections)

    if exchange:
        ready, near = lax.optimization_barrier((grad_key, near))
        first = along_dp(ready, lambda m: parts // 2, parts, groups)
        first, twice, sent, kept, distant, near, next_inputs = lax.optimization_barrier(
            (first, twice, sent, kept, distant, near, next_inputs)
        )
        pieces = shared_inputs(distant, groups)
        keys = {0: lax.dynamic_update_slice(twice, first, (rows, 0))}
        bit = parts // 4
        while bit > 1:
            for k in list(keys):
                keys[k ^ bit] = along_dp(keys[k], lambda m, bit=bit: bit, parts, groups)
            bit //= 2
        beside = [along_dp(keys[0], lambda m: 1, parts, groups)]
        pieces[1:], _ = lax.optimization_barrier((pieces[1:], (beside, keys)))
        mine = pieces + near
        theirs = [along_mp(piece, 1, groups) for piece in mine]
    came = along_mp(sent, 1, groups)
    pairs = (kept[: chips - 1].astype(F32) + came[: chips - 1].astype(F32)).astype(BF16)
    grad_input = kept[chips - 1].astype(F32) + came[chips - 1].astype(F32)
    for b in range(chips - 1):
        shift = [(m, (m + 2 * (b + 1)) % groups) for m in range(groups)]
        grad_input += lax.ppermute(pairs[b], "mp", shift).astype(F32)
    grad_input = grad_input.astype(BF16)

    if exchange:
        for k in range(2, parts // 2, 2):
            beside.append(along_dp(keys[k], lambda m: 1, parts, groups))
        turned = turned_inputs(mine, theirs, next_inputs, inputs_normed)
        beside[-1], grad_input = lax.optimization_barrier((beside[-1], grad_input))
        keys = [keys[k] for k in range(0, parts // 2, 2)] + beside
        grad_weights = summed_weights(turned, keys)
    else:
        grad_weights = gathered_weights(inputs_normed, grad_key, parts)
    return (grad_query, grad_input, grad_weights)


def solution(mesh):
    placed = (
        P("dp", "mp"),
        P("dp", "mp"),
        P("dp", "mp"),
        P("dp", "mp"),
        P("dp", None),
        P(None, None, "mp"),
    )
    return jax.shard_map(
        body,
        mesh=mesh,
        in_specs=placed,
        out_specs=(P("dp", "mp"), P("dp", "mp"), P("dp", "mp")),
        check_vma=False,
    )
```

```python
import math

import jax
import jax.numpy as jnp
from jax import lax
from jax.experimental import pallas as pl
from jax.experimental.pallas import tpu as pltpu
from jax.sharding import PartitionSpec as P

HEAD_SIZE = 128
F32 = jnp.float32
BF16 = jnp.bfloat16
NN = (((1,), (0,)), ((), ()))
NT = (((1,), (1,)), ((), ()))
TN = (((0,), (0,)), ((), ()))
IN_HBM = pl.BlockSpec(memory_space=pltpu.HBM)
ANYWHERE = pl.BlockSpec(memory_space=pl.ANY)
IN_VMEM = pl.BlockSpec(memory_space=pltpu.VMEM)
CHUNK = 512
PARAMS = pltpu.CompilerParams(vmem_limit_bytes=24 * 1024 * 1024)
WHOLE = pltpu.CompilerParams(vmem_limit_bytes=60 * 1024 * 1024)


def dot(a, b, dims=NN):
    return lax.dot_general(a, b, dims, preferred_element_type=F32)


def cost(flops, moved, transcendentals=0):
    return pl.CostEstimate(flops=flops, bytes_accessed=moved, transcendentals=transcendentals)


def attention_scores(g, q, k, v, do, scores, grad_probs):
    per_group = q.shape[1] // k.shape[1]
    cols = slice(g * HEAD_SIZE, (g + 1) * HEAD_SIZE)
    scores[g] = dot(k[:, cols], stacked(q, g, per_group), NT)
    grad_probs[g] = dot(v[:, cols], stacked(do, g, per_group), NT)


def stacked(array, g, per_group):
    first = g * per_group * HEAD_SIZE
    heads = [array[:, first + h * HEAD_SIZE : first + (h + 1) * HEAD_SIZE] for h in range(per_group)]
    return jnp.concatenate(heads, axis=0)


def attention_softmax(g, scores, grad_probs, probs_b, ds):
    length = scores.shape[1]
    group = scores.shape[2]
    scale = 1.0 / math.sqrt(HEAD_SIZE)
    targets = lax.broadcasted_iota(jnp.int32, (length, length), 0)
    positions = lax.broadcasted_iota(jnp.int32, (length, length), 1)
    allowed = targets <= positions
    for at in range(0, group, length):
        cols = slice(at, at + length)
        masked = jnp.where(allowed, scores[g, :, cols], -1e30)
        raw = jnp.exp((masked - jnp.max(masked, axis=0, keepdims=True)) * scale)
        probs = raw * (1.0 / jnp.sum(raw, axis=0, keepdims=True))
        slopes = grad_probs[g, :, cols]
        delta = jnp.sum(probs * slopes, axis=0, keepdims=True)
        probs_b[:, g * group + at : g * group + at + length] = probs.astype(BF16)
        ds[:, g * group + at : g * group + at + length] = (probs * (slopes - delta)).astype(BF16)


def attention_kernel(
    q_hbm, k_hbm, v_hbm, do_hbm, gk_ref, gv_ref, twice_ref, gq_hbm,
    q, k, v, do, probs_b, ds, gq, scores, grad_probs, sems, out_sems,
):
    length = q.shape[0]
    kv_heads = k.shape[1] // HEAD_SIZE
    group = q.shape[1] // kv_heads
    per_group = group // HEAD_SIZE
    small = [
        pltpu.make_async_copy(k_hbm, k, sems.at[0]),
        pltpu.make_async_copy(v_hbm, v, sems.at[1]),
    ]
    large, stored = [], []
    for g in range(kv_heads):
        cols = pl.ds(g * group, group)
        large.append((
            pltpu.make_async_copy(q_hbm.at[:, cols], q.at[:, cols], sems.at[2 + 2 * g]),
            pltpu.make_async_copy(do_hbm.at[:, cols], do.at[:, cols], sems.at[3 + 2 * g]),
        ))
        stored.append(pltpu.make_async_copy(gq.at[:, cols], gq_hbm.at[:, cols], out_sems.at[g]))
    for copy in small:
        copy.start()
    for pair in large:
        for copy in pair:
            copy.start()
    for copy in small:
        copy.wait()
    for g in range(kv_heads):
        for copy in large[g]:
            copy.wait()
        attention_scores(g, q, k, v, do, scores, grad_probs)
    scale = 1.0 / math.sqrt(HEAD_SIZE)
    for g in range(kv_heads):
        attention_softmax(g, scores, grad_probs, probs_b, ds)
        cols = slice(g * group, (g + 1) * group)
        head = slice(g * HEAD_SIZE, (g + 1) * HEAD_SIZE)
        grad_query = dot(ds[:, cols], k[:, head], TN) * scale
        for h in range(per_group):
            at = g * group + h * HEAD_SIZE
            gq[:, at : at + HEAD_SIZE] = grad_query[h * length : (h + 1) * length].astype(BF16)
        stored[g].start()
        grad_key = dot(ds[:, cols], stacked(q, g, per_group)) * scale
        gk_ref[:, head] = grad_key.astype(BF16)
        twice_ref[:length, head] = grad_key.astype(BF16)
        twice_ref[length:, head] = grad_key.astype(BF16)
        gv_ref[:, head] = dot(probs_b[:, cols], stacked(do, g, per_group)).astype(BF16)
    for copy in stored:
        copy.wait()


def partials_kernel(gk_ref, gv_ref, p_hbm, sent_hbm, kept_hbm, p, partial, p_sems, out_sems):
    groups, features = p.shape[0], p.shape[2]
    chips = groups // 2
    member = lax.axis_index("mp")
    chip, core = lax.div(member, 2), lax.rem(member, 2)
    blocks, stored = [], []
    for b in range(groups):
        column = core if b >= chips else 1 - core
        start = (2 * lax.rem(chip + b + 1, chips) + column) * features
        rows = pl.ds(pl.multiple_of(start, features), features)
        blocks.append(pltpu.make_async_copy(p_hbm.at[:, rows, :], p.at[b], p_sems.at[b]))
    for copy in blocks:
        copy.start()
    grads = jnp.concatenate([gk_ref[...], gv_ref[...]], axis=1)
    step = min(CHUNK, features)
    for b in range(groups):
        blocks[b].wait()
        for at in range(0, features, step):
            rows = slice(at, at + step)
            both = jnp.concatenate([p[b, 0, rows, :], p[b, 1, rows, :]], axis=1)
            partial[b, :, rows] = dot(grads, both, NT).astype(BF16)
        target = sent_hbm.at[b] if b < chips else kept_hbm.at[b - chips]
        stored.append(pltpu.make_async_copy(partial.at[b], target, out_sems.at[b]))
        stored[-1].start()
    for copy in stored:
        copy.wait()


def turned_kernel(*refs):
    *blocks, next_ref, x_hbm, out_ref, own, sem = refs
    rows, width = own.shape
    parts = out_ref.shape[1] // rows
    far = groups = parts // 2
    part, member = lax.axis_index("dp"), lax.axis_index("mp")
    cols = pl.ds(pl.multiple_of(part * width, width), width)
    copy = pltpu.make_async_copy(x_hbm.at[:, cols], own, sem)
    copy.start()

    def put(k, piece):
        place = far * lax.rem(k, 2) + 2 * lax.div(lax.rem(k, far), 2) + lax.div(k, far)
        out_ref[:, pl.ds(pl.multiple_of(place * rows, rows), rows)] = piece.T

    partners = [far + (member ^ j) for j in range(0, groups, 2)]
    partners += [k + lax.rem(member, 2) for k in range(2, far, 2)]
    for k, mine, theirs in zip(partners, blocks[: len(partners)], blocks[len(partners) :]):
        put(k, mine[...])
        put(k ^ 1, theirs[...])
    put(jnp.int32(1), next_ref[...])
    copy.wait()
    put(jnp.int32(0), own[...])


def weights_kernel(x_ref, *refs):
    *keys, out_hbm, out, sems = refs
    rows = keys[0].shape[0]
    half = x_ref.shape[0] // 2
    copies = []
    for h in range(2):
        part = slice(h * half, (h + 1) * half)
        total = dot(x_ref[part, :rows], keys[0][...])
        for j in range(1, len(keys)):
            total += dot(x_ref[part, j * rows : (j + 1) * rows], keys[j][...])
        out[part, :] = total * (1.0 / (2 * len(keys)))
        copies.append(pltpu.make_async_copy(out.at[part, :], out_hbm.at[part, :], sems.at[h]))
        copies[h].start()
    for copy in copies:
        copy.wait()


def along_dp(array, partner, parts, groups):
    pairs = [
        (i * groups + m, (i ^ partner(m)) * groups + m)
        for i in range(parts)
        for m in range(groups)
    ]
    return lax.ppermute(array, ("dp", "mp"), pairs)


def along_mp(array, bit, groups):
    return lax.ppermute(array, "mp", [(m, m ^ bit) for m in range(groups)])


def sent_inputs(inputs, parts, groups):
    far = parts // 2
    part, member = lax.axis_index("dp"), lax.axis_index("mp")
    rows, width = inputs.shape[0], inputs.shape[1] // parts

    def block(k):
        return lax.dynamic_slice(inputs, (0, (part ^ k) * width), (rows, width))

    distant = along_dp(block(far + member), lambda m: far + m, parts, groups)
    near = []
    for k in range(2, far, 2):
        sent = block(k + lax.rem(member, 2))
        near.append(along_dp(sent, lambda m, k=k: k + m % 2, parts, groups))
    return distant, near, along_dp(block(1), lambda m: 1, parts, groups)


def shared_inputs(piece, groups):
    pieces = [piece]
    bit = 2
    while bit < groups:
        pieces += [along_mp(piece, bit, groups) for piece in pieces]
        bit *= 2
    return pieces


def turned_inputs(mine, theirs, next_inputs, inputs):
    rows, width = next_inputs.shape
    blocks = [*mine, *theirs, next_inputs]
    return pl.pallas_call(
        turned_kernel,
        in_specs=[IN_VMEM] * len(blocks) + [IN_HBM],
        out_specs=IN_VMEM,
        out_shape=jax.ShapeDtypeStruct((width, inputs.shape[1] // width * rows), inputs.dtype),
        scratch_shapes=[pltpu.VMEM((rows, width), inputs.dtype), pltpu.SemaphoreType.DMA],
        compiler_params=PARAMS,
        cost_estimate=cost(0, 4 * inputs.size),
    )(*blocks, inputs)


def summed_weights(turned, keys):
    width, columns = turned.shape[0], keys[0].shape[1]
    return pl.pallas_call(
        weights_kernel,
        out_specs=ANYWHERE,
        out_shape=jax.ShapeDtypeStruct((width, columns), F32),
        scratch_shapes=[pltpu.VMEM((width, columns), F32), pltpu.SemaphoreType.DMA((2,))],
        compiler_params=PARAMS,
        cost_estimate=cost(
            2 * turned.size * columns, 2 * turned.size + 4 * width * columns
        ),
    )(turned, *keys)


def gathered_weights(inputs, grad_key, parts):
    rows = inputs.shape[0]
    width = inputs.shape[1] // parts
    blocks = inputs.reshape(rows, parts, width).transpose(1, 0, 2)
    mine = lax.all_to_all(blocks, "dp", split_axis=0, concat_axis=0, tiled=True)
    keys = lax.all_gather(grad_key, "dp", axis=0)
    return jnp.einsum("psd,psc->dc", mine, keys, preferred_element_type=F32) / parts


def body(query_states, key_states, value_states, grad_context, inputs_normed, projections):
    parts = lax.axis_size("dp")
    groups = lax.axis_size("mp")
    chips = groups // 2
    rows, width = key_states.shape
    query_width = query_states.shape[1]
    features = projections.shape[1] // groups
    kv_heads = width // HEAD_SIZE
    partial = jax.ShapeDtypeStruct((chips, rows, features), BF16)
    exchange = parts == 2 * groups and inputs_normed.shape[1] % (parts * 128) == 0
    if exchange:
        distant, near, next_inputs = sent_inputs(inputs_normed, parts, groups)

    whole = pltpu.VMEM((rows, query_width), BF16)
    narrow = pltpu.VMEM((rows, width), BF16)
    wide = pltpu.VMEM((kv_heads, rows, query_width // kv_heads), F32)
    grad_key, grad_value, twice, grad_query = pl.pallas_call(
        attention_kernel,
        in_specs=[IN_HBM] * 4,
        out_specs=[IN_VMEM, IN_VMEM, IN_VMEM, ANYWHERE],
        out_shape=(
            jax.ShapeDtypeStruct((rows, width), BF16),
            jax.ShapeDtypeStruct((rows, width), BF16),
            jax.ShapeDtypeStruct((2 * rows, width), BF16),
            jax.ShapeDtypeStruct((rows, query_width), BF16),
        ),
        scratch_shapes=[whole, narrow, narrow, whole, whole, whole, whole, wide, wide]
        + [pltpu.SemaphoreType.DMA((2 + 2 * kv_heads,)), pltpu.SemaphoreType.DMA((kv_heads,))],
        compiler_params=WHOLE,
        cost_estimate=cost(
            10 * rows * rows * query_width, 6 * rows * query_width, rows * query_width
        ),
    )(query_states, key_states, value_states, grad_context)

    sent, kept = pl.pallas_call(
        partials_kernel,
        in_specs=[IN_VMEM, IN_VMEM, IN_HBM],
        out_specs=[ANYWHERE, ANYWHERE],
        out_shape=(partial, partial),
        scratch_shapes=[
            pltpu.VMEM((groups, 2, features, width), BF16),
            pltpu.VMEM((groups, rows, features), BF16),
            pltpu.SemaphoreType.DMA((groups,)),
            pltpu.SemaphoreType.DMA((groups,)),
        ],
        compiler_params=WHOLE,
        cost_estimate=cost(
            4 * rows * width * features * groups, 4 * width * features * groups
        ),
    )(grad_key, grad_value, projections)

    if exchange:
        first = along_dp(grad_key, lambda m: parts // 2, parts, groups)
        _, distant = lax.optimization_barrier((grad_key, distant))
        pieces = shared_inputs(distant, groups)
        first, twice, sent, kept, pieces, near, next_inputs = lax.optimization_barrier(
            (first, twice, sent, kept, pieces, near, next_inputs)
        )
        keys = {0: lax.dynamic_update_slice(twice, first, (rows, 0))}
        bit = parts // 4
        while bit > 1:
            for k in list(keys):
                keys[k ^ bit] = along_dp(keys[k], lambda m, bit=bit: bit, parts, groups)
            bit //= 2
        beside = [along_dp(keys[0], lambda m: 1, parts, groups)]
        pieces[1:], _ = lax.optimization_barrier((pieces[1:], (beside, keys)))
        mine = pieces + near
        theirs = [along_mp(piece, 1, groups) for piece in mine]
    came = along_mp(sent, 1, groups)
    total = kept.astype(F32) + came.astype(F32)
    grad_input = total[chips - 1]
    for b in range(chips - 1):
        shift = [(m, (m + 2 * (b + 1)) % groups) for m in range(groups)]
        grad_input += lax.ppermute(total[b].astype(BF16), "mp", shift).astype(F32)
    grad_input = grad_input.astype(BF16)

    if exchange:
        for k in range(2, parts // 2, 2):
            beside.append(along_dp(keys[k], lambda m: 1, parts, groups))
        turned = turned_inputs(mine, theirs, next_inputs, inputs_normed)
        beside[-1], grad_input = lax.optimization_barrier((beside[-1], grad_input))
        keys = [keys[k] for k in range(0, parts // 2, 2)] + beside
        grad_weights = summed_weights(turned, keys)
    else:
        grad_weights = gathered_weights(inputs_normed, grad_key, parts)
    return (grad_query, grad_input, grad_weights)


def solution(mesh):
    placed = (
        P("dp", "mp"),
        P("dp", "mp"),
        P("dp", "mp"),
        P("dp", "mp"),
        P("dp", None),
        P(None, None, "mp"),
    )
    return jax.shard_map(
        body,
        mesh=mesh,
        in_specs=placed,
        out_specs=(P("dp", "mp"), P("dp", "mp"), P("dp", "mp")),
        check_vma=False,
    )
```

```python
import math

import jax
import jax.numpy as jnp
from jax import lax
from jax.experimental import pallas as pl
from jax.experimental.pallas import tpu as pltpu
from jax.sharding import PartitionSpec as P

HEAD_SIZE = 128
F32 = jnp.float32
BF16 = jnp.bfloat16
NN = (((1,), (0,)), ((), ()))
NT = (((1,), (1,)), ((), ()))
TN = (((0,), (0,)), ((), ()))
IN_HBM = pl.BlockSpec(memory_space=pltpu.HBM)
ANYWHERE = pl.BlockSpec(memory_space=pl.ANY)
IN_VMEM = pl.BlockSpec(memory_space=pltpu.VMEM)
CHUNK = 512
PARAMS = pltpu.CompilerParams(vmem_limit_bytes=24 * 1024 * 1024)
WHOLE = pltpu.CompilerParams(vmem_limit_bytes=60 * 1024 * 1024)


def dot(a, b, dims=NN):
    return lax.dot_general(a, b, dims, preferred_element_type=F32)


def cost(flops, moved, transcendentals=0):
    return pl.CostEstimate(flops=flops, bytes_accessed=moved, transcendentals=transcendentals)


def attention_scores(g, q, k, v, do, scores, grad_probs):
    per_group = q.shape[1] // k.shape[1]
    cols = slice(g * HEAD_SIZE, (g + 1) * HEAD_SIZE)
    scores[g] = dot(k[:, cols], stacked(q, g, per_group), NT)
    grad_probs[g] = dot(v[:, cols], stacked(do, g, per_group), NT)


def stacked(array, g, per_group):
    first = g * per_group * HEAD_SIZE
    heads = [array[:, first + h * HEAD_SIZE : first + (h + 1) * HEAD_SIZE] for h in range(per_group)]
    return jnp.concatenate(heads, axis=0)


def attention_softmax(g, scores, grad_probs, probs_b, ds):
    length = scores.shape[1]
    group = scores.shape[2]
    scale = 1.0 / math.sqrt(HEAD_SIZE)
    targets = lax.broadcasted_iota(jnp.int32, (length, length), 0)
    positions = lax.broadcasted_iota(jnp.int32, (length, length), 1)
    allowed = targets <= positions
    for at in range(0, group, length):
        cols = slice(at, at + length)
        masked = jnp.where(allowed, scores[g, :, cols], -1e30)
        raw = jnp.exp((masked - jnp.max(masked, axis=0, keepdims=True)) * scale)
        probs = raw * (1.0 / jnp.sum(raw, axis=0, keepdims=True))
        slopes = grad_probs[g, :, cols]
        delta = jnp.sum(probs * slopes, axis=0, keepdims=True)
        probs_b[:, g * group + at : g * group + at + length] = probs.astype(BF16)
        ds[:, g * group + at : g * group + at + length] = (probs * (slopes - delta)).astype(BF16)


def attention_kernel(
    q_hbm, k_hbm, v_hbm, do_hbm, gk_ref, gv_ref, twice_ref, gq_hbm,
    q, k, v, do, probs_b, ds, gq, scores, grad_probs, sems, out_sems,
):
    length = q.shape[0]
    kv_heads = k.shape[1] // HEAD_SIZE
    group = q.shape[1] // kv_heads
    per_group = group // HEAD_SIZE
    small = [
        pltpu.make_async_copy(k_hbm, k, sems.at[0]),
        pltpu.make_async_copy(v_hbm, v, sems.at[1]),
    ]
    large, stored = [], []
    for g in range(kv_heads):
        cols = pl.ds(g * group, group)
        large.append((
            pltpu.make_async_copy(q_hbm.at[:, cols], q.at[:, cols], sems.at[2 + 2 * g]),
            pltpu.make_async_copy(do_hbm.at[:, cols], do.at[:, cols], sems.at[3 + 2 * g]),
        ))
        stored.append(pltpu.make_async_copy(gq.at[:, cols], gq_hbm.at[:, cols], out_sems.at[g]))
    for copy in small:
        copy.start()
    for pair in large:
        for copy in pair:
            copy.start()
    for copy in small:
        copy.wait()
    for g in range(kv_heads):
        for copy in large[g]:
            copy.wait()
        attention_scores(g, q, k, v, do, scores, grad_probs)
    scale = 1.0 / math.sqrt(HEAD_SIZE)
    for g in range(kv_heads):
        attention_softmax(g, scores, grad_probs, probs_b, ds)
        cols = slice(g * group, (g + 1) * group)
        head = slice(g * HEAD_SIZE, (g + 1) * HEAD_SIZE)
        grad_query = dot(ds[:, cols], k[:, head], TN) * scale
        for h in range(per_group):
            at = g * group + h * HEAD_SIZE
            gq[:, at : at + HEAD_SIZE] = grad_query[h * length : (h + 1) * length].astype(BF16)
        stored[g].start()
        grad_key = dot(ds[:, cols], stacked(q, g, per_group)) * scale
        gk_ref[:, head] = grad_key.astype(BF16)
        twice_ref[:length, head] = grad_key.astype(BF16)
        twice_ref[length:, head] = grad_key.astype(BF16)
        gv_ref[:, head] = dot(probs_b[:, cols], stacked(do, g, per_group)).astype(BF16)
    for copy in stored:
        copy.wait()


def partials_kernel(gk_ref, gv_ref, p_hbm, sent_hbm, kept_hbm, p, partial, p_sems, out_sems):
    groups, features = p.shape[0], p.shape[2]
    chips = groups // 2
    member = lax.axis_index("mp")
    chip, core = lax.div(member, 2), lax.rem(member, 2)
    blocks, stored = [], []
    for b in range(groups):
        column = core if b >= chips else 1 - core
        start = (2 * lax.rem(chip + b + 1, chips) + column) * features
        rows = pl.ds(pl.multiple_of(start, features), features)
        blocks.append(pltpu.make_async_copy(p_hbm.at[:, rows, :], p.at[b], p_sems.at[b]))
    for copy in blocks:
        copy.start()
    grads = jnp.concatenate([gk_ref[...], gv_ref[...]], axis=1)
    step = min(CHUNK, features)
    for b in range(groups):
        blocks[b].wait()
        for at in range(0, features, step):
            rows = slice(at, at + step)
            both = jnp.concatenate([p[b, 0, rows, :], p[b, 1, rows, :]], axis=1)
            partial[b, :, rows] = dot(grads, both, NT).astype(BF16)
        target = sent_hbm.at[b] if b < chips else kept_hbm.at[b - chips]
        stored.append(pltpu.make_async_copy(partial.at[b], target, out_sems.at[b]))
        stored[-1].start()
    for copy in stored:
        copy.wait()


def turned_kernel(*refs):
    *blocks, next_ref, x_hbm, out_ref, own, sem = refs
    rows, width = own.shape
    parts = out_ref.shape[1] // rows
    far = groups = parts // 2
    part, member = lax.axis_index("dp"), lax.axis_index("mp")
    cols = pl.ds(pl.multiple_of(part * width, width), width)
    copy = pltpu.make_async_copy(x_hbm.at[:, cols], own, sem)
    copy.start()

    def put(k, piece):
        place = far * lax.rem(k, 2) + 2 * lax.div(lax.rem(k, far), 2) + lax.div(k, far)
        out_ref[:, pl.ds(pl.multiple_of(place * rows, rows), rows)] = piece.T

    partners = [far + (member ^ j) for j in range(0, groups, 2)]
    partners += [k + lax.rem(member, 2) for k in range(2, far, 2)]
    for k, mine, theirs in zip(partners, blocks[: len(partners)], blocks[len(partners) :]):
        put(k, mine[...])
        put(k ^ 1, theirs[...])
    put(jnp.int32(1), next_ref[...])
    copy.wait()
    put(jnp.int32(0), own[...])


def weights_kernel(x_ref, *refs):
    *keys, out_hbm, out, sems = refs
    rows = keys[0].shape[0]
    half = x_ref.shape[0] // 2
    copies = []
    for h in range(2):
        part = slice(h * half, (h + 1) * half)
        total = dot(x_ref[part, :rows], keys[0][...])
        for j in range(1, len(keys)):
            total += dot(x_ref[part, j * rows : (j + 1) * rows], keys[j][...])
        out[part, :] = total * (1.0 / (2 * len(keys)))
        copies.append(pltpu.make_async_copy(out.at[part, :], out_hbm.at[part, :], sems.at[h]))
        copies[h].start()
    for copy in copies:
        copy.wait()


def along_dp(array, partner, parts, groups):
    pairs = [
        (i * groups + m, (i ^ partner(m)) * groups + m)
        for i in range(parts)
        for m in range(groups)
    ]
    return lax.ppermute(array, ("dp", "mp"), pairs)


def along_mp(array, bit, groups):
    return lax.ppermute(array, "mp", [(m, m ^ bit) for m in range(groups)])


def sent_inputs(inputs, parts, groups):
    far = parts // 2
    part, member = lax.axis_index("dp"), lax.axis_index("mp")
    rows, width = inputs.shape[0], inputs.shape[1] // parts

    def block(k):
        return lax.dynamic_slice(inputs, (0, (part ^ k) * width), (rows, width))

    distant = along_dp(block(far + member), lambda m: far + m, parts, groups)
    near = []
    for k in range(2, far, 2):
        sent = block(k + lax.rem(member, 2))
        near.append(along_dp(sent, lambda m, k=k: k + m % 2, parts, groups))
    return distant, near, along_dp(block(1), lambda m: 1, parts, groups)


def shared_inputs(piece, groups):
    pieces = [piece]
    bit = 2
    while bit < groups:
        pieces += [along_mp(piece, bit, groups) for piece in pieces]
        bit *= 2
    return pieces


def turned_inputs(mine, theirs, next_inputs, inputs):
    rows, width = next_inputs.shape
    blocks = [*mine, *theirs, next_inputs]
    return pl.pallas_call(
        turned_kernel,
        in_specs=[IN_VMEM] * len(blocks) + [IN_HBM],
        out_specs=IN_VMEM,
        out_shape=jax.ShapeDtypeStruct((width, inputs.shape[1] // width * rows), inputs.dtype),
        scratch_shapes=[pltpu.VMEM((rows, width), inputs.dtype), pltpu.SemaphoreType.DMA],
        compiler_params=PARAMS,
        cost_estimate=cost(0, 4 * inputs.size),
    )(*blocks, inputs)


def summed_weights(turned, keys):
    width, columns = turned.shape[0], keys[0].shape[1]
    return pl.pallas_call(
        weights_kernel,
        out_specs=ANYWHERE,
        out_shape=jax.ShapeDtypeStruct((width, columns), F32),
        scratch_shapes=[pltpu.VMEM((width, columns), F32), pltpu.SemaphoreType.DMA((2,))],
        compiler_params=PARAMS,
        cost_estimate=cost(
            2 * turned.size * columns, 2 * turned.size + 4 * width * columns
        ),
    )(turned, *keys)


def gathered_weights(inputs, grad_key, parts):
    rows = inputs.shape[0]
    width = inputs.shape[1] // parts
    blocks = inputs.reshape(rows, parts, width).transpose(1, 0, 2)
    mine = lax.all_to_all(blocks, "dp", split_axis=0, concat_axis=0, tiled=True)
    keys = lax.all_gather(grad_key, "dp", axis=0)
    return jnp.einsum("psd,psc->dc", mine, keys, preferred_element_type=F32) / parts


def body(query_states, key_states, value_states, grad_context, inputs_normed, projections):
    parts = lax.axis_size("dp")
    groups = lax.axis_size("mp")
    chips = groups // 2
    rows, width = key_states.shape
    query_width = query_states.shape[1]
    features = projections.shape[1] // groups
    kv_heads = width // HEAD_SIZE
    partial = jax.ShapeDtypeStruct((chips, rows, features), BF16)
    exchange = parts == 2 * groups and inputs_normed.shape[1] % (parts * 128) == 0
    if exchange:
        distant, near, next_inputs = sent_inputs(inputs_normed, parts, groups)

    whole = pltpu.VMEM((rows, query_width), BF16)
    narrow = pltpu.VMEM((rows, width), BF16)
    wide = pltpu.VMEM((kv_heads, rows, query_width // kv_heads), F32)
    grad_key, grad_value, twice, grad_query = pl.pallas_call(
        attention_kernel,
        in_specs=[IN_HBM] * 4,
        out_specs=[IN_VMEM, IN_VMEM, IN_VMEM, ANYWHERE],
        out_shape=(
            jax.ShapeDtypeStruct((rows, width), BF16),
            jax.ShapeDtypeStruct((rows, width), BF16),
            jax.ShapeDtypeStruct((2 * rows, width), BF16),
            jax.ShapeDtypeStruct((rows, query_width), BF16),
        ),
        scratch_shapes=[whole, narrow, narrow, whole, whole, whole, whole, wide, wide]
        + [pltpu.SemaphoreType.DMA((2 + 2 * kv_heads,)), pltpu.SemaphoreType.DMA((kv_heads,))],
        compiler_params=WHOLE,
        cost_estimate=cost(
            10 * rows * rows * query_width, 6 * rows * query_width, rows * query_width
        ),
    )(query_states, key_states, value_states, grad_context)

    sent, kept = pl.pallas_call(
        partials_kernel,
        in_specs=[IN_VMEM, IN_VMEM, IN_HBM],
        out_specs=[ANYWHERE, ANYWHERE],
        out_shape=(partial, partial),
        scratch_shapes=[
            pltpu.VMEM((groups, 2, features, width), BF16),
            pltpu.VMEM((groups, rows, features), BF16),
            pltpu.SemaphoreType.DMA((groups,)),
            pltpu.SemaphoreType.DMA((groups,)),
        ],
        compiler_params=WHOLE,
        cost_estimate=cost(
            4 * rows * width * features * groups, 4 * width * features * groups
        ),
    )(grad_key, grad_value, projections)

    if exchange:
        first = along_dp(grad_key, lambda m: parts // 2, parts, groups)
        first, twice, sent, kept, distant, near, next_inputs = lax.optimization_barrier(
            (first, twice, sent, kept, distant, near, next_inputs)
        )
        pieces = shared_inputs(distant, groups)
        keys = {0: lax.dynamic_update_slice(twice, first, (rows, 0))}
        bit = parts // 4
        while bit > 1:
            for k in list(keys):
                keys[k ^ bit] = along_dp(keys[k], lambda m, bit=bit: bit, parts, groups)
            bit //= 2
        beside = [along_dp(keys[0], lambda m: 1, parts, groups)]
        pieces[1:], _ = lax.optimization_barrier((pieces[1:], (beside, keys)))
        mine = pieces + near
        theirs = [along_mp(piece, 1, groups) for piece in mine]
    came = along_mp(sent, 1, groups)
    total = kept.astype(F32) + came.astype(F32)
    grad_input = total[chips - 1]
    for b in range(chips - 1):
        shift = [(m, (m + 2 * (b + 1)) % groups) for m in range(groups)]
        grad_input += lax.ppermute(total[b].astype(BF16), "mp", shift).astype(F32)
    grad_input = grad_input.astype(BF16)

    if exchange:
        for k in range(2, parts // 2, 2):
            beside.append(along_dp(keys[k], lambda m: 1, parts, groups))
        turned = turned_inputs(mine, theirs, next_inputs, inputs_normed)
        beside[-1], grad_input = lax.optimization_barrier((beside[-1], grad_input))
        keys = [keys[k] for k in range(0, parts // 2, 2)] + beside
        grad_weights = summed_weights(turned, keys)
    else:
        grad_weights = gathered_weights(inputs_normed, grad_key, parts)
    return (grad_query, grad_input, grad_weights)


def solution(mesh):
    placed = (
        P("dp", "mp"),
        P("dp", "mp"),
        P("dp", "mp"),
        P("dp", "mp"),
        P("dp", None),
        P(None, None, "mp"),
    )
    return jax.shard_map(
        body,
        mesh=mesh,
        in_specs=placed,
        out_specs=(P("dp", "mp"), P("dp", "mp"), P("dp", "mp")),
        check_vma=False,
    )
```

```python
import math

import jax
import jax.numpy as jnp
from jax import lax
from jax.experimental import pallas as pl
from jax.experimental.pallas import tpu as pltpu
from jax.sharding import PartitionSpec as P

HEAD_SIZE = 128
F32 = jnp.float32
BF16 = jnp.bfloat16
NN = (((1,), (0,)), ((), ()))
NT = (((1,), (1,)), ((), ()))
TN = (((0,), (0,)), ((), ()))
IN_HBM = pl.BlockSpec(memory_space=pltpu.HBM)
ANYWHERE = pl.BlockSpec(memory_space=pl.ANY)
IN_VMEM = pl.BlockSpec(memory_space=pltpu.VMEM)
CHUNK = 512
PARAMS = pltpu.CompilerParams(vmem_limit_bytes=24 * 1024 * 1024)
WHOLE = pltpu.CompilerParams(vmem_limit_bytes=60 * 1024 * 1024)


def dot(a, b, dims=NN):
    return lax.dot_general(a, b, dims, preferred_element_type=F32)


def cost(flops, moved, transcendentals=0):
    return pl.CostEstimate(flops=flops, bytes_accessed=moved, transcendentals=transcendentals)


def attention_scores(g, q, k, v, do, scores, grad_probs):
    per_group = q.shape[1] // k.shape[1]
    cols = slice(g * HEAD_SIZE, (g + 1) * HEAD_SIZE)
    scores[g] = dot(k[:, cols], stacked(q, g, per_group), NT)
    grad_probs[g] = dot(v[:, cols], stacked(do, g, per_group), NT)


def stacked(array, g, per_group):
    first = g * per_group * HEAD_SIZE
    heads = [array[:, first + h * HEAD_SIZE : first + (h + 1) * HEAD_SIZE] for h in range(per_group)]
    return jnp.concatenate(heads, axis=0)


def attention_softmax(g, scores, grad_probs, probs_b, ds):
    length = scores.shape[1]
    group = scores.shape[2]
    scale = 1.0 / math.sqrt(HEAD_SIZE)
    targets = lax.broadcasted_iota(jnp.int32, (length, length), 0)
    positions = lax.broadcasted_iota(jnp.int32, (length, length), 1)
    allowed = targets <= positions
    for at in range(0, group, length):
        cols = slice(at, at + length)
        masked = jnp.where(allowed, scores[g, :, cols], -1e30)
        raw = jnp.exp((masked - jnp.max(masked, axis=0, keepdims=True)) * scale)
        probs = raw * (1.0 / jnp.sum(raw, axis=0, keepdims=True))
        slopes = grad_probs[g, :, cols]
        delta = jnp.sum(probs * slopes, axis=0, keepdims=True)
        probs_b[:, g * group + at : g * group + at + length] = probs.astype(BF16)
        ds[:, g * group + at : g * group + at + length] = (probs * (slopes - delta)).astype(BF16)


def attention_kernel(
    q_hbm, k_hbm, v_hbm, do_hbm, gk_ref, gv_ref, twice_ref, gq_hbm,
    q, k, v, do, probs_b, ds, gq, scores, grad_probs, sems, out_sems,
):
    length = q.shape[0]
    kv_heads = k.shape[1] // HEAD_SIZE
    group = q.shape[1] // kv_heads
    per_group = group // HEAD_SIZE
    small = [
        pltpu.make_async_copy(k_hbm, k, sems.at[0]),
        pltpu.make_async_copy(v_hbm, v, sems.at[1]),
    ]
    large, stored = [], []
    for g in range(kv_heads):
        cols = pl.ds(g * group, group)
        large.append((
            pltpu.make_async_copy(q_hbm.at[:, cols], q.at[:, cols], sems.at[2 + 2 * g]),
            pltpu.make_async_copy(do_hbm.at[:, cols], do.at[:, cols], sems.at[3 + 2 * g]),
        ))
        stored.append(pltpu.make_async_copy(gq.at[:, cols], gq_hbm.at[:, cols], out_sems.at[g]))
    for copy in small:
        copy.start()
    for pair in large:
        for copy in pair:
            copy.start()
    for copy in small:
        copy.wait()
    for g in range(kv_heads):
        for copy in large[g]:
            copy.wait()
        attention_scores(g, q, k, v, do, scores, grad_probs)
    scale = 1.0 / math.sqrt(HEAD_SIZE)
    for g in range(kv_heads):
        attention_softmax(g, scores, grad_probs, probs_b, ds)
        cols = slice(g * group, (g + 1) * group)
        head = slice(g * HEAD_SIZE, (g + 1) * HEAD_SIZE)
        grad_query = dot(ds[:, cols], k[:, head], TN) * scale
        for h in range(per_group):
            at = g * group + h * HEAD_SIZE
            gq[:, at : at + HEAD_SIZE] = grad_query[h * length : (h + 1) * length].astype(BF16)
        stored[g].start()
        grad_key = dot(ds[:, cols], stacked(q, g, per_group)) * scale
        gk_ref[:, head] = grad_key.astype(BF16)
        twice_ref[:length, head] = grad_key.astype(BF16)
        twice_ref[length:, head] = grad_key.astype(BF16)
        gv_ref[:, head] = dot(probs_b[:, cols], stacked(do, g, per_group)).astype(BF16)
    for copy in stored:
        copy.wait()


def partials_kernel(gk_ref, gv_ref, p_hbm, sent_hbm, kept_hbm, p, partial, p_sems, out_sems):
    groups, features = p.shape[0], p.shape[2]
    chips = groups // 2
    member = lax.axis_index("mp")
    chip, core = lax.div(member, 2), lax.rem(member, 2)
    blocks, stored = [], []
    for b in range(groups):
        column = core if b >= chips else 1 - core
        start = (2 * lax.rem(chip + b + 1, chips) + column) * features
        rows = pl.ds(pl.multiple_of(start, features), features)
        blocks.append(pltpu.make_async_copy(p_hbm.at[:, rows, :], p.at[b], p_sems.at[b]))
    for copy in blocks:
        copy.start()
    grads = jnp.concatenate([gk_ref[...], gv_ref[...]], axis=1)
    step = min(CHUNK, features)
    for b in range(groups):
        blocks[b].wait()
        for at in range(0, features, step):
            rows = slice(at, at + step)
            both = jnp.concatenate([p[b, 0, rows, :], p[b, 1, rows, :]], axis=1)
            partial[b, :, rows] = dot(grads, both, NT).astype(BF16)
        target = sent_hbm.at[b] if b < chips else kept_hbm.at[b - chips]
        stored.append(pltpu.make_async_copy(partial.at[b], target, out_sems.at[b]))
        stored[-1].start()
    for copy in stored:
        copy.wait()


def turned_kernel(*refs):
    *blocks, beside_ref, x_hbm, out_ref, own, sem = refs
    rows, width = own.shape
    parts = out_ref.shape[1] // rows
    far = groups = parts // 2
    part, member = lax.axis_index("dp"), lax.axis_index("mp")
    cols = pl.ds(pl.multiple_of(part * width, width), width)
    copy = pltpu.make_async_copy(x_hbm.at[:, cols], own, sem)
    copy.start()

    def put(k, piece, at=0):
        place = far * lax.rem(k, 2) + 2 * lax.div(lax.rem(k, far), 2) + lax.div(k, far)
        tokens = pl.ds(pl.multiple_of(place * rows, rows), rows)
        out_ref[at : at + piece.shape[1], tokens] = piece.T

    partners = [far + (member ^ j) for j in range(0, groups, 2)]
    partners += [k + lax.rem(member, 2) for k in range(2, far, 2)]
    for k, mine, theirs in zip(partners, blocks[: len(partners)], blocks[len(partners) :]):
        put(k, mine[...])
        put(k ^ 1, theirs[...])
    chunk = beside_ref.shape[1]
    for e in range(width // chunk):
        put(jnp.int32(1), beside_ref[(2 + e) * rows : (3 + e) * rows, :], e * chunk)
    copy.wait()
    put(jnp.int32(0), own[...])


def weights_kernel(x_ref, *refs):
    *keys, out_hbm, out, sems = refs
    rows = x_ref.shape[1] // len(keys)
    half = x_ref.shape[0] // 2
    copies = []
    for h in range(2):
        part = slice(h * half, (h + 1) * half)
        total = dot(x_ref[part, :rows], keys[0][:rows, :])
        for j in range(1, len(keys)):
            total += dot(x_ref[part, j * rows : (j + 1) * rows], keys[j][:rows, :])
        out[part, :] = total * (1.0 / (2 * len(keys)))
        copies.append(pltpu.make_async_copy(out.at[part, :], out_hbm.at[part, :], sems.at[h]))
        copies[h].start()
    for copy in copies:
        copy.wait()


def along_dp(array, partner, parts, groups):
    pairs = [
        (i * groups + m, (i ^ partner(m)) * groups + m)
        for i in range(parts)
        for m in range(groups)
    ]
    return lax.ppermute(array, ("dp", "mp"), pairs)


def along_mp(array, bit, groups):
    return lax.ppermute(array, "mp", [(m, m ^ bit) for m in range(groups)])


def sent_inputs(inputs, parts, groups):
    far = parts // 2
    part, member = lax.axis_index("dp"), lax.axis_index("mp")
    rows, width = inputs.shape[0], inputs.shape[1] // parts

    def block(k):
        return lax.dynamic_slice(inputs, (0, (part ^ k) * width), (rows, width))

    distant = along_dp(block(far + member), lambda m: far + m, parts, groups)
    near = []
    for k in range(2, far, 2):
        sent = block(k + lax.rem(member, 2))
        near.append(along_dp(sent, lambda m, k=k: k + m % 2, parts, groups))
    return distant, near, block(1)


def shared_inputs(piece, groups):
    pieces = [piece]
    bit = 2
    while bit < groups:
        pieces += [along_mp(piece, bit, groups) for piece in pieces]
        bit *= 2
    return pieces


def turned_inputs(mine, theirs, beside, inputs, parts):
    rows, width = inputs.shape[0], inputs.shape[1] // parts
    blocks = [*mine, *theirs, beside]
    return pl.pallas_call(
        turned_kernel,
        in_specs=[IN_VMEM] * len(blocks) + [IN_HBM],
        out_specs=IN_VMEM,
        out_shape=jax.ShapeDtypeStruct((width, parts * rows), inputs.dtype),
        scratch_shapes=[pltpu.VMEM((rows, width), inputs.dtype), pltpu.SemaphoreType.DMA],
        compiler_params=PARAMS,
        cost_estimate=cost(0, 4 * inputs.size),
    )(*blocks, inputs)


def summed_weights(turned, keys):
    width, columns = turned.shape[0], keys[0].shape[1]
    return pl.pallas_call(
        weights_kernel,
        out_specs=ANYWHERE,
        out_shape=jax.ShapeDtypeStruct((width, columns), F32),
        scratch_shapes=[pltpu.VMEM((width, columns), F32), pltpu.SemaphoreType.DMA((2,))],
        compiler_params=PARAMS,
        cost_estimate=cost(
            2 * turned.size * columns, 2 * turned.size + 4 * width * columns
        ),
    )(turned, *keys)


def gathered_weights(inputs, grad_key, parts):
    rows = inputs.shape[0]
    width = inputs.shape[1] // parts
    blocks = inputs.reshape(rows, parts, width).transpose(1, 0, 2)
    mine = lax.all_to_all(blocks, "dp", split_axis=0, concat_axis=0, tiled=True)
    keys = lax.all_gather(grad_key, "dp", axis=0)
    return jnp.einsum("psd,psc->dc", mine, keys, preferred_element_type=F32) / parts


def body(query_states, key_states, value_states, grad_context, inputs_normed, projections):
    parts = lax.axis_size("dp")
    groups = lax.axis_size("mp")
    chips = groups // 2
    rows, width = key_states.shape
    query_width = query_states.shape[1]
    features = projections.shape[1] // groups
    kv_heads = width // HEAD_SIZE
    partial = jax.ShapeDtypeStruct((chips, rows, features), BF16)
    exchange = parts == 2 * groups and inputs_normed.shape[1] % (parts * width) == 0
    if exchange:
        distant, near, next_block = sent_inputs(inputs_normed, parts, groups)

    whole = pltpu.VMEM((rows, query_width), BF16)
    narrow = pltpu.VMEM((rows, width), BF16)
    wide = pltpu.VMEM((kv_heads, rows, query_width // kv_heads), F32)
    grad_key, grad_value, twice, grad_query = pl.pallas_call(
        attention_kernel,
        in_specs=[IN_HBM] * 4,
        out_specs=[IN_VMEM, IN_VMEM, IN_VMEM, ANYWHERE],
        out_shape=(
            jax.ShapeDtypeStruct((rows, width), BF16),
            jax.ShapeDtypeStruct((rows, width), BF16),
            jax.ShapeDtypeStruct((2 * rows, width), BF16),
            jax.ShapeDtypeStruct((rows, query_width), BF16),
        ),
        scratch_shapes=[whole, narrow, narrow, whole, whole, whole, whole, wide, wide]
        + [pltpu.SemaphoreType.DMA((2 + 2 * kv_heads,)), pltpu.SemaphoreType.DMA((kv_heads,))],
        compiler_params=WHOLE,
        cost_estimate=cost(
            10 * rows * rows * query_width, 6 * rows * query_width, rows * query_width
        ),
    )(query_states, key_states, value_states, grad_context)

    sent, kept = pl.pallas_call(
        partials_kernel,
        in_specs=[IN_VMEM, IN_VMEM, IN_HBM],
        out_specs=[ANYWHERE, ANYWHERE],
        out_shape=(partial, partial),
        scratch_shapes=[
            pltpu.VMEM((groups, 2, features, width), BF16),
            pltpu.VMEM((groups, rows, features), BF16),
            pltpu.SemaphoreType.DMA((groups,)),
            pltpu.SemaphoreType.DMA((groups,)),
        ],
        compiler_params=WHOLE,
        cost_estimate=cost(
            4 * rows * width * features * groups, 4 * width * features * groups
        ),
    )(grad_key, grad_value, projections)

    if exchange:
        first = along_dp(grad_key, lambda m: parts // 2, parts, groups)
        first, twice, sent, kept, distant, near = lax.optimization_barrier(
            (first, twice, sent, kept, distant, near)
        )
        pieces = shared_inputs(distant, groups)
        keys = {0: lax.dynamic_update_slice(twice, first, (rows, 0))}
        bit = parts // 4
        while bit > 1:
            for k in list(keys):
                keys[k ^ bit] = along_dp(keys[k], lambda m, bit=bit: bit, parts, groups)
            bit //= 2
        chunks = [next_block[:, at : at + width] for at in range(0, next_block.shape[1], width)]
        beside = [along_dp(jnp.concatenate([keys[0], *chunks]), lambda m: 1, parts, groups)]
        pieces[1:], _ = lax.optimization_barrier((pieces[1:], keys))
        mine = pieces + near
        theirs = [along_mp(piece, 1, groups) for piece in mine]
    came = along_mp(sent, 1, groups)
    total = kept.astype(F32) + came.astype(F32)
    grad_input = total[chips - 1]
    for b in range(chips - 1):
        shift = [(m, (m + 2 * (b + 1)) % groups) for m in range(groups)]
        grad_input += lax.ppermute(total[b].astype(BF16), "mp", shift).astype(F32)
    grad_input = grad_input.astype(BF16)

    if exchange:
        for k in range(2, parts // 2, 2):
            beside.append(along_dp(keys[k], lambda m: 1, parts, groups))
        turned = turned_inputs(mine, theirs, beside[0], inputs_normed, parts)
        beside[-1], grad_input = lax.optimization_barrier((beside[-1], grad_input))
        keys = [keys[k] for k in range(0, parts // 2, 2)] + beside
        grad_weights = summed_weights(turned, keys)
    else:
        grad_weights = gathered_weights(inputs_normed, grad_key, parts)
    return (grad_query, grad_input, grad_weights)


def solution(mesh):
    placed = (
        P("dp", "mp"),
        P("dp", "mp"),
        P("dp", "mp"),
        P("dp", "mp"),
        P("dp", None),
        P(None, None, "mp"),
    )
    return jax.shard_map(
        body,
        mesh=mesh,
        in_specs=placed,
        out_specs=(P("dp", "mp"), P("dp", "mp"), P("dp", "mp")),
        check_vma=False,
    )
```

```python
import functools
import math

import jax
import jax.numpy as jnp
from jax import lax
from jax.experimental import pallas as pl
from jax.experimental.pallas import tpu as pltpu
from jax.sharding import PartitionSpec as P

HEAD_SIZE = 128
F32 = jnp.float32
BF16 = jnp.bfloat16
NN = (((1,), (0,)), ((), ()))
NT = (((1,), (1,)), ((), ()))
TN = (((0,), (0,)), ((), ()))
IN_HBM = pl.BlockSpec(memory_space=pltpu.HBM)
ANYWHERE = pl.BlockSpec(memory_space=pl.ANY)
IN_VMEM = pl.BlockSpec(memory_space=pltpu.VMEM)
CHUNK = 512
PARAMS = pltpu.CompilerParams(vmem_limit_bytes=24 * 1024 * 1024)
WHOLE = pltpu.CompilerParams(vmem_limit_bytes=60 * 1024 * 1024)


def dot(a, b, dims=NN):
    return lax.dot_general(a, b, dims, preferred_element_type=F32)


def cost(flops, moved, transcendentals=0):
    return pl.CostEstimate(flops=flops, bytes_accessed=moved, transcendentals=transcendentals)


def attention_scores(g, q, k, v, do, scores, grad_probs):
    per_group = q.shape[1] // k.shape[1]
    cols = slice(g * HEAD_SIZE, (g + 1) * HEAD_SIZE)
    scores[g] = dot(k[:, cols], stacked(q, g, per_group), NT)
    grad_probs[g] = dot(v[:, cols], stacked(do, g, per_group), NT)


def stacked(array, g, per_group):
    first = g * per_group * HEAD_SIZE
    heads = [array[:, first + h * HEAD_SIZE : first + (h + 1) * HEAD_SIZE] for h in range(per_group)]
    return jnp.concatenate(heads, axis=0)


def attention_softmax(g, scores, grad_probs, probs_b, ds):
    length = scores.shape[1]
    group = scores.shape[2]
    scale = 1.0 / math.sqrt(HEAD_SIZE)
    targets = lax.broadcasted_iota(jnp.int32, (length, length), 0)
    positions = lax.broadcasted_iota(jnp.int32, (length, length), 1)
    allowed = targets <= positions
    for at in range(0, group, length):
        cols = slice(at, at + length)
        masked = jnp.where(allowed, scores[g, :, cols], -1e30)
        raw = jnp.exp((masked - jnp.max(masked, axis=0, keepdims=True)) * scale)
        probs = raw * (1.0 / jnp.sum(raw, axis=0, keepdims=True))
        slopes = grad_probs[g, :, cols]
        delta = jnp.sum(probs * slopes, axis=0, keepdims=True)
        probs_b[:, g * group + at : g * group + at + length] = probs.astype(BF16)
        ds[:, g * group + at : g * group + at + length] = (probs * (slopes - delta)).astype(BF16)


def attention_kernel(
    q_hbm, k_hbm, v_hbm, do_hbm, gk_ref, gv_ref, twice_ref, gq_hbm,
    q, k, v, do, probs_b, ds, gq, scores, grad_probs, sems, out_sems,
):
    length = q.shape[0]
    kv_heads = k.shape[1] // HEAD_SIZE
    group = q.shape[1] // kv_heads
    per_group = group // HEAD_SIZE
    small = [
        pltpu.make_async_copy(k_hbm, k, sems.at[0]),
        pltpu.make_async_copy(v_hbm, v, sems.at[1]),
    ]
    large, stored = [], []
    for g in range(kv_heads):
        cols = pl.ds(g * group, group)
        large.append((
            pltpu.make_async_copy(q_hbm.at[:, cols], q.at[:, cols], sems.at[2 + 2 * g]),
            pltpu.make_async_copy(do_hbm.at[:, cols], do.at[:, cols], sems.at[3 + 2 * g]),
        ))
        stored.append(pltpu.make_async_copy(gq.at[:, cols], gq_hbm.at[:, cols], out_sems.at[g]))
    for copy in small:
        copy.start()
    for pair in large:
        for copy in pair:
            copy.start()
    for copy in small:
        copy.wait()
    for g in range(kv_heads):
        for copy in large[g]:
            copy.wait()
        attention_scores(g, q, k, v, do, scores, grad_probs)
    scale = 1.0 / math.sqrt(HEAD_SIZE)
    for g in range(kv_heads):
        attention_softmax(g, scores, grad_probs, probs_b, ds)
        cols = slice(g * group, (g + 1) * group)
        head = slice(g * HEAD_SIZE, (g + 1) * HEAD_SIZE)
        grad_query = dot(ds[:, cols], k[:, head], TN) * scale
        for h in range(per_group):
            at = g * group + h * HEAD_SIZE
            gq[:, at : at + HEAD_SIZE] = grad_query[h * length : (h + 1) * length].astype(BF16)
        stored[g].start()
        grad_key = dot(ds[:, cols], stacked(q, g, per_group)) * scale
        gk_ref[:, head] = grad_key.astype(BF16)
        twice_ref[:length, head] = grad_key.astype(BF16)
        twice_ref[length:, head] = grad_key.astype(BF16)
        gv_ref[:, head] = dot(probs_b[:, cols], stacked(do, g, per_group)).astype(BF16)
    for copy in stored:
        copy.wait()


def partials_kernel(gk_ref, gv_ref, p_hbm, sent_hbm, kept_hbm, p, partial, p_sems, out_sems):
    groups, features = p.shape[0], p.shape[2]
    chips = groups // 2
    member = lax.axis_index("mp")
    chip, core = lax.div(member, 2), lax.rem(member, 2)
    blocks, stored = [], []
    for b in range(groups):
        column = core if b >= chips else 1 - core
        start = (2 * lax.rem(chip + b + 1, chips) + column) * features
        rows = pl.ds(pl.multiple_of(start, features), features)
        blocks.append(pltpu.make_async_copy(p_hbm.at[:, rows, :], p.at[b], p_sems.at[b]))
    for copy in blocks:
        copy.start()
    grads = jnp.concatenate([gk_ref[...], gv_ref[...]], axis=1)
    step = min(CHUNK, features)
    for b in range(groups):
        blocks[b].wait()
        for at in range(0, features, step):
            rows = slice(at, at + step)
            both = jnp.concatenate([p[b, 0, rows, :], p[b, 1, rows, :]], axis=1)
            partial[b, :, rows] = dot(grads, both, NT).astype(BF16)
        target = sent_hbm.at[b] if b < chips else kept_hbm.at[b - chips]
        stored.append(pltpu.make_async_copy(partial.at[b], target, out_sems.at[b]))
        stored[-1].start()
    for copy in stored:
        copy.wait()


def turned_kernel(*refs):
    *blocks, beside_ref, x_hbm, out_ref, own, sem = refs
    rows, width = own.shape
    parts = out_ref.shape[1] // rows
    far = groups = parts // 2
    part, member = lax.axis_index("dp"), lax.axis_index("mp")
    cols = pl.ds(pl.multiple_of(part * width, width), width)
    copy = pltpu.make_async_copy(x_hbm.at[:, cols], own, sem)
    copy.start()

    def put(k, piece, at=0):
        place = far * lax.rem(k, 2) + 2 * lax.div(lax.rem(k, far), 2) + lax.div(k, far)
        tokens = pl.ds(pl.multiple_of(place * rows, rows), rows)
        out_ref[at : at + piece.shape[1], tokens] = piece.T

    partners = [far + (member ^ j) for j in range(0, groups, 2)]
    partners += [k + lax.rem(member, 2) for k in range(2, far, 2)]
    for k, mine, theirs in zip(partners, blocks[: len(partners)], blocks[len(partners) :]):
        put(k, mine[...])
        put(k ^ 1, theirs[...])
    chunk = beside_ref.shape[1]
    for e in range(width // chunk):
        put(jnp.int32(1), beside_ref[(2 + e) * rows : (3 + e) * rows, :], e * chunk)
    copy.wait()
    put(jnp.int32(0), own[...])


def weights_kernel(x_ref, *refs):
    *keys, out_ref = refs
    rows = x_ref.shape[1] // (len(keys) + 1)
    total = dot(x_ref[:, :rows], keys[0][:rows, :])
    for j in range(1, len(keys)):
        total += dot(x_ref[:, j * rows : (j + 1) * rows], keys[j][:rows, :])
    out_ref[...] = total


def last_kernel(parts, x_ref, sum_ref, key_ref, out_hbm, out, sems):
    rows = key_ref.shape[0]
    half = x_ref.shape[0] // 2
    copies = []
    for h in range(2):
        part = slice(h * half, (h + 1) * half)
        done = sum_ref[part, :] + dot(x_ref[part, x_ref.shape[1] - rows :], key_ref[...])
        out[part, :] = done * (1.0 / parts)
        copies.append(pltpu.make_async_copy(out.at[part, :], out_hbm.at[part, :], sems.at[h]))
        copies[h].start()
    for copy in copies:
        copy.wait()


def along_dp(array, partner, parts, groups):
    pairs = [
        (i * groups + m, (i ^ partner(m)) * groups + m)
        for i in range(parts)
        for m in range(groups)
    ]
    return lax.ppermute(array, ("dp", "mp"), pairs)


def along_mp(array, bit, groups):
    return lax.ppermute(array, "mp", [(m, m ^ bit) for m in range(groups)])


def sent_inputs(inputs, parts, groups):
    far = parts // 2
    part, member = lax.axis_index("dp"), lax.axis_index("mp")
    rows, width = inputs.shape[0], inputs.shape[1] // parts

    def block(k):
        return lax.dynamic_slice(inputs, (0, (part ^ k) * width), (rows, width))

    distant = along_dp(block(far + member), lambda m: far + m, parts, groups)
    near = []
    for k in range(2, far, 2):
        sent = block(k + lax.rem(member, 2))
        near.append(along_dp(sent, lambda m, k=k: k + m % 2, parts, groups))
    return distant, near, block(1)


def shared_inputs(piece, groups):
    pieces = [piece]
    bit = 2
    while bit < groups:
        pieces += [along_mp(piece, bit, groups) for piece in pieces]
        bit *= 2
    return pieces


def turned_inputs(mine, theirs, beside, inputs, parts):
    rows, width = inputs.shape[0], inputs.shape[1] // parts
    blocks = [*mine, *theirs, beside]
    return pl.pallas_call(
        turned_kernel,
        in_specs=[IN_VMEM] * len(blocks) + [IN_HBM],
        out_specs=IN_VMEM,
        out_shape=jax.ShapeDtypeStruct((width, parts * rows), inputs.dtype),
        scratch_shapes=[pltpu.VMEM((rows, width), inputs.dtype), pltpu.SemaphoreType.DMA],
        compiler_params=PARAMS,
        cost_estimate=cost(0, 4 * inputs.size),
    )(*blocks, inputs)


def summed_weights(turned, keys, parts):
    width, columns = turned.shape[0], keys[0].shape[1]
    weights = jax.ShapeDtypeStruct((width, columns), F32)
    most = pl.pallas_call(
        weights_kernel,
        out_specs=IN_VMEM,
        out_shape=weights,
        compiler_params=PARAMS,
        cost_estimate=cost(
            2 * turned.size * columns, 2 * turned.size + 4 * width * columns
        ),
    )(turned, *keys[:-1])
    return pl.pallas_call(
        functools.partial(last_kernel, parts),
        out_specs=ANYWHERE,
        out_shape=weights,
        scratch_shapes=[pltpu.VMEM(weights.shape, F32), pltpu.SemaphoreType.DMA((2,))],
        compiler_params=PARAMS,
        cost_estimate=cost(2 * width * columns * keys[-1].shape[0], 8 * width * columns),
    )(turned, most, keys[-1])


def gathered_weights(inputs, grad_key, parts):
    rows = inputs.shape[0]
    width = inputs.shape[1] // parts
    blocks = inputs.reshape(rows, parts, width).transpose(1, 0, 2)
    mine = lax.all_to_all(blocks, "dp", split_axis=0, concat_axis=0, tiled=True)
    keys = lax.all_gather(grad_key, "dp", axis=0)
    return jnp.einsum("psd,psc->dc", mine, keys, preferred_element_type=F32) / parts


def body(query_states, key_states, value_states, grad_context, inputs_normed, projections):
    parts = lax.axis_size("dp")
    groups = lax.axis_size("mp")
    chips = groups // 2
    rows, width = key_states.shape
    query_width = query_states.shape[1]
    features = projections.shape[1] // groups
    kv_heads = width // HEAD_SIZE
    partial = jax.ShapeDtypeStruct((chips, rows, features), BF16)
    exchange = parts == 2 * groups and inputs_normed.shape[1] % (parts * width) == 0
    if exchange:
        distant, near, next_block = sent_inputs(inputs_normed, parts, groups)

    whole = pltpu.VMEM((rows, query_width), BF16)
    narrow = pltpu.VMEM((rows, width), BF16)
    wide = pltpu.VMEM((kv_heads, rows, query_width // kv_heads), F32)
    grad_key, grad_value, twice, grad_query = pl.pallas_call(
        attention_kernel,
        in_specs=[IN_HBM] * 4,
        out_specs=[IN_VMEM, IN_VMEM, IN_VMEM, ANYWHERE],
        out_shape=(
            jax.ShapeDtypeStruct((rows, width), BF16),
            jax.ShapeDtypeStruct((rows, width), BF16),
            jax.ShapeDtypeStruct((2 * rows, width), BF16),
            jax.ShapeDtypeStruct((rows, query_width), BF16),
        ),
        scratch_shapes=[whole, narrow, narrow, whole, whole, whole, whole, wide, wide]
        + [pltpu.SemaphoreType.DMA((2 + 2 * kv_heads,)), pltpu.SemaphoreType.DMA((kv_heads,))],
        compiler_params=WHOLE,
        cost_estimate=cost(
            10 * rows * rows * query_width, 6 * rows * query_width, rows * query_width
        ),
    )(query_states, key_states, value_states, grad_context)

    sent, kept = pl.pallas_call(
        partials_kernel,
        in_specs=[IN_VMEM, IN_VMEM, IN_HBM],
        out_specs=[ANYWHERE, ANYWHERE],
        out_shape=(partial, partial),
        scratch_shapes=[
            pltpu.VMEM((groups, 2, features, width), BF16),
            pltpu.VMEM((groups, rows, features), BF16),
            pltpu.SemaphoreType.DMA((groups,)),
            pltpu.SemaphoreType.DMA((groups,)),
        ],
        compiler_params=WHOLE,
        cost_estimate=cost(
            4 * rows * width * features * groups, 4 * width * features * groups
        ),
    )(grad_key, grad_value, projections)

    if exchange:
        first = along_dp(grad_key, lambda m: parts // 2, parts, groups)
        first, twice, sent, kept, distant, near = lax.optimization_barrier(
            (first, twice, sent, kept, distant, near)
        )
        pieces = shared_inputs(distant, groups)
        keys = {0: lax.dynamic_update_slice(twice, first, (rows, 0))}
        bit = parts // 4
        while bit > 1:
            for k in list(keys):
                keys[k ^ bit] = along_dp(keys[k], lambda m, bit=bit: bit, parts, groups)
            bit //= 2
        chunks = [next_block[:, at : at + width] for at in range(0, next_block.shape[1], width)]
        beside = [along_dp(jnp.concatenate([keys[0], *chunks]), lambda m: 1, parts, groups)]
        pieces[1:], _ = lax.optimization_barrier((pieces[1:], keys))
        mine = pieces + near
        theirs = [along_mp(piece, 1, groups) for piece in mine]
    came = along_mp(sent, 1, groups)
    total = kept.astype(F32) + came.astype(F32)
    grad_input = total[chips - 1]
    for b in range(chips - 1):
        shift = [(m, (m + 2 * (b + 1)) % groups) for m in range(groups)]
        grad_input += lax.ppermute(total[b].astype(BF16), "mp", shift).astype(F32)
    grad_input = grad_input.astype(BF16)

    if exchange:
        for k in range(2, parts // 2, 2):
            beside.append(along_dp(keys[k], lambda m: 1, parts, groups))
        turned = turned_inputs(mine, theirs, beside[0], inputs_normed, parts)
        beside[-1], grad_input = lax.optimization_barrier((beside[-1], grad_input))
        keys = [keys[k] for k in range(0, parts // 2, 2)] + beside
        grad_weights = summed_weights(turned, keys, parts)
    else:
        grad_weights = gathered_weights(inputs_normed, grad_key, parts)
    return (grad_query, grad_input, grad_weights)


def solution(mesh):
    placed = (
        P("dp", "mp"),
        P("dp", "mp"),
        P("dp", "mp"),
        P("dp", "mp"),
        P("dp", None),
        P(None, None, "mp"),
    )
    return jax.shard_map(
        body,
        mesh=mesh,
        in_specs=placed,
        out_specs=(P("dp", "mp"), P("dp", "mp"), P("dp", "mp")),
        check_vma=False,
    )
```

```python
import functools
import math

import jax
import jax.numpy as jnp
from jax import lax
from jax.experimental import pallas as pl
from jax.experimental.pallas import tpu as pltpu
from jax.sharding import PartitionSpec as P

HEAD_SIZE = 128
F32 = jnp.float32
BF16 = jnp.bfloat16
NN = (((1,), (0,)), ((), ()))
NT = (((1,), (1,)), ((), ()))
TN = (((0,), (0,)), ((), ()))
IN_HBM = pl.BlockSpec(memory_space=pltpu.HBM)
ANYWHERE = pl.BlockSpec(memory_space=pl.ANY)
IN_VMEM = pl.BlockSpec(memory_space=pltpu.VMEM)
CHUNK = 512
PARAMS = pltpu.CompilerParams(vmem_limit_bytes=24 * 1024 * 1024)
WHOLE = pltpu.CompilerParams(vmem_limit_bytes=60 * 1024 * 1024)


def dot(a, b, dims=NN):
    return lax.dot_general(a, b, dims, preferred_element_type=F32)


def cost(flops, moved, transcendentals=0):
    return pl.CostEstimate(flops=flops, bytes_accessed=moved, transcendentals=transcendentals)


def attention_scores(g, q, k, v, do, scores, grad_probs):
    per_group = q.shape[1] // k.shape[1]
    cols = slice(g * HEAD_SIZE, (g + 1) * HEAD_SIZE)
    scores[g] = dot(k[:, cols], stacked(q, g, per_group), NT)
    grad_probs[g] = dot(v[:, cols], stacked(do, g, per_group), NT)


def stacked(array, g, per_group):
    first = g * per_group * HEAD_SIZE
    heads = [array[:, first + h * HEAD_SIZE : first + (h + 1) * HEAD_SIZE] for h in range(per_group)]
    return jnp.concatenate(heads, axis=0)


def attention_softmax(g, scores, grad_probs, probs_b, ds):
    length = scores.shape[1]
    group = scores.shape[2]
    scale = 1.0 / math.sqrt(HEAD_SIZE)
    targets = lax.broadcasted_iota(jnp.int32, (length, length), 0)
    positions = lax.broadcasted_iota(jnp.int32, (length, length), 1)
    allowed = targets <= positions
    for at in range(0, group, length):
        cols = slice(at, at + length)
        masked = jnp.where(allowed, scores[g, :, cols], -1e30)
        raw = jnp.exp((masked - jnp.max(masked, axis=0, keepdims=True)) * scale)
        probs = raw * (1.0 / jnp.sum(raw, axis=0, keepdims=True))
        slopes = grad_probs[g, :, cols]
        delta = jnp.sum(probs * slopes, axis=0, keepdims=True)
        probs_b[:, g * group + at : g * group + at + length] = probs.astype(BF16)
        ds[:, g * group + at : g * group + at + length] = (probs * (slopes - delta)).astype(BF16)


def attention_kernel(
    q_hbm, k_hbm, v_hbm, do_hbm, gk_ref, gv_ref, twice_ref, gq_hbm,
    q, k, v, do, probs_b, ds, gq, scores, grad_probs, sems, out_sems,
):
    length = q.shape[0]
    kv_heads = k.shape[1] // HEAD_SIZE
    group = q.shape[1] // kv_heads
    per_group = group // HEAD_SIZE
    small = [
        pltpu.make_async_copy(k_hbm, k, sems.at[0]),
        pltpu.make_async_copy(v_hbm, v, sems.at[1]),
    ]
    large, stored = [], []
    for g in range(kv_heads):
        cols = pl.ds(g * group, group)
        large.append((
            pltpu.make_async_copy(q_hbm.at[:, cols], q.at[:, cols], sems.at[2 + 2 * g]),
            pltpu.make_async_copy(do_hbm.at[:, cols], do.at[:, cols], sems.at[3 + 2 * g]),
        ))
        stored.append(pltpu.make_async_copy(gq.at[:, cols], gq_hbm.at[:, cols], out_sems.at[g]))
    for copy in small:
        copy.start()
    for pair in large:
        for copy in pair:
            copy.start()
    for copy in small:
        copy.wait()
    for g in range(kv_heads):
        for copy in large[g]:
            copy.wait()
        attention_scores(g, q, k, v, do, scores, grad_probs)
    scale = 1.0 / math.sqrt(HEAD_SIZE)
    for g in range(kv_heads):
        attention_softmax(g, scores, grad_probs, probs_b, ds)
        cols = slice(g * group, (g + 1) * group)
        head = slice(g * HEAD_SIZE, (g + 1) * HEAD_SIZE)
        grad_query = dot(ds[:, cols], k[:, head], TN) * scale
        for h in range(per_group):
            at = g * group + h * HEAD_SIZE
            gq[:, at : at + HEAD_SIZE] = grad_query[h * length : (h + 1) * length].astype(BF16)
        stored[g].start()
    for g in range(kv_heads):
        cols = slice(g * group, (g + 1) * group)
        head = slice(g * HEAD_SIZE, (g + 1) * HEAD_SIZE)
        grad_key = dot(ds[:, cols], stacked(q, g, per_group)) * scale
        gk_ref[:, head] = grad_key.astype(BF16)
        twice_ref[:length, head] = grad_key.astype(BF16)
        twice_ref[length:, head] = grad_key.astype(BF16)
        gv_ref[:, head] = dot(probs_b[:, cols], stacked(do, g, per_group)).astype(BF16)
    for copy in stored:
        copy.wait()


def partials_kernel(gk_ref, gv_ref, p_hbm, sent_hbm, kept_hbm, p, partial, p_sems, out_sems):
    groups, features = p.shape[0], p.shape[2]
    chips = groups // 2
    member = lax.axis_index("mp")
    chip, core = lax.div(member, 2), lax.rem(member, 2)
    blocks, stored = [], []
    for b in range(groups):
        column = core if b >= chips else 1 - core
        start = (2 * lax.rem(chip + b + 1, chips) + column) * features
        rows = pl.ds(pl.multiple_of(start, features), features)
        blocks.append(pltpu.make_async_copy(p_hbm.at[:, rows, :], p.at[b], p_sems.at[b]))
    for copy in blocks:
        copy.start()
    grads = jnp.concatenate([gk_ref[...], gv_ref[...]], axis=1)
    step = min(CHUNK, features)
    for b in range(groups):
        blocks[b].wait()
        for at in range(0, features, step):
            rows = slice(at, at + step)
            both = jnp.concatenate([p[b, 0, rows, :], p[b, 1, rows, :]], axis=1)
            partial[b, :, rows] = dot(grads, both, NT).astype(BF16)
        target = sent_hbm.at[b] if b < chips else kept_hbm.at[b - chips]
        stored.append(pltpu.make_async_copy(partial.at[b], target, out_sems.at[b]))
        stored[-1].start()
    for copy in stored:
        copy.wait()


def turned_kernel(*refs):
    *blocks, beside_ref, x_hbm, out_ref, own, sem = refs
    rows, width = own.shape
    parts = out_ref.shape[1] // rows
    far = groups = parts // 2
    part, member = lax.axis_index("dp"), lax.axis_index("mp")
    cols = pl.ds(pl.multiple_of(part * width, width), width)
    copy = pltpu.make_async_copy(x_hbm.at[:, cols], own, sem)
    copy.start()

    def put(k, piece, at=0):
        place = far * lax.rem(k, 2) + 2 * lax.div(lax.rem(k, far), 2) + lax.div(k, far)
        tokens = pl.ds(pl.multiple_of(place * rows, rows), rows)
        out_ref[at : at + piece.shape[1], tokens] = piece.T

    partners = [far + (member ^ j) for j in range(0, groups, 2)]
    partners += [k + lax.rem(member, 2) for k in range(2, far, 2)]
    for k, mine, theirs in zip(partners, blocks[: len(partners)], blocks[len(partners) :]):
        put(k, mine[...])
        put(k ^ 1, theirs[...])
    chunk = beside_ref.shape[1]
    for e in range(width // chunk):
        put(jnp.int32(1), beside_ref[(2 + e) * rows : (3 + e) * rows, :], e * chunk)
    copy.wait()
    put(jnp.int32(0), own[...])


def weights_kernel(x_ref, *refs):
    *keys, out_ref = refs
    rows = x_ref.shape[1] // (len(keys) + 1)
    total = dot(x_ref[:, :rows], keys[0][:rows, :])
    for j in range(1, len(keys)):
        total += dot(x_ref[:, j * rows : (j + 1) * rows], keys[j][:rows, :])
    out_ref[...] = total


def last_kernel(parts, x_ref, sum_ref, key_ref, out_hbm, out, sems):
    rows = key_ref.shape[0]
    half = x_ref.shape[0] // 2
    copies = []
    for h in range(2):
        part = slice(h * half, (h + 1) * half)
        done = sum_ref[part, :] + dot(x_ref[part, x_ref.shape[1] - rows :], key_ref[...])
        out[part, :] = done * (1.0 / parts)
        copies.append(pltpu.make_async_copy(out.at[part, :], out_hbm.at[part, :], sems.at[h]))
        copies[h].start()
    for copy in copies:
        copy.wait()


def along_dp(array, partner, parts, groups):
    pairs = [
        (i * groups + m, (i ^ partner(m)) * groups + m)
        for i in range(parts)
        for m in range(groups)
    ]
    return lax.ppermute(array, ("dp", "mp"), pairs)


def along_mp(array, bit, groups):
    return lax.ppermute(array, "mp", [(m, m ^ bit) for m in range(groups)])


def sent_inputs(inputs, parts, groups):
    far = parts // 2
    part, member = lax.axis_index("dp"), lax.axis_index("mp")
    rows, width = inputs.shape[0], inputs.shape[1] // parts

    def block(k):
        return lax.dynamic_slice(inputs, (0, (part ^ k) * width), (rows, width))

    distant = along_dp(block(far + member), lambda m: far + m, parts, groups)
    near = []
    for k in range(2, far, 2):
        sent = block(k + lax.rem(member, 2))
        near.append(along_dp(sent, lambda m, k=k: k + m % 2, parts, groups))
    return distant, near, block(1)


def shared_inputs(piece, groups):
    pieces = [piece]
    bit = 2
    while bit < groups:
        pieces += [along_mp(piece, bit, groups) for piece in pieces]
        bit *= 2
    return pieces


def turned_inputs(mine, theirs, beside, inputs, parts):
    rows, width = inputs.shape[0], inputs.shape[1] // parts
    blocks = [*mine, *theirs, beside]
    return pl.pallas_call(
        turned_kernel,
        in_specs=[IN_VMEM] * len(blocks) + [IN_HBM],
        out_specs=IN_VMEM,
        out_shape=jax.ShapeDtypeStruct((width, parts * rows), inputs.dtype),
        scratch_shapes=[pltpu.VMEM((rows, width), inputs.dtype), pltpu.SemaphoreType.DMA],
        compiler_params=PARAMS,
        cost_estimate=cost(0, 4 * inputs.size),
    )(*blocks, inputs)


def summed_weights(turned, keys, parts):
    width, columns = turned.shape[0], keys[0].shape[1]
    weights = jax.ShapeDtypeStruct((width, columns), F32)
    most = pl.pallas_call(
        weights_kernel,
        out_specs=IN_VMEM,
        out_shape=weights,
        compiler_params=PARAMS,
        cost_estimate=cost(
            2 * turned.size * columns, 2 * turned.size + 4 * width * columns
        ),
    )(turned, *keys[:-1])
    return pl.pallas_call(
        functools.partial(last_kernel, parts),
        out_specs=ANYWHERE,
        out_shape=weights,
        scratch_shapes=[pltpu.VMEM(weights.shape, F32), pltpu.SemaphoreType.DMA((2,))],
        compiler_params=PARAMS,
        cost_estimate=cost(2 * width * columns * keys[-1].shape[0], 8 * width * columns),
    )(turned, most, keys[-1])


def gathered_weights(inputs, grad_key, parts):
    rows = inputs.shape[0]
    width = inputs.shape[1] // parts
    blocks = inputs.reshape(rows, parts, width).transpose(1, 0, 2)
    mine = lax.all_to_all(blocks, "dp", split_axis=0, concat_axis=0, tiled=True)
    keys = lax.all_gather(grad_key, "dp", axis=0)
    return jnp.einsum("psd,psc->dc", mine, keys, preferred_element_type=F32) / parts


def body(query_states, key_states, value_states, grad_context, inputs_normed, projections):
    parts = lax.axis_size("dp")
    groups = lax.axis_size("mp")
    chips = groups // 2
    rows, width = key_states.shape
    query_width = query_states.shape[1]
    features = projections.shape[1] // groups
    kv_heads = width // HEAD_SIZE
    partial = jax.ShapeDtypeStruct((chips, rows, features), BF16)
    exchange = parts == 2 * groups and inputs_normed.shape[1] % (parts * width) == 0
    if exchange:
        distant, near, next_block = sent_inputs(inputs_normed, parts, groups)

    whole = pltpu.VMEM((rows, query_width), BF16)
    narrow = pltpu.VMEM((rows, width), BF16)
    wide = pltpu.VMEM((kv_heads, rows, query_width // kv_heads), F32)
    grad_key, grad_value, twice, grad_query = pl.pallas_call(
        attention_kernel,
        in_specs=[IN_HBM] * 4,
        out_specs=[IN_VMEM, IN_VMEM, IN_VMEM, ANYWHERE],
        out_shape=(
            jax.ShapeDtypeStruct((rows, width), BF16),
            jax.ShapeDtypeStruct((rows, width), BF16),
            jax.ShapeDtypeStruct((2 * rows, width), BF16),
            jax.ShapeDtypeStruct((rows, query_width), BF16),
        ),
        scratch_shapes=[whole, narrow, narrow, whole, whole, whole, whole, wide, wide]
        + [pltpu.SemaphoreType.DMA((2 + 2 * kv_heads,)), pltpu.SemaphoreType.DMA((kv_heads,))],
        compiler_params=WHOLE,
        cost_estimate=cost(
            10 * rows * rows * query_width, 6 * rows * query_width, rows * query_width
        ),
    )(query_states, key_states, value_states, grad_context)

    sent, kept = pl.pallas_call(
        partials_kernel,
        in_specs=[IN_VMEM, IN_VMEM, IN_HBM],
        out_specs=[ANYWHERE, ANYWHERE],
        out_shape=(partial, partial),
        scratch_shapes=[
            pltpu.VMEM((groups, 2, features, width), BF16),
            pltpu.VMEM((groups, rows, features), BF16),
            pltpu.SemaphoreType.DMA((groups,)),
            pltpu.SemaphoreType.DMA((groups,)),
        ],
        compiler_params=WHOLE,
        cost_estimate=cost(
            4 * rows * width * features * groups, 4 * width * features * groups
        ),
    )(grad_key, grad_value, projections)

    if exchange:
        first = along_dp(grad_key, lambda m: parts // 2, parts, groups)
        first, twice, sent, kept, distant, near = lax.optimization_barrier(
            (first, twice, sent, kept, distant, near)
        )
        pieces = shared_inputs(distant, groups)
        keys = {0: lax.dynamic_update_slice(twice, first, (rows, 0))}
        bit = parts // 4
        while bit > 1:
            for k in list(keys):
                keys[k ^ bit] = along_dp(keys[k], lambda m, bit=bit: bit, parts, groups)
            bit //= 2
        chunks = [next_block[:, at : at + width] for at in range(0, next_block.shape[1], width)]
        beside = [along_dp(jnp.concatenate([keys[0], *chunks]), lambda m: 1, parts, groups)]
        pieces[1:], _ = lax.optimization_barrier((pieces[1:], keys))
        mine = pieces + near
        theirs = [along_mp(piece, 1, groups) for piece in mine]
    came = along_mp(sent, 1, groups)
    total = kept.astype(F32) + came.astype(F32)
    grad_input = total[chips - 1]
    for b in range(chips - 1):
        shift = [(m, (m + 2 * (b + 1)) % groups) for m in range(groups)]
        grad_input += lax.ppermute(total[b].astype(BF16), "mp", shift).astype(F32)
    grad_input = grad_input.astype(BF16)

    if exchange:
        for k in range(2, parts // 2, 2):
            beside.append(along_dp(keys[k], lambda m: 1, parts, groups))
        turned = turned_inputs(mine, theirs, beside[0], inputs_normed, parts)
        beside[-1], grad_input = lax.optimization_barrier((beside[-1], grad_input))
        keys = [keys[k] for k in range(0, parts // 2, 2)] + beside
        grad_weights = summed_weights(turned, keys, parts)
    else:
        grad_weights = gathered_weights(inputs_normed, grad_key, parts)
    return (grad_query, grad_input, grad_weights)


def solution(mesh):
    placed = (
        P("dp", "mp"),
        P("dp", "mp"),
        P("dp", "mp"),
        P("dp", "mp"),
        P("dp", None),
        P(None, None, "mp"),
    )
    return jax.shard_map(
        body,
        mesh=mesh,
        in_specs=placed,
        out_specs=(P("dp", "mp"), P("dp", "mp"), P("dp", "mp")),
        check_vma=False,
    )
```

```python
import functools
import math

import jax
import jax.numpy as jnp
from jax import lax
from jax.experimental import pallas as pl
from jax.experimental.pallas import tpu as pltpu
from jax.sharding import PartitionSpec as P

HEAD_SIZE = 128
F32 = jnp.float32
BF16 = jnp.bfloat16
NN = (((1,), (0,)), ((), ()))
NT = (((1,), (1,)), ((), ()))
TN = (((0,), (0,)), ((), ()))
IN_HBM = pl.BlockSpec(memory_space=pltpu.HBM)
ANYWHERE = pl.BlockSpec(memory_space=pl.ANY)
IN_VMEM = pl.BlockSpec(memory_space=pltpu.VMEM)
CHUNK = 256
PARAMS = pltpu.CompilerParams(vmem_limit_bytes=24 * 1024 * 1024)
WHOLE = pltpu.CompilerParams(vmem_limit_bytes=60 * 1024 * 1024)


def dot(a, b, dims=NN):
    return lax.dot_general(a, b, dims, preferred_element_type=F32)


def cost(flops, moved, transcendentals=0):
    return pl.CostEstimate(flops=flops, bytes_accessed=moved, transcendentals=transcendentals)


def attention_scores(g, q, k, v, do, scores, grad_probs):
    per_group = q.shape[1] // k.shape[1]
    cols = slice(g * HEAD_SIZE, (g + 1) * HEAD_SIZE)
    scores[g] = dot(k[:, cols], stacked(q, g, per_group), NT)
    grad_probs[g] = dot(v[:, cols], stacked(do, g, per_group), NT)


def stacked(array, g, per_group):
    first = g * per_group * HEAD_SIZE
    heads = [array[:, first + h * HEAD_SIZE : first + (h + 1) * HEAD_SIZE] for h in range(per_group)]
    return jnp.concatenate(heads, axis=0)


def attention_softmax(g, scores, grad_probs, probs_b, ds):
    length = scores.shape[1]
    group = scores.shape[2]
    scale = 1.0 / math.sqrt(HEAD_SIZE)
    targets = lax.broadcasted_iota(jnp.int32, (length, length), 0)
    positions = lax.broadcasted_iota(jnp.int32, (length, length), 1)
    allowed = targets <= positions
    for at in range(0, group, length):
        cols = slice(at, at + length)
        masked = jnp.where(allowed, scores[g, :, cols], -1e30)
        raw = jnp.exp((masked - jnp.max(masked, axis=0, keepdims=True)) * scale)
        probs = raw * (1.0 / jnp.sum(raw, axis=0, keepdims=True))
        slopes = grad_probs[g, :, cols]
        delta = jnp.sum(probs * slopes, axis=0, keepdims=True)
        probs_b[:, g * group + at : g * group + at + length] = probs.astype(BF16)
        ds[:, g * group + at : g * group + at + length] = (probs * (slopes - delta)).astype(BF16)


def attention_kernel(
    q_hbm, k_hbm, v_hbm, do_hbm, gk_ref, gv_ref, twice_ref, gq_hbm,
    q, k, v, do, probs_b, ds, gq, scores, grad_probs, sems, out_sems,
):
    length = q.shape[0]
    kv_heads = k.shape[1] // HEAD_SIZE
    group = q.shape[1] // kv_heads
    per_group = group // HEAD_SIZE
    small = [
        pltpu.make_async_copy(k_hbm, k, sems.at[0]),
        pltpu.make_async_copy(v_hbm, v, sems.at[1]),
    ]
    large, stored = [], []
    for g in range(kv_heads):
        cols = pl.ds(g * group, group)
        large.append((
            pltpu.make_async_copy(q_hbm.at[:, cols], q.at[:, cols], sems.at[2 + 2 * g]),
            pltpu.make_async_copy(do_hbm.at[:, cols], do.at[:, cols], sems.at[3 + 2 * g]),
        ))
        stored.append(pltpu.make_async_copy(gq.at[:, cols], gq_hbm.at[:, cols], out_sems.at[g]))
    for copy in small:
        copy.start()
    for pair in large:
        for copy in pair:
            copy.start()
    for copy in small:
        copy.wait()
    for g in range(kv_heads):
        for copy in large[g]:
            copy.wait()
        attention_scores(g, q, k, v, do, scores, grad_probs)
    scale = 1.0 / math.sqrt(HEAD_SIZE)
    for g in range(kv_heads):
        attention_softmax(g, scores, grad_probs, probs_b, ds)
        cols = slice(g * group, (g + 1) * group)
        head = slice(g * HEAD_SIZE, (g + 1) * HEAD_SIZE)
        grad_query = dot(ds[:, cols], k[:, head], TN) * scale
        for h in range(per_group):
            at = g * group + h * HEAD_SIZE
            gq[:, at : at + HEAD_SIZE] = grad_query[h * length : (h + 1) * length].astype(BF16)
        stored[g].start()
    for g in range(kv_heads):
        cols = slice(g * group, (g + 1) * group)
        head = slice(g * HEAD_SIZE, (g + 1) * HEAD_SIZE)
        grad_key = dot(ds[:, cols], stacked(q, g, per_group)) * scale
        gk_ref[:, head] = grad_key.astype(BF16)
        twice_ref[:length, head] = grad_key.astype(BF16)
        twice_ref[length:, head] = grad_key.astype(BF16)
        gv_ref[:, head] = dot(probs_b[:, cols], stacked(do, g, per_group)).astype(BF16)
    for copy in stored:
        copy.wait()


def partials_kernel(gk_ref, gv_ref, p_hbm, sent_hbm, kept_hbm, p, partial, p_sems, out_sems):
    groups, features = p.shape[0], p.shape[2]
    chips = groups // 2
    member = lax.axis_index("mp")
    chip, core = lax.div(member, 2), lax.rem(member, 2)
    blocks, stored = [], []
    for b in range(groups):
        column = core if b >= chips else 1 - core
        start = (2 * lax.rem(chip + b + 1, chips) + column) * features
        rows = pl.ds(pl.multiple_of(start, features), features)
        blocks.append(pltpu.make_async_copy(p_hbm.at[:, rows, :], p.at[b], p_sems.at[b]))
    for copy in blocks:
        copy.start()
    grads = jnp.concatenate([gk_ref[...], gv_ref[...]], axis=1)
    step = min(CHUNK, features)
    for b in range(groups):
        blocks[b].wait()
        for at in range(0, features, step):
            rows = slice(at, at + step)
            both = jnp.concatenate([p[b, 0, rows, :], p[b, 1, rows, :]], axis=1)
            partial[b, :, rows] = dot(grads, both, NT).astype(BF16)
        target = sent_hbm.at[b] if b < chips else kept_hbm.at[b - chips]
        stored.append(pltpu.make_async_copy(partial.at[b], target, out_sems.at[b]))
        stored[-1].start()
    for copy in stored:
        copy.wait()


def turned_kernel(*refs):
    *blocks, beside_ref, x_hbm, out_ref, own, sem = refs
    rows, width = own.shape
    parts = out_ref.shape[1] // rows
    far = groups = parts // 2
    part, member = lax.axis_index("dp"), lax.axis_index("mp")
    cols = pl.ds(pl.multiple_of(part * width, width), width)
    copy = pltpu.make_async_copy(x_hbm.at[:, cols], own, sem)
    copy.start()

    def put(k, piece, at=0):
        place = far * lax.rem(k, 2) + 2 * lax.div(lax.rem(k, far), 2) + lax.div(k, far)
        tokens = pl.ds(pl.multiple_of(place * rows, rows), rows)
        out_ref[at : at + piece.shape[1], tokens] = piece.T

    partners = [far + (member ^ j) for j in range(0, groups, 2)]
    partners += [k + lax.rem(member, 2) for k in range(2, far, 2)]
    for k, mine, theirs in zip(partners, blocks[: len(partners)], blocks[len(partners) :]):
        put(k, mine[...])
        put(k ^ 1, theirs[...])
    chunk = beside_ref.shape[1]
    for e in range(width // chunk):
        put(jnp.int32(1), beside_ref[(2 + e) * rows : (3 + e) * rows, :], e * chunk)
    copy.wait()
    put(jnp.int32(0), own[...])


def weights_kernel(x_ref, *refs):
    *keys, out_ref = refs
    rows = x_ref.shape[1] // (len(keys) + 1)
    total = dot(x_ref[:, :rows], keys[0][:rows, :])
    for j in range(1, len(keys)):
        total += dot(x_ref[:, j * rows : (j + 1) * rows], keys[j][:rows, :])
    out_ref[...] = total


def last_kernel(parts, x_ref, sum_ref, key_ref, out_hbm, out, sems):
    rows = key_ref.shape[0]
    half = x_ref.shape[0] // 2
    copies = []
    for h in range(2):
        part = slice(h * half, (h + 1) * half)
        done = sum_ref[part, :] + dot(x_ref[part, x_ref.shape[1] - rows :], key_ref[...])
        out[part, :] = done * (1.0 / parts)
        copies.append(pltpu.make_async_copy(out.at[part, :], out_hbm.at[part, :], sems.at[h]))
        copies[h].start()
    for copy in copies:
        copy.wait()


def along_dp(array, partner, parts, groups):
    pairs = [
        (i * groups + m, (i ^ partner(m)) * groups + m)
        for i in range(parts)
        for m in range(groups)
    ]
    return lax.ppermute(array, ("dp", "mp"), pairs)


def along_mp(array, bit, groups):
    return lax.ppermute(array, "mp", [(m, m ^ bit) for m in range(groups)])


def sent_inputs(inputs, parts, groups):
    far = parts // 2
    part, member = lax.axis_index("dp"), lax.axis_index("mp")
    rows, width = inputs.shape[0], inputs.shape[1] // parts

    def block(k):
        return lax.dynamic_slice(inputs, (0, (part ^ k) * width), (rows, width))

    distant = along_dp(block(far + member), lambda m: far + m, parts, groups)
    near = []
    for k in range(2, far, 2):
        sent = block(k + lax.rem(member, 2))
        near.append(along_dp(sent, lambda m, k=k: k + m % 2, parts, groups))
    return distant, near, block(1)


def shared_inputs(piece, groups):
    pieces = [piece]
    bit = 2
    while bit < groups:
        pieces += [along_mp(piece, bit, groups) for piece in pieces]
        bit *= 2
    return pieces


def turned_inputs(mine, theirs, beside, inputs, parts):
    rows, width = inputs.shape[0], inputs.shape[1] // parts
    blocks = [*mine, *theirs, beside]
    return pl.pallas_call(
        turned_kernel,
        in_specs=[IN_VMEM] * len(blocks) + [IN_HBM],
        out_specs=IN_VMEM,
        out_shape=jax.ShapeDtypeStruct((width, parts * rows), inputs.dtype),
        scratch_shapes=[pltpu.VMEM((rows, width), inputs.dtype), pltpu.SemaphoreType.DMA],
        compiler_params=PARAMS,
        cost_estimate=cost(0, 4 * inputs.size),
    )(*blocks, inputs)


def summed_weights(turned, keys, parts):
    width, columns = turned.shape[0], keys[0].shape[1]
    weights = jax.ShapeDtypeStruct((width, columns), F32)
    most = pl.pallas_call(
        weights_kernel,
        out_specs=IN_VMEM,
        out_shape=weights,
        compiler_params=PARAMS,
        cost_estimate=cost(
            2 * turned.size * columns, 2 * turned.size + 4 * width * columns
        ),
    )(turned, *keys[:-1])
    return pl.pallas_call(
        functools.partial(last_kernel, parts),
        out_specs=ANYWHERE,
        out_shape=weights,
        scratch_shapes=[pltpu.VMEM(weights.shape, F32), pltpu.SemaphoreType.DMA((2,))],
        compiler_params=PARAMS,
        cost_estimate=cost(2 * width * columns * keys[-1].shape[0], 8 * width * columns),
    )(turned, most, keys[-1])


def gathered_weights(inputs, grad_key, parts):
    rows = inputs.shape[0]
    width = inputs.shape[1] // parts
    blocks = inputs.reshape(rows, parts, width).transpose(1, 0, 2)
    mine = lax.all_to_all(blocks, "dp", split_axis=0, concat_axis=0, tiled=True)
    keys = lax.all_gather(grad_key, "dp", axis=0)
    return jnp.einsum("psd,psc->dc", mine, keys, preferred_element_type=F32) / parts


def body(query_states, key_states, value_states, grad_context, inputs_normed, projections):
    parts = lax.axis_size("dp")
    groups = lax.axis_size("mp")
    chips = groups // 2
    rows, width = key_states.shape
    query_width = query_states.shape[1]
    features = projections.shape[1] // groups
    kv_heads = width // HEAD_SIZE
    partial = jax.ShapeDtypeStruct((chips, rows, features), BF16)
    exchange = parts == 2 * groups and inputs_normed.shape[1] % (parts * width) == 0
    if exchange:
        distant, near, next_block = sent_inputs(inputs_normed, parts, groups)

    whole = pltpu.VMEM((rows, query_width), BF16)
    narrow = pltpu.VMEM((rows, width), BF16)
    wide = pltpu.VMEM((kv_heads, rows, query_width // kv_heads), F32)
    grad_key, grad_value, twice, grad_query = pl.pallas_call(
        attention_kernel,
        in_specs=[IN_HBM] * 4,
        out_specs=[IN_VMEM, IN_VMEM, IN_VMEM, ANYWHERE],
        out_shape=(
            jax.ShapeDtypeStruct((rows, width), BF16),
            jax.ShapeDtypeStruct((rows, width), BF16),
            jax.ShapeDtypeStruct((2 * rows, width), BF16),
            jax.ShapeDtypeStruct((rows, query_width), BF16),
        ),
        scratch_shapes=[whole, narrow, narrow, whole, whole, whole, whole, wide, wide]
        + [pltpu.SemaphoreType.DMA((2 + 2 * kv_heads,)), pltpu.SemaphoreType.DMA((kv_heads,))],
        compiler_params=WHOLE,
        cost_estimate=cost(
            10 * rows * rows * query_width, 6 * rows * query_width, rows * query_width
        ),
    )(query_states, key_states, value_states, grad_context)

    sent, kept = pl.pallas_call(
        partials_kernel,
        in_specs=[IN_VMEM, IN_VMEM, IN_HBM],
        out_specs=[ANYWHERE, ANYWHERE],
        out_shape=(partial, partial),
        scratch_shapes=[
            pltpu.VMEM((groups, 2, features, width), BF16),
            pltpu.VMEM((groups, rows, features), BF16),
            pltpu.SemaphoreType.DMA((groups,)),
            pltpu.SemaphoreType.DMA((groups,)),
        ],
        compiler_params=WHOLE,
        cost_estimate=cost(
            4 * rows * width * features * groups, 4 * width * features * groups
        ),
    )(grad_key, grad_value, projections)

    if exchange:
        first = along_dp(grad_key, lambda m: parts // 2, parts, groups)
        first, twice, sent, kept, distant, near = lax.optimization_barrier(
            (first, twice, sent, kept, distant, near)
        )
        pieces = shared_inputs(distant, groups)
        keys = {0: lax.dynamic_update_slice(twice, first, (rows, 0))}
        bit = parts // 4
        while bit > 1:
            for k in list(keys):
                keys[k ^ bit] = along_dp(keys[k], lambda m, bit=bit: bit, parts, groups)
            bit //= 2
        chunks = [next_block[:, at : at + width] for at in range(0, next_block.shape[1], width)]
        beside = [along_dp(jnp.concatenate([keys[0], *chunks]), lambda m: 1, parts, groups)]
        pieces[1:], _ = lax.optimization_barrier((pieces[1:], keys))
        mine = pieces + near
        theirs = [along_mp(piece, 1, groups) for piece in mine]
    came = along_mp(sent, 1, groups)
    total = kept.astype(F32) + came.astype(F32)
    grad_input = total[chips - 1]
    for b in range(chips - 1):
        shift = [(m, (m + 2 * (b + 1)) % groups) for m in range(groups)]
        grad_input += lax.ppermute(total[b].astype(BF16), "mp", shift).astype(F32)
    grad_input = grad_input.astype(BF16)

    if exchange:
        for k in range(2, parts // 2, 2):
            beside.append(along_dp(keys[k], lambda m: 1, parts, groups))
        turned = turned_inputs(mine, theirs, beside[0], inputs_normed, parts)
        beside[-1], grad_input = lax.optimization_barrier((beside[-1], grad_input))
        keys = [keys[k] for k in range(0, parts // 2, 2)] + beside
        grad_weights = summed_weights(turned, keys, parts)
    else:
        grad_weights = gathered_weights(inputs_normed, grad_key, parts)
    return (grad_query, grad_input, grad_weights)


def solution(mesh):
    placed = (
        P("dp", "mp"),
        P("dp", "mp"),
        P("dp", "mp"),
        P("dp", "mp"),
        P("dp", None),
        P(None, None, "mp"),
    )
    return jax.shard_map(
        body,
        mesh=mesh,
        in_specs=placed,
        out_specs=(P("dp", "mp"), P("dp", "mp"), P("dp", "mp")),
        check_vma=False,
    )
```

```python
import functools
import math

import jax
import jax.numpy as jnp
from jax import lax
from jax.experimental import pallas as pl
from jax.experimental.pallas import tpu as pltpu
from jax.sharding import PartitionSpec as P

HEAD_SIZE = 128
F32 = jnp.float32
BF16 = jnp.bfloat16
NN = (((1,), (0,)), ((), ()))
NT = (((1,), (1,)), ((), ()))
TN = (((0,), (0,)), ((), ()))
IN_HBM = pl.BlockSpec(memory_space=pltpu.HBM)
ANYWHERE = pl.BlockSpec(memory_space=pl.ANY)
IN_VMEM = pl.BlockSpec(memory_space=pltpu.VMEM)
CHUNK = 512
PARAMS = pltpu.CompilerParams(vmem_limit_bytes=24 * 1024 * 1024)
WHOLE = pltpu.CompilerParams(vmem_limit_bytes=60 * 1024 * 1024)


def dot(a, b, dims=NN):
    return lax.dot_general(a, b, dims, preferred_element_type=F32)


def cost(flops, moved, transcendentals=0):
    return pl.CostEstimate(flops=flops, bytes_accessed=moved, transcendentals=transcendentals)


def attention_scores(g, q, k, v, do, scores, grad_probs):
    per_group = q.shape[1] // k.shape[1]
    cols = slice(g * HEAD_SIZE, (g + 1) * HEAD_SIZE)
    scores[g] = dot(k[:, cols], stacked(q, g, per_group), NT)
    grad_probs[g] = dot(v[:, cols], stacked(do, g, per_group), NT)


def stacked(array, g, per_group):
    first = g * per_group * HEAD_SIZE
    heads = [array[:, first + h * HEAD_SIZE : first + (h + 1) * HEAD_SIZE] for h in range(per_group)]
    return jnp.concatenate(heads, axis=0)


def attention_softmax(g, scores, grad_probs, probs_b, ds):
    length = scores.shape[1]
    group = scores.shape[2]
    scale = 1.0 / math.sqrt(HEAD_SIZE)
    targets = lax.broadcasted_iota(jnp.int32, (length, length), 0)
    positions = lax.broadcasted_iota(jnp.int32, (length, length), 1)
    allowed = targets <= positions
    for at in range(0, group, length):
        cols = slice(at, at + length)
        masked = jnp.where(allowed, scores[g, :, cols], -1e30)
        raw = jnp.exp((masked - jnp.max(masked, axis=0, keepdims=True)) * scale)
        probs = raw * (1.0 / jnp.sum(raw, axis=0, keepdims=True))
        slopes = grad_probs[g, :, cols]
        delta = jnp.sum(probs * slopes, axis=0, keepdims=True)
        probs_b[:, g * group + at : g * group + at + length] = probs.astype(BF16)
        ds[:, g * group + at : g * group + at + length] = (probs * (slopes - delta)).astype(BF16)


def attention_kernel(
    q_hbm, k_hbm, v_hbm, do_hbm, gk_ref, gv_ref, twice_ref, gq_hbm,
    q, k, v, do, probs_b, ds, gq, scores, grad_probs, sems, out_sems,
):
    length = q.shape[0]
    kv_heads = k.shape[1] // HEAD_SIZE
    group = q.shape[1] // kv_heads
    per_group = group // HEAD_SIZE
    small = [
        pltpu.make_async_copy(k_hbm, k, sems.at[0]),
        pltpu.make_async_copy(v_hbm, v, sems.at[1]),
    ]
    large, stored = [], []
    for g in range(kv_heads):
        cols = pl.ds(g * group, group)
        large.append((
            pltpu.make_async_copy(q_hbm.at[:, cols], q.at[:, cols], sems.at[2 + 2 * g]),
            pltpu.make_async_copy(do_hbm.at[:, cols], do.at[:, cols], sems.at[3 + 2 * g]),
        ))
        stored.append(pltpu.make_async_copy(gq.at[:, cols], gq_hbm.at[:, cols], out_sems.at[g]))
    for copy in small:
        copy.start()
    for pair in large:
        for copy in pair:
            copy.start()
    scale = 1.0 / math.sqrt(HEAD_SIZE)
    for copy in small:
        copy.wait()
    for g in range(kv_heads):
        for copy in large[g]:
            copy.wait()
        attention_scores(g, q, k, v, do, scores, grad_probs)
        attention_softmax(g, scores, grad_probs, probs_b, ds)
        cols = slice(g * group, (g + 1) * group)
        head = slice(g * HEAD_SIZE, (g + 1) * HEAD_SIZE)
        grad_query = dot(ds[:, cols], k[:, head], TN) * scale
        for h in range(per_group):
            at = g * group + h * HEAD_SIZE
            gq[:, at : at + HEAD_SIZE] = grad_query[h * length : (h + 1) * length].astype(BF16)
        stored[g].start()
    for g in range(kv_heads):
        cols = slice(g * group, (g + 1) * group)
        head = slice(g * HEAD_SIZE, (g + 1) * HEAD_SIZE)
        grad_key = dot(ds[:, cols], stacked(q, g, per_group)) * scale
        gk_ref[:, head] = grad_key.astype(BF16)
        twice_ref[:length, head] = grad_key.astype(BF16)
        twice_ref[length:, head] = grad_key.astype(BF16)
        gv_ref[:, head] = dot(probs_b[:, cols], stacked(do, g, per_group)).astype(BF16)
    for copy in stored:
        copy.wait()


def partials_kernel(gk_ref, gv_ref, p_hbm, sent_hbm, kept_hbm, p, partial, p_sems, out_sems):
    groups, features = p.shape[0], p.shape[2]
    chips = groups // 2
    member = lax.axis_index("mp")
    chip, core = lax.div(member, 2), lax.rem(member, 2)
    blocks, stored = [], []
    for b in range(groups):
        column = core if b >= chips else 1 - core
        start = (2 * lax.rem(chip + b + 1, chips) + column) * features
        rows = pl.ds(pl.multiple_of(start, features), features)
        blocks.append(pltpu.make_async_copy(p_hbm.at[:, rows, :], p.at[b], p_sems.at[b]))
    for copy in blocks:
        copy.start()
    grads = jnp.concatenate([gk_ref[...], gv_ref[...]], axis=1)
    step = min(CHUNK, features)
    for b in range(groups):
        blocks[b].wait()
        for at in range(0, features, step):
            rows = slice(at, at + step)
            both = jnp.concatenate([p[b, 0, rows, :], p[b, 1, rows, :]], axis=1)
            partial[b, :, rows] = dot(grads, both, NT).astype(BF16)
        target = sent_hbm.at[b] if b < chips else kept_hbm.at[b - chips]
        stored.append(pltpu.make_async_copy(partial.at[b], target, out_sems.at[b]))
        stored[-1].start()
    for copy in stored:
        copy.wait()


def turned_kernel(*refs):
    *blocks, beside_ref, x_hbm, out_ref, own, sem = refs
    rows, width = own.shape
    parts = out_ref.shape[1] // rows
    far = groups = parts // 2
    part, member = lax.axis_index("dp"), lax.axis_index("mp")
    cols = pl.ds(pl.multiple_of(part * width, width), width)
    copy = pltpu.make_async_copy(x_hbm.at[:, cols], own, sem)
    copy.start()

    def put(k, piece, at=0):
        place = far * lax.rem(k, 2) + 2 * lax.div(lax.rem(k, far), 2) + lax.div(k, far)
        tokens = pl.ds(pl.multiple_of(place * rows, rows), rows)
        out_ref[at : at + piece.shape[1], tokens] = piece.T

    partners = [far + (member ^ j) for j in range(0, groups, 2)]
    partners += [k + lax.rem(member, 2) for k in range(2, far, 2)]
    for k, mine, theirs in zip(partners, blocks[: len(partners)], blocks[len(partners) :]):
        put(k, mine[...])
        put(k ^ 1, theirs[...])
    chunk = beside_ref.shape[1]
    for e in range(width // chunk):
        put(jnp.int32(1), beside_ref[(2 + e) * rows : (3 + e) * rows, :], e * chunk)
    copy.wait()
    put(jnp.int32(0), own[...])


def weights_kernel(x_ref, *refs):
    *keys, out_ref = refs
    rows = x_ref.shape[1] // (len(keys) + 1)
    total = dot(x_ref[:, :rows], keys[0][:rows, :])
    for j in range(1, len(keys)):
        total += dot(x_ref[:, j * rows : (j + 1) * rows], keys[j][:rows, :])
    out_ref[...] = total


def last_kernel(parts, x_ref, sum_ref, key_ref, out_hbm, out, sems):
    rows = key_ref.shape[0]
    half = x_ref.shape[0] // 2
    copies = []
    for h in range(2):
        part = slice(h * half, (h + 1) * half)
        done = sum_ref[part, :] + dot(x_ref[part, x_ref.shape[1] - rows :], key_ref[...])
        out[part, :] = done * (1.0 / parts)
        copies.append(pltpu.make_async_copy(out.at[part, :], out_hbm.at[part, :], sems.at[h]))
        copies[h].start()
    for copy in copies:
        copy.wait()


def along_dp(array, partner, parts, groups):
    pairs = [
        (i * groups + m, (i ^ partner(m)) * groups + m)
        for i in range(parts)
        for m in range(groups)
    ]
    return lax.ppermute(array, ("dp", "mp"), pairs)


def along_mp(array, bit, groups):
    return lax.ppermute(array, "mp", [(m, m ^ bit) for m in range(groups)])


def sent_inputs(inputs, parts, groups):
    far = parts // 2
    part, member = lax.axis_index("dp"), lax.axis_index("mp")
    rows, width = inputs.shape[0], inputs.shape[1] // parts

    def block(k):
        return lax.dynamic_slice(inputs, (0, (part ^ k) * width), (rows, width))

    distant = along_dp(block(far + member), lambda m: far + m, parts, groups)
    near = []
    for k in range(2, far, 2):
        sent = block(k + lax.rem(member, 2))
        near.append(along_dp(sent, lambda m, k=k: k + m % 2, parts, groups))
    return distant, near, block(1)


def shared_inputs(piece, groups):
    pieces = [piece]
    bit = 2
    while bit < groups:
        pieces += [along_mp(piece, bit, groups) for piece in pieces]
        bit *= 2
    return pieces


def turned_inputs(mine, theirs, beside, inputs, parts):
    rows, width = inputs.shape[0], inputs.shape[1] // parts
    blocks = [*mine, *theirs, beside]
    return pl.pallas_call(
        turned_kernel,
        in_specs=[IN_VMEM] * len(blocks) + [IN_HBM],
        out_specs=IN_VMEM,
        out_shape=jax.ShapeDtypeStruct((width, parts * rows), inputs.dtype),
        scratch_shapes=[pltpu.VMEM((rows, width), inputs.dtype), pltpu.SemaphoreType.DMA],
        compiler_params=PARAMS,
        cost_estimate=cost(0, 4 * inputs.size),
    )(*blocks, inputs)


def summed_weights(turned, keys, parts):
    width, columns = turned.shape[0], keys[0].shape[1]
    weights = jax.ShapeDtypeStruct((width, columns), F32)
    most = pl.pallas_call(
        weights_kernel,
        out_specs=IN_VMEM,
        out_shape=weights,
        compiler_params=PARAMS,
        cost_estimate=cost(
            2 * turned.size * columns, 2 * turned.size + 4 * width * columns
        ),
    )(turned, *keys[:-1])
    return pl.pallas_call(
        functools.partial(last_kernel, parts),
        out_specs=ANYWHERE,
        out_shape=weights,
        scratch_shapes=[pltpu.VMEM(weights.shape, F32), pltpu.SemaphoreType.DMA((2,))],
        compiler_params=PARAMS,
        cost_estimate=cost(2 * width * columns * keys[-1].shape[0], 8 * width * columns),
    )(turned, most, keys[-1])


def gathered_weights(inputs, grad_key, parts):
    rows = inputs.shape[0]
    width = inputs.shape[1] // parts
    blocks = inputs.reshape(rows, parts, width).transpose(1, 0, 2)
    mine = lax.all_to_all(blocks, "dp", split_axis=0, concat_axis=0, tiled=True)
    keys = lax.all_gather(grad_key, "dp", axis=0)
    return jnp.einsum("psd,psc->dc", mine, keys, preferred_element_type=F32) / parts


def body(query_states, key_states, value_states, grad_context, inputs_normed, projections):
    parts = lax.axis_size("dp")
    groups = lax.axis_size("mp")
    chips = groups // 2
    rows, width = key_states.shape
    query_width = query_states.shape[1]
    features = projections.shape[1] // groups
    kv_heads = width // HEAD_SIZE
    partial = jax.ShapeDtypeStruct((chips, rows, features), BF16)
    exchange = parts == 2 * groups and inputs_normed.shape[1] % (parts * width) == 0
    if exchange:
        distant, near, next_block = sent_inputs(inputs_normed, parts, groups)

    whole = pltpu.VMEM((rows, query_width), BF16)
    narrow = pltpu.VMEM((rows, width), BF16)
    wide = pltpu.VMEM((kv_heads, rows, query_width // kv_heads), F32)
    grad_key, grad_value, twice, grad_query = pl.pallas_call(
        attention_kernel,
        in_specs=[IN_HBM] * 4,
        out_specs=[IN_VMEM, IN_VMEM, IN_VMEM, ANYWHERE],
        out_shape=(
            jax.ShapeDtypeStruct((rows, width), BF16),
            jax.ShapeDtypeStruct((rows, width), BF16),
            jax.ShapeDtypeStruct((2 * rows, width), BF16),
            jax.ShapeDtypeStruct((rows, query_width), BF16),
        ),
        scratch_shapes=[whole, narrow, narrow, whole, whole, whole, whole, wide, wide]
        + [pltpu.SemaphoreType.DMA((2 + 2 * kv_heads,)), pltpu.SemaphoreType.DMA((kv_heads,))],
        compiler_params=WHOLE,
        cost_estimate=cost(
            10 * rows * rows * query_width, 6 * rows * query_width, rows * query_width
        ),
    )(query_states, key_states, value_states, grad_context)

    sent, kept = pl.pallas_call(
        partials_kernel,
        in_specs=[IN_VMEM, IN_VMEM, IN_HBM],
        out_specs=[ANYWHERE, ANYWHERE],
        out_shape=(partial, partial),
        scratch_shapes=[
            pltpu.VMEM((groups, 2, features, width), BF16),
            pltpu.VMEM((groups, rows, features), BF16),
            pltpu.SemaphoreType.DMA((groups,)),
            pltpu.SemaphoreType.DMA((groups,)),
        ],
        compiler_params=WHOLE,
        cost_estimate=cost(
            4 * rows * width * features * groups, 4 * width * features * groups
        ),
    )(grad_key, grad_value, projections)

    if exchange:
        first = along_dp(grad_key, lambda m: parts // 2, parts, groups)
        first, twice, sent, kept, distant, near = lax.optimization_barrier(
            (first, twice, sent, kept, distant, near)
        )
        pieces = shared_inputs(distant, groups)
        keys = {0: lax.dynamic_update_slice(twice, first, (rows, 0))}
        bit = parts // 4
        while bit > 1:
            for k in list(keys):
                keys[k ^ bit] = along_dp(keys[k], lambda m, bit=bit: bit, parts, groups)
            bit //= 2
        chunks = [next_block[:, at : at + width] for at in range(0, next_block.shape[1], width)]
        beside = [along_dp(jnp.concatenate([keys[0], *chunks]), lambda m: 1, parts, groups)]
        pieces[1:], _ = lax.optimization_barrier((pieces[1:], keys))
        mine = pieces + near
        theirs = [along_mp(piece, 1, groups) for piece in mine]
    came = along_mp(sent, 1, groups)
    total = kept.astype(F32) + came.astype(F32)
    grad_input = total[chips - 1]
    for b in range(chips - 1):
        shift = [(m, (m + 2 * (b + 1)) % groups) for m in range(groups)]
        grad_input += lax.ppermute(total[b].astype(BF16), "mp", shift).astype(F32)
    grad_input = grad_input.astype(BF16)

    if exchange:
        for k in range(2, parts // 2, 2):
            beside.append(along_dp(keys[k], lambda m: 1, parts, groups))
        turned = turned_inputs(mine, theirs, beside[0], inputs_normed, parts)
        beside[-1], grad_input = lax.optimization_barrier((beside[-1], grad_input))
        keys = [keys[k] for k in range(0, parts // 2, 2)] + beside
        grad_weights = summed_weights(turned, keys, parts)
    else:
        grad_weights = gathered_weights(inputs_normed, grad_key, parts)
    return (grad_query, grad_input, grad_weights)


def solution(mesh):
    placed = (
        P("dp", "mp"),
        P("dp", "mp"),
        P("dp", "mp"),
        P("dp", "mp"),
        P("dp", None),
        P(None, None, "mp"),
    )
    return jax.shard_map(
        body,
        mesh=mesh,
        in_specs=placed,
        out_specs=(P("dp", "mp"), P("dp", "mp"), P("dp", "mp")),
        check_vma=False,
    )
```
